256 devices in a mesh: dp: 8 (over z), seq: 32 (over y, x, core).
Axes of the slice: x: 4, y: 4, z: 8, core: 2. Of those that a mesh axis runs over, the one named last changes fastest.
Arguments:
- inputs: bfloat16 [16, 2048, 1024], P('dp', 'seq'), may hold values from -32 to 32
- grad_out: bfloat16 [16, 2048, 1024], P('dp', 'seq'), may hold values from -6 to 6
- w_qkv: bfloat16 [1024, 3072], replicated, may hold values from -0.1875 to 0.1875
Outputs:
- grad_inputs: bfloat16 [16, 2048, 1024], P('dp', 'seq')
- grad_weights: float32 [1024, 3072], P(('dp', 'seq'))
The draws below stay inside these ranges and needn't reach their ends.
All inputs are finite; a program needn't handle non-finite values.
Results may differ from the reference program's by a relative error of at most 0.0075.
Values sent between devices are 32-bit elements; how exact they have to be, the bound alone decides.
No kernel may reach another device: no remote copies, remote signals or barrier semaphores. Data moves between devices by JAX's collectives and lax.ppermute only.
A program may use at most 192 MiB of HBM per device.

```python
import math
import jax
import jax.numpy as jnp
from jax import lax

H = 8
DH = 128
D = 1024
TOK_DEV = 64
SEQLEN = 2048
USERS = 16


def draw_inputs(key, part):
    noise_key = jax.random.fold_in(key, 11)
    scale_key = jax.random.fold_in(key, 12)
    position = jnp.arange(D, dtype=jnp.float32) / (D - 1)
    normal_part = jnp.clip(jax.random.normal(noise_key, (USERS, SEQLEN, D), jnp.float32), -6.0, 6.0)
    log_low = math.log(0.5)
    log_span = math.log(8.0)
    roughness = jax.random.uniform(scale_key, (D,), jnp.float32, 0.7, 1.3)
    feature_scale = jnp.exp(log_low + log_span * position) * roughness
    return (normal_part * feature_scale).astype(jnp.bfloat16)


def level_of(rng, shape, split, least, high):
    def one(dim, shards_of):
        draws = jax.random.uniform(jax.random.fold_in(jax.random.fold_in(rng, 6), dim), (shards_of,), jnp.float32, least / len(split), high / len(split))
        return jnp.repeat(jnp.exp(draws), shape[dim] // shards_of).reshape((-1,) + (1,) * (len(shape) - dim - 1))

    factor_of = one(*split[0])
    for cut in split[1:]:
        factor_of = factor_of * one(*cut)
    return factor_of


def gaussian(rng, extent, deviation, reach, split=(), kind=jnp.bfloat16):
    loudness = level_of(rng, extent, split, -0.22, 0.18) if split else 1.0
    result = jax.random.normal(rng, extent, jnp.float32) * deviation * loudness
    return jnp.minimum(jnp.maximum(result, -reach), reach).astype(kind)


def setup_inputs(seed: int = 0) -> dict:
    streams_of = jax.random.split(jax.random.key(seed), 4)
    return {
        "inputs": draw_inputs(jax.random.fold_in(streams_of[3], 71), 0),
        "grad_out": gaussian(streams_of[1], (USERS, SEQLEN, D), 1.0, 6.0, ((0, 8), (1, 32))),
        "w_qkv": gaussian(streams_of[2], (D, 3 * D), D ** -0.5, 0.1875),
    }


def round_half(array):
    return lax.optimization_barrier(array.astype(jnp.bfloat16)).astype(jnp.float32)

def reference(inputs, grad_out, w_qkv):
    block_count = SEQLEN // TOK_DEV
    scaling = 1.0 / math.sqrt(DH * SEQLEN)
    causal = jnp.arange(TOK_DEV)[:, None] >= jnp.arange(TOK_DEV)[None, :]

    def one_user(accumulated, user_pair):
        user_inputs, user_grads = user_pair
        projected = jnp.dot(user_inputs, w_qkv, preferred_element_type=jnp.float32).astype(jnp.bfloat16)
        queries = projected[:, :D].reshape(block_count, TOK_DEV, H, DH).astype(jnp.float32)
        key_rows = projected[:, D:2 * D].reshape(block_count, TOK_DEV, H, DH).astype(jnp.float32)
        values = projected[:, 2 * D:].reshape(block_count, TOK_DEV, H, DH).astype(jnp.float32)
        cotangent = user_grads.reshape(block_count, TOK_DEV, H, DH).astype(jnp.float32)
        key_state = jnp.einsum('nshd,nshe->nhde', key_rows, values)
        query_state = jnp.einsum('nthd,nthe->nhde', queries, cotangent)
        empty_state = jnp.zeros((1, H, DH, DH), jnp.float32)
        prior_state = jnp.concatenate([empty_state, jnp.cumsum(key_state, axis=0)[:-1]], axis=0)
        suffix = jnp.cumsum(query_state[::-1], axis=0)[::-1]
        later_state = jnp.concatenate([suffix[1:], empty_state], axis=0)
        prior_state = round_half(prior_state)
        later_state = round_half(later_state)
        out_value = jnp.einsum('nthe,nshe->nhts', cotangent, values)
        out_value = round_half(jnp.where(causal, out_value, 0.0))
        query_key = jnp.einsum('nthd,nshd->nhts', queries, key_rows)
        query_key = round_half(jnp.where(causal, query_key, 0.0))
        grad_query = scaling * (jnp.einsum('nhts,nshd->nthd', out_value, key_rows) + jnp.einsum('nthe,nhde->nthd', cotangent, prior_state))
        grad_key = scaling * (jnp.einsum('nhts,nthd->nshd', out_value, queries) + jnp.einsum('nshe,nhde->nshd', values, later_state))
        grad_value = scaling * (jnp.einsum('nhts,nthe->nshe', query_key, cotangent) + jnp.einsum('nshd,nhde->nshe', key_rows, later_state))
        grad_proj = jnp.concatenate([grad_query.reshape(SEQLEN, D).astype(jnp.bfloat16), grad_key.reshape(SEQLEN, D).astype(jnp.bfloat16), grad_value.reshape(SEQLEN, D).astype(jnp.bfloat16)], axis=1)
        grad_rows = jnp.dot(grad_proj, w_qkv.T, preferred_element_type=jnp.float32).astype(jnp.bfloat16)
        accumulated = accumulated + jnp.dot(user_inputs.T, grad_proj, preferred_element_type=jnp.float32)
        return (accumulated, grad_rows)
    raw_grad, grad_inputs = lax.scan(one_user, jnp.zeros((D, 3 * D), jnp.float32), (inputs, grad_out))
    total_sq = jnp.sum(raw_grad * raw_grad)
    factor = jnp.minimum(1.0, D / jnp.sqrt(total_sq + 1e-06))
    return (grad_inputs, raw_grad * factor)
```

```python
import functools
import math

import jax
import jax.numpy as jnp
from jax import lax
from jax.experimental import pallas as pl
from jax.experimental.pallas import tpu as pltpu
from jax.sharding import PartitionSpec as P

H = 8
DH = 128
D = 1024
NY = 4
NX = 4
GROUP = 2 * NX
BF16 = jnp.bfloat16
F32 = jnp.float32
VMEM = pl.BlockSpec(memory_space=pltpu.VMEM)
SMEM = pl.BlockSpec(memory_space=pltpu.SMEM)
MIB = 1 << 20


def seq_perm(dy, dx, dc):
    moves = []
    for y in range(NY):
        for x in range(NX):
            for c in range(2):
                source = (y * NX + x) * 2 + c
                target = (((y + dy) % NY) * NX + (x + dx) % NX) * 2 + (c ^ dc)
                moves.append((source, target))
    return moves


def send(value, dy=0, dx=0, dc=0):
    return lax.ppermute(value, "seq", seq_perm(dy, dx, dc))


def head_columns(array, head):
    return lax.dynamic_slice_in_dim(array, head * DH, DH, 1)


def struct(shape, dtype):
    return jax.ShapeDtypeStruct(shape, dtype)


def dot(a, b, over_a, over_b):
    return lax.dot_general(a, b, (((over_a,), (over_b,)), ((), ())), preferred_element_type=F32)


def block_kernel(users, *refs):
    first, second, w, cot, rows_t, proj, cot_half, key_state, query_state, intra = refs
    total = first.shape[0]
    size = total // users
    causal = lax.broadcasted_iota(jnp.int32, (size, size), 0) >= lax.broadcasted_iota(
        jnp.int32, (size, size), 1
    )
    cot_half[...] = cot[...].astype(BF16)
    for i, ref in enumerate((first, second)):
        x = ref[...].astype(BF16)
        rows_t[:, i * total : (i + 1) * total] = x.T
        proj[i * total : (i + 1) * total, :] = dot(x, w[...], 1, 0).astype(BF16)
        for u in range(users):
            here = slice(i * total + u * size, i * total + (u + 1) * size)
            q, k, v = (proj[here, part * DH : (part + 1) * DH] for part in range(3))
            g = cot_half[here, :]
            key_state[i, u] = dot(k, v, 0, 0)
            query_state[i, u] = dot(q, g, 0, 0)
            out_value = jnp.where(causal, dot(g, v, 1, 1), 0.0).astype(BF16)
            query_key = jnp.where(causal, dot(q, k, 1, 1), 0.0).astype(BF16)
            intra[here, :DH] = dot(out_value, k, 1, 0)
            intra[here, DH : 2 * DH] = dot(out_value, q, 0, 0)
            intra[here, 2 * DH :] = dot(query_key, g, 0, 0)


def blocks(first, second, w_head, cot, users):
    total, features = first.shape
    return pl.pallas_call(
        functools.partial(block_kernel, users),
        out_shape=(
            struct((features, 2 * total), BF16),
            struct((2 * total, 3 * DH), BF16),
            struct((2 * total, DH), BF16),
            struct((2, users, DH, DH), F32),
            struct((2, users, DH, DH), F32),
            struct((2 * total, 3 * DH), F32),
        ),
        in_specs=[VMEM] * 4,
        out_specs=(VMEM,) * 6,
        compiler_params=pltpu.CompilerParams(vmem_limit_bytes=24 * MIB),
        cost_estimate=pl.CostEstimate(
            flops=2 * 2 * total * features * 3 * DH, bytes_accessed=4 * MIB, transcendentals=0
        ),
        name="blocks",
    )(first, second, w_head, cot)


def total_kernel(place, *refs):
    keys, queries, outs = refs[:NX], refs[NX : 2 * NX], refs[2 * NX :]
    key_total = sum(ref[i] for ref in keys for i in range(2))
    query_total = sum(ref[i] for ref in queries for i in range(2))
    for dy in range(1, NY):
        outs[dy - 1][...] = jnp.where(place[0] + dy < NY, key_total, query_total)


def totals(place, key_states, query_states):
    shape = key_states[0].shape[1:]
    return pl.pallas_call(
        total_kernel,
        out_shape=(struct(shape, F32),) * (NY - 1),
        in_specs=[SMEM] + [VMEM] * (2 * NX),
        out_specs=(VMEM,) * (NY - 1),
        compiler_params=pltpu.CompilerParams(vmem_limit_bytes=16 * MIB),
        cost_estimate=pl.CostEstimate(flops=MIB, bytes_accessed=3 * MIB, transcendentals=0),
        name="totals",
    )(place, *key_states, *query_states)


def grad_kernel(scaling, users, dp_count, place, *refs):
    y, x, c = place[0], place[1], place[2]
    arrived, refs = refs[: NY - 1], refs[NY - 1 :]
    keys, refs = refs[:NX], refs[NX:]
    queries, refs = refs[:NX], refs[NX:]
    rows_t, refs = refs[:NX], refs[NX:]
    proj, refs = refs[:NX], refs[NX:]
    cots, refs = refs[:NX], refs[NX:]
    intra, refs = refs[:NX], refs[NX:]
    grad_proj, pieces, refs = refs[0], refs[1 : 1 + NY], refs[1 + NY :]
    key_all, query_all, prior_all, later_all, product = refs
    for dx in range(NX):
        key_all[2 * dx : 2 * dx + 2] = keys[dx][...]
        query_all[2 * dx : 2 * dx + 2] = queries[dx][...]
    prior = jnp.zeros(arrived[0].shape, F32)
    later = jnp.zeros(arrived[0].shape, F32)
    for dy in range(1, NY):
        value = arrived[dy - 1][...]
        prior = prior + jnp.where(y >= dy, value, 0.0)
        later = later + jnp.where(y >= dy, 0.0, value)

    def slot(position):
        return ((x + NX - position // 2) % NX) * 2 + (c ^ (position % 2))

    for position in range(GROUP):
        here = slot(position)
        prior_all[here] = prior.astype(BF16)
        prior = prior + key_all[here]
    for position in reversed(range(GROUP)):
        here = slot(position)
        later_all[here] = later.astype(BF16)
        later = later + query_all[here]
    total = proj[0].shape[0] // 2
    size = total // users
    for dx in range(NX):
        for i in range(2):
            for u in range(users):
                here = slice(i * total + u * size, i * total + (u + 1) * size)
                there = slice(dx * 2 * total + here.start, dx * 2 * total + here.stop)
                k, v = proj[dx][here, DH : 2 * DH], proj[dx][here, 2 * DH :]
                prior_state = prior_all[2 * dx + i, u]
                later_state = later_all[2 * dx + i, u]
                parts = (
                    dot(cots[dx][here, :], prior_state, 1, 1),
                    dot(v, later_state, 1, 1),
                    dot(k, later_state, 1, 0),
                )
                for part in range(3):
                    columns = slice(part * DH, (part + 1) * DH)
                    grad_proj[there, columns] = (
                        scaling * (intra[dx][here, columns] + parts[part])
                    ).astype(BF16)
    span = 2 * total
    product[...] = sum(
        dot(rows_t[dx][...], grad_proj[dx * span : (dx + 1) * span, :], 1, 0)
        for dx in range(NX)
    )
    row_block = product.shape[0] // (dp_count * NY)
    for dy in range(NY):
        target = (y + dy) % NY
        for z in range(dp_count):
            start = pl.multiple_of((z * NY + target) * row_block, row_block)
            pieces[dy][z] = product[pl.ds(start, row_block), :]


def gradients(place, arrived, parts, scaling, users, dp_count):
    rows_t, proj, cots, keys, queries, intra = zip(*parts)
    features, span = rows_t[0].shape
    row_block = features // (dp_count * NY)
    return pl.pallas_call(
        functools.partial(grad_kernel, scaling, users, dp_count),
        out_shape=(struct((NX * span, 3 * DH), BF16),)
        + (struct((dp_count, row_block, 3 * DH), F32),) * NY,
        in_specs=[SMEM] + [VMEM] * (NY - 1 + 6 * NX),
        out_specs=(VMEM,) * (1 + NY),
        scratch_shapes=[
            pltpu.VMEM((GROUP, users, DH, DH), F32),
            pltpu.VMEM((GROUP, users, DH, DH), F32),
            pltpu.VMEM((GROUP, users, DH, DH), BF16),
            pltpu.VMEM((GROUP, users, DH, DH), BF16),
            pltpu.VMEM((features, 3 * DH), F32),
        ],
        compiler_params=pltpu.CompilerParams(vmem_limit_bytes=32 * MIB),
        cost_estimate=pl.CostEstimate(
            flops=2 * NX * span * features * 3 * DH, bytes_accessed=10 * MIB, transcendentals=0
        ),
        name="gradients",
    )(place, *arrived, *keys, *queries, *rows_t, *proj, *cots, *intra)


def input_kernel(place, *refs):
    x, c = place[1], place[2]
    keep, swap, w, out, full = refs[:NX], refs[NX], refs[NX + 1], refs[NX + 2], refs[NX + 3]
    total = out.shape[0]
    for dx in range(NX):
        for dc in range(2):
            head = ((x + dx) % NX) * 2 + (c ^ dc)
            for part in range(3):
                columns = slice(part * DH, (part + 1) * DH)
                value = keep[dx][:total, columns] if dc == 0 else swap[dx, :, columns]
                start = pl.multiple_of((part * H + head) * DH, DH)
                full[:, pl.ds(start, DH)] = value.astype(BF16)
    out[...] = dot(full[...], w[...], 1, 1).astype(BF16)


def input_gradient(place, keep, swap, w_qkv):
    total = swap.shape[1]
    features, width = w_qkv.shape
    return pl.pallas_call(
        input_kernel,
        out_shape=struct((total, features), BF16),
        in_specs=[SMEM] + [VMEM] * (NX + 2),
        out_specs=VMEM,
        scratch_shapes=[pltpu.VMEM((total, width), BF16)],
        compiler_params=pltpu.CompilerParams(vmem_limit_bytes=24 * MIB),
        cost_estimate=pl.CostEstimate(
            flops=2 * total * features * width, bytes_accessed=10 * MIB, transcendentals=0
        ),
        name="input_gradient",
    )(place, *keep, swap, w_qkv)


def body(inputs, grad_out, w_qkv):
    user_count, row_count, feature_count = inputs.shape
    seqlen_total = row_count * lax.axis_size("seq")
    dp_count = lax.axis_size("dp")
    scaling = 1.0 / math.sqrt(DH * seqlen_total)
    index = lax.axis_index("seq")
    y, x, c = index // GROUP, (index // 2) % NX, index % 2
    place = jnp.stack([y, x, c])
    head = x * 2 + c
    total_rows = user_count * row_count

    own = inputs.reshape(total_rows, feature_count).astype(F32)
    half = total_rows // 2
    from_left = send(own, dx=1)
    from_right = send(own, dx=-1)
    other = send(own, dc=1)
    far_low = send(from_left[:half], dx=1)
    far_high = send(from_right[half:], dx=-1)
    left_other = send(from_left, dc=1)
    right_other = send(from_right, dc=1)
    far = jnp.concatenate([far_low, far_high], axis=0)
    far_other = send(far, dc=1)

    cot = grad_out.reshape(total_rows, feature_count).astype(F32)
    by_head = cot.reshape(total_rows, NX, 2, DH)
    mine = lax.dynamic_index_in_dim(by_head, c, 2, False)
    theirs = lax.dynamic_index_in_dim(by_head, 1 - c, 2, False)
    swapped = send(theirs.reshape(total_rows, NX * DH), dc=1)
    pair = jnp.concatenate([mine.reshape(total_rows, NX * DH), swapped], axis=0)
    cot_pieces = [head_columns(pair, x)]
    for dx in range(1, NX):
        piece = send(head_columns(pair, (x + dx) % NX), dx=dx)
        cot_pieces.append(piece)

    w_head = jnp.concatenate(
        [head_columns(w_qkv, part * H + head) for part in range(3)], axis=1
    )
    pairs = [(own, other), (from_left, left_other), (far, far_other), (from_right, right_other)]
    parts = [
        blocks(first, second, w_head, cot_piece, user_count)
        for (first, second), cot_piece in zip(pairs, cot_pieces)
    ]
    sent = totals(place, [part[3] for part in parts], [part[4] for part in parts])
    arrived = [send(sent[dy - 1], dy=dy) for dy in range(1, NY)]
    grad_proj, *pieces = gradients(place, arrived, parts, scaling, user_count, dp_count)

    summed = pieces[0]
    for dy in range(1, NY):
        summed = summed + send(pieces[dy], dy=dy)
    tile = jnp.sum(lax.all_to_all(summed, "dp", 0, 0), axis=0)

    span = 2 * total_rows
    back = [grad_proj[:span].astype(F32)]
    for dx in range(1, NX):
        back.append(send(grad_proj[dx * span : (dx + 1) * span].astype(F32), dx=-dx))
    swap = send(jnp.stack([piece[total_rows:] for piece in back]), dc=1)
    grad_rows = input_gradient(place, back, swap, w_qkv)
    grad_inputs = grad_rows.reshape(user_count, row_count, feature_count)

    square = jnp.sum(tile * tile)
    row_block = tile.shape[0]
    out_rows = row_block // H
    by_owner = tile.reshape(H, out_rows * 3, DH)
    got = jnp.zeros((H, out_rows * 3, DH), F32)
    for dx in range(NX):
        for dc in range(2):
            target = ((x + dx) % NX) * 2 + (c ^ dc)
            piece = lax.dynamic_index_in_dim(by_owner, target, 0, False)
            if dx or dc:
                piece = send(piece, dx=dx, dc=dc)
            source = ((x - dx) % NX) * 2 + (c ^ dc)
            got = lax.dynamic_update_index_in_dim(got, piece, source, 0)
    device_count = dp_count * lax.axis_size("seq")
    squares = lax.all_to_all(
        jnp.full((device_count, DH), square), ("dp", "seq"), 0, 0, tiled=True
    )
    total_sq = jnp.sum(squares[:, 0])
    factor = jnp.minimum(1.0, D / jnp.sqrt(total_sq + 1e-06))
    weights = jnp.transpose(got.reshape(H, out_rows, 3, DH), (1, 2, 0, 3))
    return (grad_inputs, weights.reshape(out_rows, 3 * feature_count) * factor)


def solution(mesh):
    in_specs = (P("dp", "seq", None), P("dp", "seq", None), P())
    out_specs = (P("dp", "seq", None), P(("dp", "seq"), None))
    return jax.shard_map(body, mesh=mesh, in_specs=in_specs, out_specs=out_specs, check_vma=False)
```

```python
import functools
import math

import jax
import jax.numpy as jnp
from jax import lax
from jax.experimental import pallas as pl
from jax.experimental.pallas import tpu as pltpu
from jax.sharding import PartitionSpec as P

H = 8
DH = 128
D = 1024
NY = 4
NX = 4
GROUP = 2 * NX
BF16 = jnp.bfloat16
F32 = jnp.float32
VMEM = pl.BlockSpec(memory_space=pltpu.VMEM)
SMEM = pl.BlockSpec(memory_space=pltpu.SMEM)
MIB = 1 << 20


def seq_perm(dy, dx, dc):
    moves = []
    for y in range(NY):
        for x in range(NX):
            for c in range(2):
                source = (y * NX + x) * 2 + c
                target = (((y + dy) % NY) * NX + (x + dx) % NX) * 2 + (c ^ dc)
                moves.append((source, target))
    return moves


def send(value, dy=0, dx=0, dc=0):
    return lax.ppermute(value, "seq", seq_perm(dy, dx, dc))


def head_columns(array, head):
    return lax.dynamic_slice_in_dim(array, head * DH, DH, 1)


def struct(shape, dtype):
    return jax.ShapeDtypeStruct(shape, dtype)


def dot(a, b, over_a, over_b):
    return lax.dot_general(a, b, (((over_a,), (over_b,)), ((), ())), preferred_element_type=F32)


def message_kernel(place, inputs, grad_out, right, left, cross):
    x, c = place[1], place[2]

    def rows(user, j):
        return inputs[user, :, j * DH : (j + 1) * DH].astype(F32)

    def cot(user, dx, core):
        head = ((x + dx) % NX) * 2 + core
        return grad_out[user, :, pl.ds(pl.multiple_of(head * DH, DH), DH)].astype(F32)

    for j in range(H):
        right[j] = rows(0, j)
        right[10 + j] = rows(1, j)
        left[j] = rows(1, j)
        left[10 + j] = rows(0, j)
        cross[j] = rows(0, j)
        cross[8 + j] = rows(1, j)
    for core in range(2):
        right[8 + core] = cot(0, 2, core)
        left[8 + core] = cot(1, 2, core)
        for user in range(2):
            right[18 + 2 * core + user] = cot(user, 1, core)
            left[18 + 2 * core + user] = cot(user, NX - 1, core)
    for user in range(2):
        cross[16 + user] = cot(user, 0, 1 - c)


def messages(place, inputs, grad_out):
    size = inputs.shape[1]
    return pl.pallas_call(
        message_kernel,
        out_shape=tuple(struct((count, size, DH), F32) for count in (22, 22, 18)),
        in_specs=[SMEM, VMEM, VMEM],
        out_specs=(VMEM,) * 3,
        compiler_params=pltpu.CompilerParams(vmem_limit_bytes=16 * MIB),
        cost_estimate=pl.CostEstimate(flops=MIB, bytes_accessed=3 * MIB, transcendentals=0),
        name="messages",
    )(place, inputs, grad_out)


def block_kernel(units, place, w, *refs):
    sources, refs = refs[:-7], refs[-7:]
    rows_t, proj, cot_half, key_state, query_state, intra, x_all = refs
    x, c = place[1], place[2]
    features, total = rows_t.shape
    size = total // len(units)
    causal = lax.broadcasted_iota(jnp.int32, (size, size), 0) >= lax.broadcasted_iota(
        jnp.int32, (size, size), 1
    )
    for n, (source, start, cot_start, cot_step) in enumerate(units):
        here = slice(n * size, (n + 1) * size)
        if start is None:
            x_all[here, :] = sources[source][n]
            columns = pl.ds(pl.multiple_of((x * 2 + c) * DH, DH), DH)
            cot_half[here, :] = sources[source + 1][n, :, columns]
        else:
            for j in range(features // DH):
                x_all[here, j * DH : (j + 1) * DH] = sources[source][start + j].astype(BF16)
            cot_half[here, :] = sources[source][cot_start + cot_step * c].astype(BF16)
    rows = x_all[...]
    proj[...] = dot(rows, w[...], 1, 0).astype(BF16)
    rows_t[...] = rows.T
    for n in range(len(units)):
        here = slice(n * size, (n + 1) * size)
        i, u = n // 2, n % 2
        q, k, v = (proj[here, part * DH : (part + 1) * DH] for part in range(3))
        g = cot_half[here, :]
        key_state[i, u] = dot(k, v, 0, 0)
        query_state[i, u] = dot(q, g, 0, 0)
        out_value = jnp.where(causal, dot(g, v, 1, 1), 0.0).astype(BF16)
        query_key = jnp.where(causal, dot(q, k, 1, 1), 0.0).astype(BF16)
        intra[here, :DH] = dot(out_value, k, 1, 0)
        intra[here, DH : 2 * DH] = dot(out_value, q, 0, 0)
        intra[here, 2 * DH :] = dot(query_key, g, 0, 0)


def blocks(place, w_head, sources, units):
    features = w_head.shape[0]
    size = sources[0].shape[1]
    total = len(units) * size
    return pl.pallas_call(
        functools.partial(block_kernel, units),
        out_shape=(
            struct((features, total), BF16),
            struct((total, 3 * DH), BF16),
            struct((total, DH), BF16),
            struct((2, 2, DH, DH), F32),
            struct((2, 2, DH, DH), F32),
            struct((total, 3 * DH), F32),
        ),
        in_specs=[SMEM] + [VMEM] * (1 + len(sources)),
        out_specs=(VMEM,) * 6,
        scratch_shapes=[pltpu.VMEM((total, features), BF16)],
        compiler_params=pltpu.CompilerParams(vmem_limit_bytes=24 * MIB),
        cost_estimate=pl.CostEstimate(
            flops=2 * total * features * 3 * DH, bytes_accessed=4 * MIB, transcendentals=0
        ),
        name="blocks",
    )(place, w_head, *sources)


def total_kernel(place, *refs):
    keys, queries, outs = refs[:NX], refs[NX : 2 * NX], refs[2 * NX :]
    key_total = sum(ref[i] for ref in keys for i in range(2))
    query_total = sum(ref[i] for ref in queries for i in range(2))
    for dy in range(1, NY):
        outs[dy - 1][...] = jnp.where(place[0] + dy < NY, key_total, query_total)


def totals(place, key_states, query_states):
    shape = key_states[0].shape[1:]
    return pl.pallas_call(
        total_kernel,
        out_shape=(struct(shape, F32),) * (NY - 1),
        in_specs=[SMEM] + [VMEM] * (2 * NX),
        out_specs=(VMEM,) * (NY - 1),
        compiler_params=pltpu.CompilerParams(vmem_limit_bytes=16 * MIB),
        cost_estimate=pl.CostEstimate(flops=MIB, bytes_accessed=3 * MIB, transcendentals=0),
        name="totals",
    )(place, *key_states, *query_states)


def grad_kernel(scaling, users, dp_count, place, *refs):
    y, x, c = place[0], place[1], place[2]
    arrived, refs = refs[: NY - 1], refs[NY - 1 :]
    keys, refs = refs[:NX], refs[NX:]
    queries, refs = refs[:NX], refs[NX:]
    rows_t, refs = refs[:NX], refs[NX:]
    proj, refs = refs[:NX], refs[NX:]
    cots, refs = refs[:NX], refs[NX:]
    intra, refs = refs[:NX], refs[NX:]
    grad_proj, pieces, refs = refs[0], refs[1 : 1 + NY], refs[1 + NY :]
    key_all, query_all, prior_all, later_all, product = refs
    for dx in range(NX):
        key_all[2 * dx : 2 * dx + 2] = keys[dx][...]
        query_all[2 * dx : 2 * dx + 2] = queries[dx][...]
    prior = jnp.zeros(arrived[0].shape, F32)
    later = jnp.zeros(arrived[0].shape, F32)
    for dy in range(1, NY):
        value = arrived[dy - 1][...]
        prior = prior + jnp.where(y >= dy, value, 0.0)
        later = later + jnp.where(y >= dy, 0.0, value)

    def slot(position):
        return ((x + NX - position // 2) % NX) * 2 + (c ^ (position % 2))

    for position in range(GROUP):
        here = slot(position)
        prior_all[here] = prior.astype(BF16)
        prior = prior + key_all[here]
    for position in reversed(range(GROUP)):
        here = slot(position)
        later_all[here] = later.astype(BF16)
        later = later + query_all[here]
    total = proj[0].shape[0] // 2
    size = total // users
    for dx in range(NX):
        for i in range(2):
            for u in range(users):
                here = slice(i * total + u * size, i * total + (u + 1) * size)
                there = slice(dx * 2 * total + here.start, dx * 2 * total + here.stop)
                k, v = proj[dx][here, DH : 2 * DH], proj[dx][here, 2 * DH :]
                prior_state = prior_all[2 * dx + i, u]
                later_state = later_all[2 * dx + i, u]
                parts = (
                    dot(cots[dx][here, :], prior_state, 1, 1),
                    dot(v, later_state, 1, 1),
                    dot(k, later_state, 1, 0),
                )
                for part in range(3):
                    columns = slice(part * DH, (part + 1) * DH)
                    grad_proj[there, columns] = (
                        scaling * (intra[dx][here, columns] + parts[part])
                    ).astype(BF16)
    span = 2 * total
    product[...] = sum(
        dot(rows_t[dx][...], grad_proj[dx * span : (dx + 1) * span, :], 1, 0)
        for dx in range(NX)
    )
    row_block = product.shape[0] // (dp_count * NY)
    for dy in range(NY):
        target = (y + dy) % NY
        for z in range(dp_count):
            start = pl.multiple_of((z * NY + target) * row_block, row_block)
            pieces[dy][z] = product[pl.ds(start, row_block), :]


def gradients(place, arrived, parts, scaling, users, dp_count):
    rows_t, proj, cots, keys, queries, intra = zip(*parts)
    features, span = rows_t[0].shape
    row_block = features // (dp_count * NY)
    return pl.pallas_call(
        functools.partial(grad_kernel, scaling, users, dp_count),
        out_shape=(struct((NX * span, 3 * DH), BF16),)
        + (struct((dp_count, row_block, 3 * DH), F32),) * NY,
        in_specs=[SMEM] + [VMEM] * (NY - 1 + 6 * NX),
        out_specs=(VMEM,) * (1 + NY),
        scratch_shapes=[
            pltpu.VMEM((GROUP, users, DH, DH), F32),
            pltpu.VMEM((GROUP, users, DH, DH), F32),
            pltpu.VMEM((GROUP, users, DH, DH), BF16),
            pltpu.VMEM((GROUP, users, DH, DH), BF16),
            pltpu.VMEM((features, 3 * DH), F32),
        ],
        compiler_params=pltpu.CompilerParams(vmem_limit_bytes=32 * MIB),
        cost_estimate=pl.CostEstimate(
            flops=2 * NX * span * features * 3 * DH, bytes_accessed=10 * MIB, transcendentals=0
        ),
        name="gradients",
    )(place, *arrived, *keys, *queries, *rows_t, *proj, *cots, *intra)


def input_kernel(place, *refs):
    x, c = place[1], place[2]
    keep = refs[:NX]
    swap, w, out, done, full = refs[NX:]
    total = out.shape[0]
    for dx in range(NX):
        for dc in range(2):
            head = ((x + dx) % NX) * 2 + (c ^ dc)
            for part in range(3):
                columns = slice(part * DH, (part + 1) * DH)
                value = keep[dx][:total, columns] if dc == 0 else swap[dx, :, columns]
                start = pl.multiple_of((part * H + head) * DH, DH)
                full[:, pl.ds(start, DH)] = value.astype(BF16)
    out[...] = dot(full[...], w[...], 1, 1).astype(BF16)
    done[...] = jnp.zeros(done.shape, F32)


def input_gradient(place, keep, swap, w_qkv):
    total = swap.shape[1]
    features, width = w_qkv.shape
    return pl.pallas_call(
        input_kernel,
        out_shape=(struct((total, features), BF16), struct((8, DH), F32)),
        in_specs=[SMEM] + [VMEM] * (NX + 2),
        out_specs=(VMEM, VMEM),
        scratch_shapes=[pltpu.VMEM((total, width), BF16)],
        compiler_params=pltpu.CompilerParams(vmem_limit_bytes=24 * MIB),
        cost_estimate=pl.CostEstimate(
            flops=2 * total * features * width, bytes_accessed=10 * MIB, transcendentals=0
        ),
        name="input_gradient",
    )(place, *keep, swap, w_qkv)


def fold_kernel(*refs):
    out = refs[-1]
    dp_count, row_block = refs[0].shape[0], refs[0].shape[1]
    rows = out.shape[1]
    for z in range(dp_count):
        value = sum(ref[z] for ref in refs[:-1])
        for t in range(GROUP):
            out[z * GROUP + t] = value[t * rows : (t + 1) * rows, :]


def fold(parts):
    dp_count, row_block, width = parts[0].shape
    return pl.pallas_call(
        fold_kernel,
        out_shape=struct((dp_count * GROUP, row_block // GROUP, width), F32),
        in_specs=[VMEM] * len(parts),
        out_specs=VMEM,
        compiler_params=pltpu.CompilerParams(vmem_limit_bytes=8 * MIB),
        cost_estimate=pl.CostEstimate(flops=MIB, bytes_accessed=2 * MIB, transcendentals=0),
        name="fold",
    )(*parts)


def collect_kernel(got, after, weights, squares):
    count = got.shape[0] // H
    square = jnp.zeros((), F32)
    for head in range(H):
        value = sum(got[z * H + head] for z in range(count))
        square = square + jnp.sum(value * value)
        for part in range(3):
            start = (part * H + head) * DH
            weights[:, start : start + DH] = value[:, part * DH : (part + 1) * DH]
    squares[...] = jnp.full(squares.shape, square)


def collect(got, after, device_count):
    rows, width = got.shape[1], got.shape[2]
    return pl.pallas_call(
        collect_kernel,
        out_shape=(struct((rows, H * width), F32), struct((device_count, DH), F32)),
        in_specs=[VMEM, pl.BlockSpec(memory_space=pl.ANY)],
        out_specs=(VMEM, VMEM),
        compiler_params=pltpu.CompilerParams(vmem_limit_bytes=8 * MIB),
        cost_estimate=pl.CostEstimate(flops=MIB, bytes_accessed=MIB, transcendentals=0),
        name="collect",
    )(got, after)


def clip_kernel(weights, squares, out):
    total_sq = jnp.sum(squares[...], axis=0, keepdims=True)
    factor = jnp.minimum(1.0, D / jnp.sqrt(total_sq + 1e-06))
    for j in range(out.shape[1] // DH):
        columns = slice(j * DH, (j + 1) * DH)
        out[:, columns] = weights[:, columns] * factor


def clip(weights, squares):
    return pl.pallas_call(
        clip_kernel,
        out_shape=struct(weights.shape, F32),
        in_specs=[VMEM, VMEM],
        out_specs=VMEM,
        compiler_params=pltpu.CompilerParams(vmem_limit_bytes=8 * MIB),
        cost_estimate=pl.CostEstimate(flops=MIB, bytes_accessed=MIB, transcendentals=0),
        name="clip",
    )(weights, squares)


def body(inputs, grad_out, w_qkv):
    user_count, row_count, feature_count = inputs.shape
    seqlen_total = row_count * lax.axis_size("seq")
    dp_count = lax.axis_size("dp")
    scaling = 1.0 / math.sqrt(DH * seqlen_total)
    index = lax.axis_index("seq")
    y, x, c = index // GROUP, (index // 2) % NX, index % 2
    place = jnp.stack([y, x, c])
    head = x * 2 + c
    total_rows = user_count * row_count

    to_right, to_left, to_other = messages(place, inputs, grad_out)
    left = send(to_right, dx=1)
    right = send(to_left, dx=-1)
    other = send(to_other, dc=1)
    far_low = send(left[:10], dx=1)
    far_high = send(right[:10], dx=-1)
    left_other = send(left, dc=1)
    right_other = send(right, dc=1)
    far_low_other = send(far_low, dc=1)
    far_high_other = send(far_high, dc=1)

    w_head = jnp.concatenate(
        [head_columns(w_qkv, part * H + head) for part in range(3)], axis=1
    )
    own_units = ((0, None, 0, 0), (0, None, 0, 0), (2, 0, 16, 0), (2, 8, 17, 0))
    left_units = ((0, 0, 18, 2), (0, 10, 19, 2), (1, 0, 18, 2), (1, 10, 19, 2))
    right_units = ((0, 10, 18, 2), (0, 0, 19, 2), (1, 10, 18, 2), (1, 0, 19, 2))
    far_units = ((0, 0, 8, 1), (1, 0, 8, 1), (2, 0, 8, 1), (3, 0, 8, 1))
    far_sources = (far_low, far_high, far_low_other, far_high_other)
    parts = [
        blocks(place, w_head, (inputs, grad_out, other), own_units),
        blocks(place, w_head, (left, left_other), left_units),
        blocks(place, w_head, far_sources, far_units),
        blocks(place, w_head, (right, right_other), right_units),
    ]
    sent = totals(place, [part[3] for part in parts], [part[4] for part in parts])
    arrived = [send(sent[dy - 1], dy=dy) for dy in range(1, NY)]
    grad_proj, *pieces = gradients(place, arrived, parts, scaling, user_count, dp_count)

    folded = fold([pieces[0]] + [send(pieces[dy], dy=dy) for dy in range(1, NY)])
    planes = [
        [z * NY * GROUP + plane * GROUP + t for z in range(dp_count) for t in range(GROUP)]
        for plane in range(NY)
    ]
    got = lax.all_to_all(folded, ("dp", "seq"), 0, 0, axis_index_groups=planes)

    span = 2 * total_rows
    back = [grad_proj[:span].astype(F32)]
    for dx in range(1, NX):
        back.append(send(grad_proj[dx * span : (dx + 1) * span].astype(F32), dx=-dx))
    swap = send(jnp.stack([piece[total_rows:] for piece in back]), dc=1)
    grad_rows, done = input_gradient(place, back, swap, w_qkv)
    grad_inputs = grad_rows.reshape(user_count, row_count, feature_count)

    device_count = dp_count * lax.axis_size("seq")
    weights, squares = collect(got, done, device_count)
    squares = lax.all_to_all(squares, ("dp", "seq"), 0, 0, tiled=True)
    return (grad_inputs, clip(weights, squares))


def solution(mesh):
    in_specs = (P("dp", "seq", None), P("dp", "seq", None), P())
    out_specs = (P("dp", "seq", None), P(("dp", "seq"), None))
    return jax.shard_map(body, mesh=mesh, in_specs=in_specs, out_specs=out_specs, check_vma=False)
```

```python
import functools
import math

import jax
import jax.numpy as jnp
from jax import lax
from jax.experimental import pallas as pl
from jax.experimental.pallas import tpu as pltpu
from jax.sharding import PartitionSpec as P

H = 8
DH = 128
D = 1024
NY = 4
NX = 4
GROUP = 2 * NX
BF16 = jnp.bfloat16
F32 = jnp.float32
VMEM = pl.BlockSpec(memory_space=pltpu.VMEM)
SMEM = pl.BlockSpec(memory_space=pltpu.SMEM)
ANY = pl.BlockSpec(memory_space=pl.ANY)
MIB = 1 << 20


def seq_perm(dy, dx, dc):
    moves = []
    for y in range(NY):
        for x in range(NX):
            for c in range(2):
                source = (y * NX + x) * 2 + c
                target = (((y + dy) % NY) * NX + (x + dx) % NX) * 2 + (c ^ dc)
                moves.append((source, target))
    return moves


def send(value, dy=0, dx=0, dc=0):
    return lax.ppermute(value, "seq", seq_perm(dy, dx, dc))


def head_columns(array, head):
    return lax.dynamic_slice_in_dim(array, head * DH, DH, 1)


def struct(shape, dtype):
    return jax.ShapeDtypeStruct(shape, dtype)


def dot(a, b, over_a, over_b):
    return lax.dot_general(a, b, (((over_a,), (over_b,)), ((), ())), preferred_element_type=F32)


def message_kernel(place, inputs, grad_out, right, left, cross):
    x, c = place[1], place[2]

    def cot(user, dx, core):
        head = ((x + dx) % NX) * 2 + core
        return grad_out[user, :, pl.ds(pl.multiple_of(head * DH, DH), DH)].astype(F32)

    for user in range(2):
        passed, kept = (right, left) if user == 0 else (left, right)
        for j in range(H):
            value = inputs[user, :, j * DH : (j + 1) * DH].astype(F32)
            passed[j] = value
            kept[10 + j] = value
            cross[user * H + j] = value
        for core in range(2):
            passed[8 + core] = cot(user, 2, core)
            right[18 + 2 * core + user] = cot(user, 1, core)
            left[18 + 2 * core + user] = cot(user, NX - 1, core)
        cross[2 * H + user] = cot(user, 0, 1 - c)


def messages(place, inputs, grad_out):
    size = inputs.shape[1]
    return pl.pallas_call(
        message_kernel,
        out_shape=tuple(struct((count, size, DH), F32) for count in (22, 22, 18)),
        in_specs=[SMEM, VMEM, VMEM],
        out_specs=(VMEM,) * 3,
        compiler_params=pltpu.CompilerParams(vmem_limit_bytes=16 * MIB),
        cost_estimate=pl.CostEstimate(flops=MIB, bytes_accessed=3 * MIB, transcendentals=0),
        name="messages",
    )(place, inputs, grad_out)


def relay_kernel(cuts, *refs):
    sources, outs = refs
    for out, source, first, last, at in cuts:
        outs[out][at : at + last - first] = sources[source][first:last].astype(outs[out].dtype)


def relay(sources, shapes, cuts, after=()):
    def kernel(*refs):
        relay_kernel(cuts, refs[: len(sources)], refs[len(sources) + len(after) :])

    return pl.pallas_call(
        kernel,
        out_shape=tuple(struct(shape, F32) for shape in shapes),
        in_specs=[VMEM] * len(sources) + [ANY] * len(after),
        out_specs=(VMEM,) * len(shapes),
        compiler_params=pltpu.CompilerParams(vmem_limit_bytes=12 * MIB),
        cost_estimate=pl.CostEstimate(flops=MIB, bytes_accessed=2 * MIB, transcendentals=0),
        name="relay",
    )(*sources, *after)


def block_kernel(units, place, w, *refs):
    sources, refs = refs[:-7], refs[-7:]
    rows_t, proj, cot_half, key_state, query_state, intra, x_all = refs
    x, c = place[1], place[2]
    features, total = rows_t.shape
    size = total // len(units)
    causal = lax.broadcasted_iota(jnp.int32, (size, size), 0) >= lax.broadcasted_iota(
        jnp.int32, (size, size), 1
    )
    for n, (source, start, cot_start, cot_step) in enumerate(units):
        here = slice(n * size, (n + 1) * size)
        if start is None:
            x_all[here, :] = sources[source][n]
            columns = pl.ds(pl.multiple_of((x * 2 + c) * DH, DH), DH)
            cot_half[here, :] = sources[source + 1][n, :, columns]
        else:
            for j in range(features // DH):
                x_all[here, j * DH : (j + 1) * DH] = sources[source][start + j].astype(BF16)
            cot_half[here, :] = sources[source][cot_start + cot_step * c].astype(BF16)
    rows = x_all[...]
    proj[...] = dot(rows, w[...], 1, 0).astype(BF16)
    rows_t[...] = rows.T
    for n in range(len(units)):
        here = slice(n * size, (n + 1) * size)
        i, u = n // 2, n % 2
        q, k, v = (proj[here, part * DH : (part + 1) * DH] for part in range(3))
        g = cot_half[here, :]
        key_state[i, u] = dot(k, v, 0, 0)
        query_state[i, u] = dot(q, g, 0, 0)
        out_value = jnp.where(causal, dot(g, v, 1, 1), 0.0).astype(BF16)
        query_key = jnp.where(causal, dot(q, k, 1, 1), 0.0).astype(BF16)
        intra[here, :DH] = dot(out_value, k, 1, 0)
        intra[here, DH : 2 * DH] = dot(out_value, q, 0, 0)
        intra[here, 2 * DH :] = dot(query_key, g, 0, 0)


def blocks(place, w_head, sources, units):
    features = w_head.shape[0]
    size = sources[0].shape[1]
    total = len(units) * size
    return pl.pallas_call(
        functools.partial(block_kernel, units),
        out_shape=(
            struct((features, total), BF16),
            struct((total, 3 * DH), BF16),
            struct((total, DH), BF16),
            struct((len(units) // 2, 2, DH, DH), F32),
            struct((len(units) // 2, 2, DH, DH), F32),
            struct((total, 3 * DH), F32),
        ),
        in_specs=[SMEM] + [VMEM] * (1 + len(sources)),
        out_specs=(VMEM,) * 6,
        scratch_shapes=[pltpu.VMEM((total, features), BF16)],
        compiler_params=pltpu.CompilerParams(vmem_limit_bytes=24 * MIB),
        cost_estimate=pl.CostEstimate(
            flops=2 * total * features * 3 * DH, bytes_accessed=4 * MIB, transcendentals=0
        ),
        name="blocks",
    )(place, w_head, *sources)


def total_kernel(place, *refs):
    count = (len(refs) - NY + 1) // 2
    keys, queries, outs = refs[:count], refs[count : 2 * count], refs[2 * count :]
    key_total = sum(ref[i] for ref in keys for i in range(ref.shape[0]))
    query_total = sum(ref[i] for ref in queries for i in range(ref.shape[0]))
    for dy in range(1, NY):
        outs[dy - 1][...] = jnp.where(place[0] + dy < NY, key_total, query_total)


def totals(place, key_states, query_states):
    shape = key_states[0].shape[1:]
    return pl.pallas_call(
        total_kernel,
        out_shape=(struct(shape, F32),) * (NY - 1),
        in_specs=[SMEM] + [VMEM] * (2 * len(key_states)),
        out_specs=(VMEM,) * (NY - 1),
        compiler_params=pltpu.CompilerParams(vmem_limit_bytes=16 * MIB),
        cost_estimate=pl.CostEstimate(flops=MIB, bytes_accessed=3 * MIB, transcendentals=0),
        name="totals",
    )(place, *key_states, *query_states)


def grad_kernel(scaling, users, dp_count, count, place, *refs):
    y, x, c = place[0], place[1], place[2]
    arrived, refs = refs[: NY - 1], refs[NY - 1 :]
    keys, refs = refs[:count], refs[count:]
    queries, refs = refs[:count], refs[count:]
    rows_t, refs = refs[:count], refs[count:]
    proj, refs = refs[:count], refs[count:]
    cots, refs = refs[:count], refs[count:]
    intra, refs = refs[:count], refs[count:]
    grad_proj, give, pieces, refs = refs[0], refs[1], refs[2 : 2 + NY], refs[2 + NY :]
    key_all, query_all, prior_all, later_all, product = refs
    first = 0
    for part in range(count):
        last = first + keys[part].shape[0]
        key_all[first:last] = keys[part][...]
        query_all[first:last] = queries[part][...]
        first = last
    prior = jnp.zeros(arrived[0].shape, F32)
    later = jnp.zeros(arrived[0].shape, F32)
    for dy in range(1, NY):
        value = arrived[dy - 1][...]
        prior = prior + jnp.where(y >= dy, value, 0.0)
        later = later + jnp.where(y >= dy, 0.0, value)

    def slot(position):
        return ((x + NX - position // 2) % NX) * 2 + (c ^ (position % 2))

    for position in range(GROUP):
        here = slot(position)
        prior_all[here] = prior.astype(BF16)
        prior = prior + key_all[here]
    for position in reversed(range(GROUP)):
        here = slot(position)
        later_all[here] = later.astype(BF16)
        later = later + query_all[here]
    size = intra[0].shape[0] // (keys[0].shape[0] * users)
    block = 0
    for part in range(count):
        for i in range(keys[part].shape[0]):
            for u in range(users):
                here = slice((i * users + u) * size, (i * users + u + 1) * size)
                there = slice((block * users + u) * size, (block * users + u + 1) * size)
                k, v = proj[part][here, DH : 2 * DH], proj[part][here, 2 * DH :]
                prior_state, later_state = prior_all[block, u], later_all[block, u]
                inter = (
                    dot(cots[part][here, :], prior_state, 1, 1),
                    dot(v, later_state, 1, 1),
                    dot(k, later_state, 1, 0),
                )
                for kind in range(3):
                    columns = slice(kind * DH, (kind + 1) * DH)
                    grad_proj[there, columns] = (
                        scaling * (intra[part][here, columns] + inter[kind])
                    ).astype(BF16)
            block += 1
    total = users * size
    for dx in range(NX):
        there = slice((2 * dx + 1) * total, (2 * dx + 2) * total)
        give[dx * total : (dx + 1) * total, :] = grad_proj[there, :].astype(F32)
    value, first = 0.0, 0
    for part in range(count):
        last = first + rows_t[part].shape[1]
        value = value + dot(rows_t[part][...], grad_proj[first:last, :], 1, 0)
        first = last
    product[...] = value
    row_block = product.shape[0] // (dp_count * NY)
    for dy in range(NY):
        target = (y + dy) % NY
        for z in range(dp_count):
            start = pl.multiple_of((z * NY + target) * row_block, row_block)
            pieces[dy][z] = product[pl.ds(start, row_block), :]


def gradients(place, arrived, parts, scaling, users, dp_count):
    rows_t, proj, cots, keys, queries, intra = zip(*parts)
    features = rows_t[0].shape[0]
    rows = sum(part.shape[1] for part in rows_t)
    row_block = features // (dp_count * NY)
    count = len(parts)
    return pl.pallas_call(
        functools.partial(grad_kernel, scaling, users, dp_count, count),
        out_shape=(struct((rows, 3 * DH), BF16), struct((rows // 2, 3 * DH), F32))
        + (struct((dp_count, row_block, 3 * DH), F32),) * NY,
        in_specs=[SMEM] + [VMEM] * (NY - 1 + 6 * count),
        out_specs=(VMEM,) * (2 + NY),
        scratch_shapes=[
            pltpu.VMEM((GROUP, users, DH, DH), F32),
            pltpu.VMEM((GROUP, users, DH, DH), F32),
            pltpu.VMEM((GROUP, users, DH, DH), BF16),
            pltpu.VMEM((GROUP, users, DH, DH), BF16),
            pltpu.VMEM((features, 3 * DH), F32),
        ],
        compiler_params=pltpu.CompilerParams(vmem_limit_bytes=32 * MIB),
        cost_estimate=pl.CostEstimate(
            flops=2 * rows * features * 3 * DH, bytes_accessed=10 * MIB, transcendentals=0
        ),
        name="gradients",
    )(place, *arrived, *keys, *queries, *rows_t, *proj, *cots, *intra)


def input_kernel(place, *refs):
    x, c = place[1], place[2]
    own, theirs, back = refs[0], refs[1], refs[2 : 1 + NX]
    w, out, done, full = refs[1 + NX :]
    total = out.shape[0]
    for dx in range(NX):
        for dc in range(2):
            head = ((x + dx) % NX) * 2 + (c ^ dc)
            source = (theirs if dc else own) if dx == 0 else back[dx - 1]
            first = total if dx and dc else 0
            for part in range(3):
                columns = slice(part * DH, (part + 1) * DH)
                start = pl.multiple_of((part * H + head) * DH, DH)
                full[:, pl.ds(start, DH)] = source[first : first + total, columns].astype(BF16)
    out[...] = dot(full[...], w[...], 1, 1).astype(BF16)
    done[...] = jnp.zeros(done.shape, F32)


def input_gradient(place, sources, total, w_qkv):
    features, width = w_qkv.shape
    return pl.pallas_call(
        input_kernel,
        out_shape=(struct((total, features), BF16), struct((8, DH), F32)),
        in_specs=[SMEM] + [VMEM] * (len(sources) + 1),
        out_specs=(VMEM, VMEM),
        scratch_shapes=[pltpu.VMEM((total, width), BF16)],
        compiler_params=pltpu.CompilerParams(vmem_limit_bytes=24 * MIB),
        cost_estimate=pl.CostEstimate(
            flops=16 * total * features * width, bytes_accessed=80 * MIB, transcendentals=0
        ),
        name="input_gradient",
    )(place, *sources, w_qkv)


def fold_kernel(count, *refs):
    out = refs[-1]
    dp_count, row_block = refs[0].shape[0], refs[0].shape[1]
    rows = out.shape[1]
    for z in range(dp_count):
        value = sum(ref[z] for ref in refs[:count])
        for t in range(GROUP):
            out[z * GROUP + t] = value[t * rows : (t + 1) * rows, :]


def fold(parts, after):
    dp_count, row_block, width = parts[0].shape
    return pl.pallas_call(
        functools.partial(fold_kernel, len(parts)),
        out_shape=struct((dp_count * GROUP, row_block // GROUP, width), F32),
        in_specs=[VMEM] * len(parts) + [ANY],
        out_specs=VMEM,
        compiler_params=pltpu.CompilerParams(vmem_limit_bytes=8 * MIB),
        cost_estimate=pl.CostEstimate(flops=MIB, bytes_accessed=2 * MIB, transcendentals=0),
        name="fold",
    )(*parts, after)


def square_kernel(got, after, squares):
    count = got.shape[0] // H
    lanes = jnp.zeros((1, got.shape[2]), F32)
    for head in range(H):
        value = sum(got[z * H + head] for z in range(count))
        lanes = lanes + jnp.sum(value * value, axis=0, keepdims=True)
    squares[...] = jnp.full(squares.shape, jnp.sum(lanes))


def square_sum(got, after, device_count):
    return pl.pallas_call(
        square_kernel,
        out_shape=struct((device_count, DH), F32),
        in_specs=[VMEM, ANY],
        out_specs=VMEM,
        compiler_params=pltpu.CompilerParams(vmem_limit_bytes=8 * MIB),
        cost_estimate=pl.CostEstimate(flops=MIB, bytes_accessed=MIB, transcendentals=0),
        name="square_sum",
    )(got, after)


def assemble_kernel(got, after, weights):
    count = got.shape[0] // H
    for head in range(H):
        value = sum(got[z * H + head] for z in range(count))
        for part in range(3):
            start = (part * H + head) * DH
            weights[:, start : start + DH] = value[:, part * DH : (part + 1) * DH]


def assemble(got, after):
    rows, width = got.shape[1], got.shape[2]
    return pl.pallas_call(
        assemble_kernel,
        out_shape=struct((rows, H * width), F32),
        in_specs=[VMEM, ANY],
        out_specs=VMEM,
        compiler_params=pltpu.CompilerParams(vmem_limit_bytes=8 * MIB),
        cost_estimate=pl.CostEstimate(flops=MIB, bytes_accessed=MIB, transcendentals=0),
        name="assemble",
    )(got, after)


def clip_kernel(weights, squares, out):
    total_sq = jnp.sum(squares[...], axis=0, keepdims=True)
    factor = jnp.minimum(1.0, D / jnp.sqrt(total_sq + 1e-06))
    for j in range(out.shape[1] // DH):
        columns = slice(j * DH, (j + 1) * DH)
        out[:, columns] = weights[:, columns] * factor


def clip(weights, squares):
    return pl.pallas_call(
        clip_kernel,
        out_shape=struct(weights.shape, F32),
        in_specs=[VMEM, VMEM],
        out_specs=VMEM,
        compiler_params=pltpu.CompilerParams(vmem_limit_bytes=8 * MIB),
        cost_estimate=pl.CostEstimate(flops=MIB, bytes_accessed=MIB, transcendentals=0),
        name="clip",
    )(weights, squares)


def body(inputs, grad_out, w_qkv):
    user_count, row_count, feature_count = inputs.shape
    seqlen_total = row_count * lax.axis_size("seq")
    dp_count = lax.axis_size("dp")
    scaling = 1.0 / math.sqrt(DH * seqlen_total)
    index = lax.axis_index("seq")
    y, x, c = index // GROUP, (index // 2) % NX, index % 2
    place = jnp.stack([y, x, c])
    head = x * 2 + c
    total_rows = user_count * row_count

    to_right, to_left, to_other = messages(place, inputs, grad_out)
    left = send(to_right, dx=1)
    right = send(to_left, dx=-1)
    other = send(to_other, dc=1)
    w_head = jnp.concatenate(
        [head_columns(w_qkv, part * H + head) for part in range(3)], axis=1
    )
    own_units = ((0, None, 0, 0), (0, None, 0, 0), (2, 0, 16, 0), (2, 8, 17, 0))
    left_units = ((0, 0, 18, 2), (0, 10, 19, 2), (1, 0, 18, 2), (1, 10, 19, 2))
    right_units = ((0, 10, 18, 2), (0, 0, 19, 2), (1, 10, 18, 2), (1, 0, 19, 2))
    far_units = ((0, 0, 8, 1), (0, 10, 18, 1))
    own_part = blocks(place, w_head, (inputs, grad_out, other), own_units)

    far_low = send(left[:10], dx=1)
    far_high = send(right[:10], dx=-1)
    count = left.shape[0]
    crossing = relay(
        (left, right),
        (left.shape, right.shape),
        ((0, 0, 0, count, 0), (1, 1, 0, count, 0)),
        (own_part[3],),
    )
    left_other, right_other = (send(value, dc=1) for value in crossing)
    left_part = blocks(place, w_head, (left, left_other), left_units)
    right_part = blocks(place, w_head, (right, right_other), right_units)
    (far,) = relay(
        (far_low, far_high),
        ((20,) + left.shape[1:],),
        ((0, 0, 0, 10, 0), (0, 1, 0, 10, 10)),
        (own_part[3], left_part[3], right_part[3]),
    )
    far_other = send(far, dc=1)
    parts = [
        own_part,
        left_part,
        blocks(place, w_head, (far,), far_units),
        blocks(place, w_head, (far_other,), far_units),
        right_part,
    ]
    sent = totals(place, [part[3] for part in parts], [part[4] for part in parts])
    arrived = [send(sent[dy - 1], dy=dy) for dy in range(1, NY)]
    grad_proj, give, *pieces = gradients(place, arrived, parts, scaling, user_count, dp_count)

    span = 2 * total_rows
    theirs = send(give, dc=1)
    returns = relay(
        (grad_proj, theirs),
        ((span, 3 * DH),) * (NX - 1),
        tuple((dx - 1, 0, dx * span, dx * span + total_rows, 0) for dx in range(1, NX))
        + tuple(
            (dx - 1, 1, dx * total_rows, (dx + 1) * total_rows, total_rows)
            for dx in range(1, NX)
        ),
    )
    back = [send(returns[dx - 1], dx=-dx) for dx in range(1, NX)]
    summands = [pieces[0]] + [send(pieces[dy], dy=dy) for dy in range(1, NY)]
    folded = fold(summands, returns[0])
    planes = [
        [z * NY * GROUP + plane * GROUP + t for z in range(dp_count) for t in range(GROUP)]
        for plane in range(NY)
    ]
    got = lax.all_to_all(folded, ("dp", "seq"), 0, 0, axis_index_groups=planes)

    grad_rows, done = input_gradient(place, (grad_proj, theirs, *back), total_rows, w_qkv)
    grad_inputs = grad_rows.reshape(user_count, row_count, feature_count)

    squares = square_sum(got, done, dp_count * lax.axis_size("seq"))
    weights = assemble(got, squares)
    squares = lax.all_to_all(squares, ("dp", "seq"), 0, 0, tiled=True)
    return (grad_inputs, clip(weights, squares))


def solution(mesh):
    in_specs = (P("dp", "seq", None), P("dp", "seq", None), P())
    out_specs = (P("dp", "seq", None), P(("dp", "seq"), None))
    return jax.shard_map(body, mesh=mesh, in_specs=in_specs, out_specs=out_specs, check_vma=False)
```

```python
import functools
import math

import jax
import jax.numpy as jnp
from jax import lax
from jax.experimental import pallas as pl
from jax.experimental.pallas import tpu as pltpu
from jax.sharding import PartitionSpec as P

H = 8
DH = 128
D = 1024
NY = 4
NX = 4
GROUP = 2 * NX
FAR_FIRST = (2, 1, 3)
BF16 = jnp.bfloat16
F32 = jnp.float32
VMEM = pl.BlockSpec(memory_space=pltpu.VMEM)
SMEM = pl.BlockSpec(memory_space=pltpu.SMEM)
ANY = pl.BlockSpec(memory_space=pl.ANY)
MIB = 1 << 20


def seq_perm(dy, dx, dc):
    moves = []
    for y in range(NY):
        for x in range(NX):
            for c in range(2):
                source = (y * NX + x) * 2 + c
                target = (((y + dy) % NY) * NX + (x + dx) % NX) * 2 + (c ^ dc)
                moves.append((source, target))
    return moves


def send(value, dy=0, dx=0, dc=0):
    return lax.ppermute(value, "seq", seq_perm(dy, dx, dc))


def head_columns(array, head):
    return lax.dynamic_slice_in_dim(array, head * DH, DH, 1)


def struct(shape, dtype):
    return jax.ShapeDtypeStruct(shape, dtype)


def dot(a, b, over_a, over_b):
    return lax.dot_general(a, b, (((over_a,), (over_b,)), ((), ())), preferred_element_type=F32)


def message_kernel(place, inputs, grad_out, right, left, cross):
    x, c = place[1], place[2]

    def cot(user, dx, core):
        head = ((x + dx) % NX) * 2 + core
        return grad_out[user, :, pl.ds(pl.multiple_of(head * DH, DH), DH)].astype(F32)

    for user in range(2):
        passed, kept = (right, left) if user == 0 else (left, right)
        for j in range(H):
            value = inputs[user, :, j * DH : (j + 1) * DH].astype(F32)
            passed[j] = value
            kept[10 + j] = value
            cross[user * H + j] = value
        for core in range(2):
            passed[8 + core] = cot(user, 2, core)
            right[18 + 2 * core + user] = cot(user, 1, core)
            left[18 + 2 * core + user] = cot(user, NX - 1, core)
        cross[2 * H + user] = cot(user, 0, 1 - c)


def messages(place, inputs, grad_out):
    size = inputs.shape[1]
    return pl.pallas_call(
        message_kernel,
        out_shape=tuple(struct((count, size, DH), F32) for count in (22, 22, 18)),
        in_specs=[SMEM, VMEM, VMEM],
        out_specs=(VMEM,) * 3,
        compiler_params=pltpu.CompilerParams(vmem_limit_bytes=16 * MIB),
        cost_estimate=pl.CostEstimate(flops=MIB, bytes_accessed=3 * MIB, transcendentals=0),
        name="messages",
    )(place, inputs, grad_out)


def relay_kernel(cuts, *refs):
    sources, outs = refs
    for out, source, first, last, at in cuts:
        outs[out][at : at + last - first] = sources[source][first:last].astype(outs[out].dtype)


def relay(sources, shapes, cuts, after=()):
    def kernel(*refs):
        relay_kernel(cuts, refs[: len(sources)], refs[len(sources) + len(after) :])

    return pl.pallas_call(
        kernel,
        out_shape=tuple(struct(shape, F32) for shape in shapes),
        in_specs=[VMEM] * len(sources) + [ANY] * len(after),
        out_specs=(VMEM,) * len(shapes),
        compiler_params=pltpu.CompilerParams(vmem_limit_bytes=12 * MIB),
        cost_estimate=pl.CostEstimate(flops=MIB, bytes_accessed=2 * MIB, transcendentals=0),
        name="relay",
    )(*sources, *after)


def block_kernel(units, place, w, *refs):
    sources, refs = refs[:-7], refs[-7:]
    rows_t, proj, cot_half, key_state, query_state, intra, x_all = refs
    x, c = place[1], place[2]
    features, total = rows_t.shape
    size = total // len(units)
    causal = lax.broadcasted_iota(jnp.int32, (size, size), 0) >= lax.broadcasted_iota(
        jnp.int32, (size, size), 1
    )
    for n, (source, start, cot_start, cot_step) in enumerate(units):
        here = slice(n * size, (n + 1) * size)
        if start is None:
            x_all[here, :] = sources[source][n]
            columns = pl.ds(pl.multiple_of((x * 2 + c) * DH, DH), DH)
            cot_half[here, :] = sources[source + 1][n, :, columns]
        else:
            for j in range(features // DH):
                x_all[here, j * DH : (j + 1) * DH] = sources[source][start + j].astype(BF16)
            cot_half[here, :] = sources[source][cot_start + cot_step * c].astype(BF16)
    rows = x_all[...]
    proj[...] = dot(rows, w[...], 1, 0).astype(BF16)
    rows_t[...] = rows.T
    for n in range(len(units)):
        here = slice(n * size, (n + 1) * size)
        i, u = n // 2, n % 2
        q, k, v = (proj[here, part * DH : (part + 1) * DH] for part in range(3))
        g = cot_half[here, :]
        key_state[i, u] = dot(k, v, 0, 0)
        query_state[i, u] = dot(q, g, 0, 0)
        out_value = jnp.where(causal, dot(g, v, 1, 1), 0.0).astype(BF16)
        query_key = jnp.where(causal, dot(q, k, 1, 1), 0.0).astype(BF16)
        intra[here, :DH] = dot(out_value, k, 1, 0)
        intra[here, DH : 2 * DH] = dot(out_value, q, 0, 0)
        intra[here, 2 * DH :] = dot(query_key, g, 0, 0)


def blocks(place, w_head, sources, units):
    features = w_head.shape[0]
    size = sources[0].shape[1]
    total = len(units) * size
    return pl.pallas_call(
        functools.partial(block_kernel, units),
        out_shape=(
            struct((features, total), BF16),
            struct((total, 3 * DH), BF16),
            struct((total, DH), BF16),
            struct((len(units) // 2, 2, DH, DH), F32),
            struct((len(units) // 2, 2, DH, DH), F32),
            struct((total, 3 * DH), F32),
        ),
        in_specs=[SMEM] + [VMEM] * (1 + len(sources)),
        out_specs=(VMEM,) * 6,
        scratch_shapes=[pltpu.VMEM((total, features), BF16)],
        compiler_params=pltpu.CompilerParams(vmem_limit_bytes=24 * MIB),
        cost_estimate=pl.CostEstimate(
            flops=2 * total * features * 3 * DH, bytes_accessed=4 * MIB, transcendentals=0
        ),
        name="blocks",
    )(place, w_head, *sources)


def total_kernel(place, *refs):
    count = (len(refs) - NY + 1) // 2
    keys, queries, outs = refs[:count], refs[count : 2 * count], refs[2 * count :]
    key_total = sum(ref[i] for ref in keys for i in range(ref.shape[0]))
    query_total = sum(ref[i] for ref in queries for i in range(ref.shape[0]))
    for out, dy in zip(outs, FAR_FIRST):
        out[...] = jnp.where(place[0] + dy < NY, key_total, query_total)


def totals(place, key_states, query_states):
    shape = key_states[0].shape[1:]
    return pl.pallas_call(
        total_kernel,
        out_shape=(struct(shape, F32),) * (NY - 1),
        in_specs=[SMEM] + [VMEM] * (2 * len(key_states)),
        out_specs=(VMEM,) * (NY - 1),
        compiler_params=pltpu.CompilerParams(vmem_limit_bytes=16 * MIB),
        cost_estimate=pl.CostEstimate(flops=MIB, bytes_accessed=3 * MIB, transcendentals=0),
        name="totals",
    )(place, *key_states, *query_states)


def grad_kernel(scaling, users, dp_count, count, place, *refs):
    y, x, c = place[0], place[1], place[2]
    arrived, refs = refs[: NY - 1], refs[NY - 1 :]
    keys, refs = refs[:count], refs[count:]
    queries, refs = refs[:count], refs[count:]
    rows_t, refs = refs[:count], refs[count:]
    proj, refs = refs[:count], refs[count:]
    cots, refs = refs[:count], refs[count:]
    intra, refs = refs[:count], refs[count:]
    grad_proj, give, pieces, refs = refs[0], refs[1], refs[2 : 2 + NY], refs[2 + NY :]
    key_all, query_all, prior_all, later_all, product = refs
    first = 0
    for part in range(count):
        last = first + keys[part].shape[0]
        key_all[first:last] = keys[part][...]
        query_all[first:last] = queries[part][...]
        first = last
    prior = jnp.zeros(arrived[0].shape, F32)
    later = jnp.zeros(arrived[0].shape, F32)
    for ref, dy in zip(arrived, FAR_FIRST):
        value = ref[...]
        prior = prior + jnp.where(y >= dy, value, 0.0)
        later = later + jnp.where(y >= dy, 0.0, value)

    def slot(position):
        return ((x + NX - position // 2) % NX) * 2 + (c ^ (position % 2))

    for position in range(GROUP):
        here = slot(position)
        prior_all[here] = prior.astype(BF16)
        prior = prior + key_all[here]
    for position in reversed(range(GROUP)):
        here = slot(position)
        later_all[here] = later.astype(BF16)
        later = later + query_all[here]
    size = intra[0].shape[0] // (keys[0].shape[0] * users)
    block = 0
    for part in range(count):
        for i in range(keys[part].shape[0]):
            for u in range(users):
                here = slice((i * users + u) * size, (i * users + u + 1) * size)
                there = slice((block * users + u) * size, (block * users + u + 1) * size)
                k, v = proj[part][here, DH : 2 * DH], proj[part][here, 2 * DH :]
                prior_state, later_state = prior_all[block, u], later_all[block, u]
                inter = (
                    dot(cots[part][here, :], prior_state, 1, 1),
                    dot(v, later_state, 1, 1),
                    dot(k, later_state, 1, 0),
                )
                for kind in range(3):
                    columns = slice(kind * DH, (kind + 1) * DH)
                    grad_proj[there, columns] = (
                        scaling * (intra[part][here, columns] + inter[kind])
                    ).astype(BF16)
            block += 1
    total = users * size
    for dx in range(NX):
        there = slice((2 * dx + 1) * total, (2 * dx + 2) * total)
        give[dx * total : (dx + 1) * total, :] = grad_proj[there, :].astype(F32)
    value, first = 0.0, 0
    for part in range(count):
        last = first + rows_t[part].shape[1]
        value = value + dot(rows_t[part][...], grad_proj[first:last, :], 1, 0)
        first = last
    product[...] = value
    row_block = product.shape[0] // (dp_count * NY)
    for piece, dy in zip(pieces, (0,) + FAR_FIRST):
        target = (y + dy) % NY
        for z in range(dp_count):
            start = pl.multiple_of((z * NY + target) * row_block, row_block)
            piece[z] = product[pl.ds(start, row_block), :]


def gradients(place, arrived, parts, scaling, users, dp_count):
    rows_t, proj, cots, keys, queries, intra = zip(*parts)
    features = rows_t[0].shape[0]
    rows = sum(part.shape[1] for part in rows_t)
    row_block = features // (dp_count * NY)
    count = len(parts)
    return pl.pallas_call(
        functools.partial(grad_kernel, scaling, users, dp_count, count),
        out_shape=(struct((rows, 3 * DH), BF16), struct((rows // 2, 3 * DH), F32))
        + (struct((dp_count, row_block, 3 * DH), F32),) * NY,
        in_specs=[SMEM] + [VMEM] * (NY - 1 + 6 * count),
        out_specs=(VMEM,) * (2 + NY),
        scratch_shapes=[
            pltpu.VMEM((GROUP, users, DH, DH), F32),
            pltpu.VMEM((GROUP, users, DH, DH), F32),
            pltpu.VMEM((GROUP, users, DH, DH), BF16),
            pltpu.VMEM((GROUP, users, DH, DH), BF16),
            pltpu.VMEM((features, 3 * DH), F32),
        ],
        compiler_params=pltpu.CompilerParams(vmem_limit_bytes=32 * MIB),
        cost_estimate=pl.CostEstimate(
            flops=2 * rows * features * 3 * DH, bytes_accessed=10 * MIB, transcendentals=0
        ),
        name="gradients",
    )(place, *arrived, *keys, *queries, *rows_t, *proj, *cots, *intra)


def input_kernel(place, *refs):
    x, c = place[1], place[2]
    own, theirs, back = refs[0], refs[1], refs[2 : 1 + NX]
    w, out, done, full = refs[1 + NX :]
    total = out.shape[0]

    @pl.when(pl.program_id(0) == 0)
    def _():
        for dx in range(NX):
            for dc in range(2):
                head = ((x + dx) % NX) * 2 + (c ^ dc)
                source = (theirs if dc else own) if dx == 0 else back[dx - 1]
                first = total if dx and dc else 0
                for part in range(3):
                    columns = slice(part * DH, (part + 1) * DH)
                    start = pl.multiple_of((part * H + head) * DH, DH)
                    full[:, pl.ds(start, DH)] = source[first : first + total, columns].astype(BF16)
        done[...] = jnp.zeros(done.shape, F32)

    out[...] = dot(full[...], w[...], 1, 1).astype(BF16)


def input_gradient(place, sources, total, w_qkv):
    features, width = w_qkv.shape
    step = 256
    return pl.pallas_call(
        input_kernel,
        grid=(features // step,),
        out_shape=(struct((total, features), BF16), struct((8, DH), F32)),
        in_specs=[SMEM]
        + [VMEM] * len(sources)
        + [pl.BlockSpec((step, width), lambda i: (i, 0))],
        out_specs=(
            pl.BlockSpec((total, step), lambda i: (0, i)),
            pl.BlockSpec((8, DH), lambda i: (0, 0)),
        ),
        scratch_shapes=[pltpu.VMEM((total, width), BF16)],
        compiler_params=pltpu.CompilerParams(vmem_limit_bytes=48 * MIB),
        cost_estimate=pl.CostEstimate(
            flops=16 * total * features * width, bytes_accessed=80 * MIB, transcendentals=0
        ),
        name="input_gradient",
    )(place, *sources, w_qkv)


def fold_kernel(count, *refs):
    out = refs[-1]
    dp_count, row_block = refs[0].shape[0], refs[0].shape[1]
    rows = row_block // GROUP
    for z in range(dp_count):
        value = sum(ref[z] for ref in refs[:count])
        for t in range(GROUP):
            to = (t // 2) * rows
            out[2 * z + t % 2, to : to + rows, :] = value[t * rows : (t + 1) * rows, :]


def fold(parts, after):
    dp_count, row_block, width = parts[0].shape
    return pl.pallas_call(
        functools.partial(fold_kernel, len(parts)),
        out_shape=struct((dp_count * 2, row_block // 2, width), F32),
        in_specs=[VMEM] * len(parts) + [ANY],
        out_specs=VMEM,
        compiler_params=pltpu.CompilerParams(vmem_limit_bytes=8 * MIB),
        cost_estimate=pl.CostEstimate(flops=MIB, bytes_accessed=2 * MIB, transcendentals=0),
        name="fold",
    )(*parts, after)


def square_kernel(place, got, after, squares, *refs):
    x, pieces, rows_of = place[1], refs[:NX], refs[NX]
    count, rows = got.shape[0] // 2, got.shape[1] // NX
    lanes = jnp.zeros((1, got.shape[2]), F32)
    for core in range(2):
        value = sum(got[2 * z + core] for z in range(count))
        lanes = lanes + jnp.sum(value * value, axis=0, keepdims=True)
        for to in range(NX):
            rows_of[to, core * rows : (core + 1) * rows, :] = value[to * rows : (to + 1) * rows, :]
    squares[...] = jnp.full(squares.shape, jnp.sum(lanes))
    for dx in range(NX):
        pieces[dx][...] = rows_of[(x + dx) % NX]


def square_sum(place, got, after, device_count):
    rows, width = 2 * got.shape[1] // NX, got.shape[2]
    return pl.pallas_call(
        square_kernel,
        out_shape=(struct((device_count, DH), F32),) + (struct((rows, width), F32),) * NX,
        in_specs=[SMEM, VMEM, ANY],
        out_specs=(VMEM,) * (1 + NX),
        scratch_shapes=[pltpu.VMEM((NX, rows, width), F32)],
        compiler_params=pltpu.CompilerParams(vmem_limit_bytes=8 * MIB),
        cost_estimate=pl.CostEstimate(flops=MIB, bytes_accessed=MIB, transcendentals=0),
        name="square_sum",
    )(place, got, after)


def clip_kernel(place, squares, *refs):
    x, pieces, out = place[1], refs[:NX], refs[NX]
    rows = out.shape[0]
    total_sq = jnp.sum(squares[...], axis=0, keepdims=True)
    factor = jnp.minimum(1.0, D / jnp.sqrt(total_sq + 1e-06))
    for dx in range(NX):
        for core in range(2):
            head = ((x + NX - dx) % NX) * 2 + core
            for part in range(3):
                columns = slice(part * DH, (part + 1) * DH)
                start = pl.multiple_of((part * H + head) * DH, DH)
                value = pieces[dx][core * rows : (core + 1) * rows, columns]
                out[:, pl.ds(start, DH)] = value * factor


def clip(place, squares, pieces):
    rows, width = pieces[0].shape[0] // 2, pieces[0].shape[1] * H
    return pl.pallas_call(
        clip_kernel,
        out_shape=struct((rows, width), F32),
        in_specs=[SMEM] + [VMEM] * (1 + NX),
        out_specs=VMEM,
        compiler_params=pltpu.CompilerParams(vmem_limit_bytes=8 * MIB),
        cost_estimate=pl.CostEstimate(flops=MIB, bytes_accessed=MIB, transcendentals=0),
        name="clip",
    )(place, squares, *pieces)


def body(inputs, grad_out, w_qkv):
    user_count, row_count, feature_count = inputs.shape
    seqlen_total = row_count * lax.axis_size("seq")
    dp_count = lax.axis_size("dp")
    scaling = 1.0 / math.sqrt(DH * seqlen_total)
    index = lax.axis_index("seq")
    y, x, c = index // GROUP, (index // 2) % NX, index % 2
    place = jnp.stack([y, x, c])
    head = x * 2 + c
    total_rows = user_count * row_count

    to_right, to_left, to_other = messages(place, inputs, grad_out)
    left = send(to_right, dx=1)
    right = send(to_left, dx=-1)
    other = send(to_other, dc=1)
    w_head = jnp.concatenate(
        [head_columns(w_qkv, part * H + head) for part in range(3)], axis=1
    )
    own_units = ((0, None, 0, 0), (0, None, 0, 0), (2, 0, 16, 0), (2, 8, 17, 0))
    left_units = ((0, 0, 18, 2), (0, 10, 19, 2), (1, 0, 18, 2), (1, 10, 19, 2))
    right_units = ((0, 10, 18, 2), (0, 0, 19, 2), (1, 10, 18, 2), (1, 0, 19, 2))
    far_units = ((0, 0, 8, 1), (0, 10, 18, 1))
    own_part = blocks(place, w_head, (inputs, grad_out, other), own_units)

    far_low = send(left[:10], dx=1)
    far_high = send(right[:10], dx=-1)
    count = left.shape[0]
    crossing = relay(
        (left, right),
        (left.shape, right.shape),
        ((0, 0, 0, count, 0), (1, 1, 0, count, 0)),
        (own_part[3],),
    )
    left_other, right_other = (send(value, dc=1) for value in crossing)
    left_part = blocks(place, w_head, (left, left_other), left_units)
    right_part = blocks(place, w_head, (right, right_other), right_units)
    (far,) = relay(
        (far_low, far_high),
        ((20,) + left.shape[1:],),
        ((0, 0, 0, 10, 0), (0, 1, 0, 10, 10)),
        (own_part[3], left_part[3], right_part[3]),
    )
    far_other = send(far, dc=1)
    parts = [
        own_part,
        left_part,
        blocks(place, w_head, (far,), far_units),
        blocks(place, w_head, (far_other,), far_units),
        right_part,
    ]
    sent = totals(place, [part[3] for part in parts], [part[4] for part in parts])
    arrived = [send(value, dy=dy) for value, dy in zip(sent, FAR_FIRST)]
    grad_proj, give, *pieces = gradients(place, arrived, parts, scaling, user_count, dp_count)

    span = 2 * total_rows
    theirs = send(give, dc=1)
    returns = relay(
        (grad_proj, theirs),
        ((span, 3 * DH),) * (NX - 1),
        tuple((dx - 1, 0, dx * span, dx * span + total_rows, 0) for dx in range(1, NX))
        + tuple(
            (dx - 1, 1, dx * total_rows, (dx + 1) * total_rows, total_rows)
            for dx in range(1, NX)
        ),
    )
    back = [send(returns[dx - 1], dx=-dx) for dx in range(1, NX)]
    summands = pieces[:1] + [send(value, dy=dy) for value, dy in zip(pieces[1:], FAR_FIRST)]
    folded = fold(summands, returns[0])
    columns_of = [
        [z * NY * GROUP + place_of + core for z in range(dp_count) for core in range(2)]
        for place_of in range(0, NY * GROUP, 2)
    ]
    got = lax.all_to_all(folded, ("dp", "seq"), 0, 0, axis_index_groups=columns_of)
    grad_rows, done = input_gradient(place, (grad_proj, theirs, *back), total_rows, w_qkv)
    grad_inputs = grad_rows.reshape(user_count, row_count, feature_count)

    device_count = dp_count * lax.axis_size("seq")
    squares, *parts = square_sum(place, got, done, device_count)
    squares = lax.all_to_all(squares, ("dp", "seq"), 0, 0, tiled=True)
    parts = parts[:1] + [send(parts[dx], dx=dx) for dx in range(1, NX)]
    return (grad_inputs, clip(place, squares, parts))


def solution(mesh):
    in_specs = (P("dp", "seq", None), P("dp", "seq", None), P())
    out_specs = (P("dp", "seq", None), P(("dp", "seq"), None))
    return jax.shard_map(body, mesh=mesh, in_specs=in_specs, out_specs=out_specs, check_vma=False)
```

```python
import functools
import math

import jax
import jax.numpy as jnp
from jax import lax
from jax.experimental import pallas as pl
from jax.experimental.pallas import tpu as pltpu
from jax.sharding import PartitionSpec as P

H = 8
DH = 128
D = 1024
NY = 4
NX = 4
GROUP = 2 * NX
FAR_FIRST = (2, 1, 3)
BF16 = jnp.bfloat16
F32 = jnp.float32
VMEM = pl.BlockSpec(memory_space=pltpu.VMEM)
SMEM = pl.BlockSpec(memory_space=pltpu.SMEM)
ANY = pl.BlockSpec(memory_space=pl.ANY)
MIB = 1 << 20


def seq_perm(dy, dx, dc):
    moves = []
    for y in range(NY):
        for x in range(NX):
            for c in range(2):
                source = (y * NX + x) * 2 + c
                target = (((y + dy) % NY) * NX + (x + dx) % NX) * 2 + (c ^ dc)
                moves.append((source, target))
    return moves


def send(value, dy=0, dx=0, dc=0):
    return lax.ppermute(value, "seq", seq_perm(dy, dx, dc))


def head_columns(array, head):
    return lax.dynamic_slice_in_dim(array, head * DH, DH, 1)


def struct(shape, dtype):
    return jax.ShapeDtypeStruct(shape, dtype)


def dot(a, b, over_a, over_b):
    return lax.dot_general(a, b, (((over_a,), (over_b,)), ((), ())), preferred_element_type=F32)


def message_kernel(place, inputs, grad_out, right, left, cross):
    x, c = place[1], place[2]

    def cot(user, dx, core):
        head = ((x + dx) % NX) * 2 + core
        return grad_out[user, :, pl.ds(pl.multiple_of(head * DH, DH), DH)].astype(F32)

    for user in range(2):
        passed, kept = (right, left) if user == 0 else (left, right)
        for j in range(H):
            value = inputs[user, :, j * DH : (j + 1) * DH].astype(F32)
            passed[j] = value
            kept[10 + j] = value
            cross[user * H + j] = value
        for core in range(2):
            passed[8 + core] = cot(user, 2, core)
            right[18 + 2 * core + user] = cot(user, 1, core)
            left[18 + 2 * core + user] = cot(user, NX - 1, core)
        cross[2 * H + user] = cot(user, 0, 1 - c)


def messages(place, inputs, grad_out):
    size = inputs.shape[1]
    return pl.pallas_call(
        message_kernel,
        out_shape=tuple(struct((count, size, DH), F32) for count in (22, 22, 18)),
        in_specs=[SMEM, VMEM, VMEM],
        out_specs=(VMEM,) * 3,
        compiler_params=pltpu.CompilerParams(vmem_limit_bytes=16 * MIB),
        cost_estimate=pl.CostEstimate(flops=MIB, bytes_accessed=3 * MIB, transcendentals=0),
        name="messages",
    )(place, inputs, grad_out)


def relay_kernel(cuts, *refs):
    sources, outs = refs
    for out, source, first, last, at in cuts:
        outs[out][at : at + last - first] = sources[source][first:last].astype(outs[out].dtype)


def relay(sources, shapes, cuts, after=()):
    def kernel(*refs):
        relay_kernel(cuts, refs[: len(sources)], refs[len(sources) + len(after) :])

    return pl.pallas_call(
        kernel,
        out_shape=tuple(struct(shape, F32) for shape in shapes),
        in_specs=[VMEM] * len(sources) + [ANY] * len(after),
        out_specs=(VMEM,) * len(shapes),
        compiler_params=pltpu.CompilerParams(vmem_limit_bytes=12 * MIB),
        cost_estimate=pl.CostEstimate(flops=MIB, bytes_accessed=2 * MIB, transcendentals=0),
        name="relay",
    )(*sources, *after)


def block_kernel(units, place, w, *refs):
    sources, refs = refs[:-7], refs[-7:]
    rows_t, proj, cot_half, key_state, query_state, intra, x_all = refs
    x, c = place[1], place[2]
    features, total = rows_t.shape
    size = total // len(units)
    causal = lax.broadcasted_iota(jnp.int32, (size, size), 0) >= lax.broadcasted_iota(
        jnp.int32, (size, size), 1
    )
    for n, (source, start, cot_start, cot_step) in enumerate(units):
        here = slice(n * size, (n + 1) * size)
        if start is None:
            x_all[here, :] = sources[source][n]
            columns = pl.ds(pl.multiple_of((x * 2 + c) * DH, DH), DH)
            cot_half[here, :] = sources[source + 1][n, :, columns]
        else:
            for j in range(features // DH):
                x_all[here, j * DH : (j + 1) * DH] = sources[source][start + j].astype(BF16)
            cot_half[here, :] = sources[source][cot_start + cot_step * c].astype(BF16)
    rows = x_all[...]
    proj[...] = dot(rows, w[...], 1, 0).astype(BF16)
    rows_t[...] = rows.T
    for n in range(len(units)):
        here = slice(n * size, (n + 1) * size)
        i, u = n // 2, n % 2
        q, k, v = (proj[here, part * DH : (part + 1) * DH] for part in range(3))
        g = cot_half[here, :]
        key_state[i, u] = dot(k, v, 0, 0)
        query_state[i, u] = dot(q, g, 0, 0)
        out_value = jnp.where(causal, dot(g, v, 1, 1), 0.0).astype(BF16)
        query_key = jnp.where(causal, dot(q, k, 1, 1), 0.0).astype(BF16)
        intra[here, :DH] = dot(out_value, k, 1, 0)
        intra[here, DH : 2 * DH] = dot(out_value, q, 0, 0)
        intra[here, 2 * DH :] = dot(query_key, g, 0, 0)


def blocks(place, w_head, sources, units):
    features = w_head.shape[0]
    size = sources[0].shape[1]
    total = len(units) * size
    return pl.pallas_call(
        functools.partial(block_kernel, units),
        out_shape=(
            struct((features, total), BF16),
            struct((total, 3 * DH), BF16),
            struct((total, DH), BF16),
            struct((len(units) // 2, 2, DH, DH), F32),
            struct((len(units) // 2, 2, DH, DH), F32),
            struct((total, 3 * DH), F32),
        ),
        in_specs=[SMEM] + [VMEM] * (1 + len(sources)),
        out_specs=(VMEM,) * 6,
        scratch_shapes=[pltpu.VMEM((total, features), BF16)],
        compiler_params=pltpu.CompilerParams(vmem_limit_bytes=24 * MIB),
        cost_estimate=pl.CostEstimate(
            flops=2 * total * features * 3 * DH, bytes_accessed=4 * MIB, transcendentals=0
        ),
        name="blocks",
    )(place, w_head, *sources)


def total_kernel(place, *refs):
    count = (len(refs) - NY + 1) // 2
    keys, queries, outs = refs[:count], refs[count : 2 * count], refs[2 * count :]
    key_total = sum(ref[i] for ref in keys for i in range(ref.shape[0]))
    query_total = sum(ref[i] for ref in queries for i in range(ref.shape[0]))
    for out, dy in zip(outs, FAR_FIRST):
        out[...] = jnp.where(place[0] + dy < NY, key_total, query_total)


def totals(place, key_states, query_states):
    shape = key_states[0].shape[1:]
    return pl.pallas_call(
        total_kernel,
        out_shape=(struct(shape, F32),) * (NY - 1),
        in_specs=[SMEM] + [VMEM] * (2 * len(key_states)),
        out_specs=(VMEM,) * (NY - 1),
        compiler_params=pltpu.CompilerParams(vmem_limit_bytes=16 * MIB),
        cost_estimate=pl.CostEstimate(flops=MIB, bytes_accessed=3 * MIB, transcendentals=0),
        name="totals",
    )(place, *key_states, *query_states)


def grad_kernel(scaling, users, dp_count, count, place, *refs):
    y, x, c = place[0], place[1], place[2]
    arrived, refs = refs[: NY - 1], refs[NY - 1 :]
    keys, refs = refs[:count], refs[count:]
    queries, refs = refs[:count], refs[count:]
    rows_t, refs = refs[:count], refs[count:]
    proj, refs = refs[:count], refs[count:]
    cots, refs = refs[:count], refs[count:]
    intra, refs = refs[:count], refs[count:]
    grad_proj, give, pieces, refs = refs[0], refs[1], refs[2 : 2 + NY], refs[2 + NY :]
    key_all, query_all, prior_all, later_all, product = refs
    first = 0
    for part in range(count):
        last = first + keys[part].shape[0]
        key_all[first:last] = keys[part][...]
        query_all[first:last] = queries[part][...]
        first = last
    prior = jnp.zeros(arrived[0].shape, F32)
    later = jnp.zeros(arrived[0].shape, F32)
    for ref, dy in zip(arrived, FAR_FIRST):
        value = ref[...]
        prior = prior + jnp.where(y >= dy, value, 0.0)
        later = later + jnp.where(y >= dy, 0.0, value)

    def slot(position):
        return ((x + NX - position // 2) % NX) * 2 + (c ^ (position % 2))

    for position in range(GROUP):
        here = slot(position)
        prior_all[here] = prior.astype(BF16)
        prior = prior + key_all[here]
    for position in reversed(range(GROUP)):
        here = slot(position)
        later_all[here] = later.astype(BF16)
        later = later + query_all[here]
    size = intra[0].shape[0] // (keys[0].shape[0] * users)
    block = 0
    for part in range(count):
        for i in range(keys[part].shape[0]):
            for u in range(users):
                here = slice((i * users + u) * size, (i * users + u + 1) * size)
                there = slice((block * users + u) * size, (block * users + u + 1) * size)
                k, v = proj[part][here, DH : 2 * DH], proj[part][here, 2 * DH :]
                prior_state, later_state = prior_all[block, u], later_all[block, u]
                inter = (
                    dot(cots[part][here, :], prior_state, 1, 1),
                    dot(v, later_state, 1, 1),
                    dot(k, later_state, 1, 0),
                )
                for kind in range(3):
                    columns = slice(kind * DH, (kind + 1) * DH)
                    grad_proj[there, columns] = (
                        scaling * (intra[part][here, columns] + inter[kind])
                    ).astype(BF16)
            block += 1
    total = users * size
    for dx in range(NX):
        there = slice((2 * dx + 1) * total, (2 * dx + 2) * total)
        give[dx * total : (dx + 1) * total, :] = grad_proj[there, :].astype(F32)
    value, first = 0.0, 0
    for part in range(count):
        last = first + rows_t[part].shape[1]
        value = value + dot(rows_t[part][...], grad_proj[first:last, :], 1, 0)
        first = last
    product[...] = value
    row_block = product.shape[0] // (dp_count * NY)
    for piece, dy in zip(pieces, (0,) + FAR_FIRST):
        target = (y + dy) % NY
        for z in range(dp_count):
            start = pl.multiple_of((z * NY + target) * row_block, row_block)
            piece[z] = product[pl.ds(start, row_block), :]


def gradients(place, arrived, parts, scaling, users, dp_count):
    rows_t, proj, cots, keys, queries, intra = zip(*parts)
    features = rows_t[0].shape[0]
    rows = sum(part.shape[1] for part in rows_t)
    row_block = features // (dp_count * NY)
    count = len(parts)
    return pl.pallas_call(
        functools.partial(grad_kernel, scaling, users, dp_count, count),
        out_shape=(struct((rows, 3 * DH), BF16), struct((rows // 2, 3 * DH), F32))
        + (struct((dp_count, row_block, 3 * DH), F32),) * NY,
        in_specs=[SMEM] + [VMEM] * (NY - 1 + 6 * count),
        out_specs=(VMEM,) * (2 + NY),
        scratch_shapes=[
            pltpu.VMEM((GROUP, users, DH, DH), F32),
            pltpu.VMEM((GROUP, users, DH, DH), F32),
            pltpu.VMEM((GROUP, users, DH, DH), BF16),
            pltpu.VMEM((GROUP, users, DH, DH), BF16),
            pltpu.VMEM((features, 3 * DH), F32),
        ],
        compiler_params=pltpu.CompilerParams(vmem_limit_bytes=32 * MIB),
        cost_estimate=pl.CostEstimate(
            flops=2 * rows * features * 3 * DH, bytes_accessed=10 * MIB, transcendentals=0
        ),
        name="gradients",
    )(place, *arrived, *keys, *queries, *rows_t, *proj, *cots, *intra)


def input_kernel(place, *refs):
    x, c = place[1], place[2]
    own, theirs, back = refs[0], refs[1], refs[2 : 1 + NX]
    w, out, done, full = refs[1 + NX :]
    total = out.shape[0]

    @pl.when(pl.program_id(0) == 0)
    def _():
        for dx in range(NX):
            for dc in range(2):
                head = ((x + dx) % NX) * 2 + (c ^ dc)
                source = (theirs if dc else own) if dx == 0 else back[dx - 1]
                first = total if dx and dc else 0
                for part in range(3):
                    columns = slice(part * DH, (part + 1) * DH)
                    start = pl.multiple_of((part * H + head) * DH, DH)
                    full[:, pl.ds(start, DH)] = source[first : first + total, columns].astype(BF16)
        done[...] = jnp.zeros(done.shape, F32)

    out[...] = dot(full[...], w[...], 1, 1).astype(BF16)


def input_gradient(place, sources, total, w_qkv):
    features, width = w_qkv.shape
    step = 256
    return pl.pallas_call(
        input_kernel,
        grid=(features // step,),
        out_shape=(struct((total, features), BF16), struct((8, DH), F32)),
        in_specs=[SMEM]
        + [VMEM] * len(sources)
        + [pl.BlockSpec((step, width), lambda i: (i, 0))],
        out_specs=(
            pl.BlockSpec((total, step), lambda i: (0, i)),
            pl.BlockSpec((8, DH), lambda i: (0, 0)),
        ),
        scratch_shapes=[pltpu.VMEM((total, width), BF16)],
        compiler_params=pltpu.CompilerParams(vmem_limit_bytes=48 * MIB),
        cost_estimate=pl.CostEstimate(
            flops=16 * total * features * width, bytes_accessed=80 * MIB, transcendentals=0
        ),
        name="input_gradient",
    )(place, *sources, w_qkv)


def fold_kernel(count, *refs):
    out = refs[-1]
    for z in range(out.shape[0]):
        out[z] = sum(ref[z] for ref in refs[:count])


def fold(parts, after):
    return pl.pallas_call(
        functools.partial(fold_kernel, len(parts)),
        out_shape=struct(parts[0].shape, F32),
        in_specs=[VMEM] * len(parts) + [ANY],
        out_specs=VMEM,
        compiler_params=pltpu.CompilerParams(vmem_limit_bytes=8 * MIB),
        cost_estimate=pl.CostEstimate(flops=MIB, bytes_accessed=2 * MIB, transcendentals=0),
        name="fold",
    )(*parts, after)


def square_kernel(place, got, after, squares, own, theirs, rows_of):
    c = place[2]
    count, rows = got.shape[0], own.shape[0] // NX
    value = sum(got[z] for z in range(count))
    for to in range(GROUP):
        there = slice((to // 2) * rows, (to // 2 + 1) * rows)
        rows_of[to % 2, there, :] = value[to * rows : (to + 1) * rows, :]
    squares[...] = jnp.full(squares.shape, jnp.sum(jnp.sum(value * value, axis=0, keepdims=True)))
    own[...] = rows_of[c]
    theirs[...] = rows_of[1 - c]


def square_sum(place, got, after, copies):
    rows, width = got.shape[1] // 2, got.shape[2]
    return pl.pallas_call(
        square_kernel,
        out_shape=(struct((copies, DH), F32),) + (struct((rows, width), F32),) * 2,
        in_specs=[SMEM, VMEM, ANY],
        out_specs=(VMEM,) * 3,
        scratch_shapes=[pltpu.VMEM((2, rows, width), F32)],
        compiler_params=pltpu.CompilerParams(vmem_limit_bytes=8 * MIB),
        cost_estimate=pl.CostEstimate(flops=MIB, bytes_accessed=MIB, transcendentals=0),
        name="square_sum",
    )(place, got, after)


def total_square_kernel(squares, out):
    out[...] = jnp.broadcast_to(jnp.sum(squares[...], axis=0, keepdims=True), out.shape)


def total_square(squares, count):
    return pl.pallas_call(
        total_square_kernel,
        out_shape=struct((count, DH), F32),
        in_specs=[VMEM],
        out_specs=VMEM,
        compiler_params=pltpu.CompilerParams(vmem_limit_bytes=4 * MIB),
        cost_estimate=pl.CostEstimate(flops=4096, bytes_accessed=16384, transcendentals=0),
        name="total_square",
    )(squares)


def pair_kernel(place, own, theirs, *refs):
    x, pieces, rows_of = place[1], refs[:NX], refs[NX]
    rows = own.shape[0] // NX
    for to in range(NX):
        rows_of[to, :rows, :] = own[to * rows : (to + 1) * rows, :]
        rows_of[to, rows:, :] = theirs[to * rows : (to + 1) * rows, :]
    for dx in range(NX):
        pieces[dx][...] = rows_of[(x + dx) % NX]


def pair_rows(place, own, theirs):
    rows, width = 2 * own.shape[0] // NX, own.shape[1]
    return pl.pallas_call(
        pair_kernel,
        out_shape=(struct((rows, width), F32),) * NX,
        in_specs=[SMEM, VMEM, VMEM],
        out_specs=(VMEM,) * NX,
        scratch_shapes=[pltpu.VMEM((NX, rows, width), F32)],
        compiler_params=pltpu.CompilerParams(vmem_limit_bytes=8 * MIB),
        cost_estimate=pl.CostEstimate(flops=MIB, bytes_accessed=MIB, transcendentals=0),
        name="pair_rows",
    )(place, own, theirs)


def clip_kernel(place, squares, *refs):
    x, c, pieces, out = place[1], place[2], refs[:NX], refs[NX]
    rows = out.shape[0]
    total_sq = jnp.sum(squares[...], axis=0, keepdims=True)
    factor = jnp.minimum(1.0, D / jnp.sqrt(total_sq + 1e-06))
    for dx in range(NX):
        for core in range(2):
            head = ((x + NX - dx) % NX) * 2 + (c ^ core)
            for part in range(3):
                columns = slice(part * DH, (part + 1) * DH)
                start = pl.multiple_of((part * H + head) * DH, DH)
                value = pieces[dx][core * rows : (core + 1) * rows, columns]
                out[:, pl.ds(start, DH)] = value * factor


def clip(place, squares, pieces):
    rows, width = pieces[0].shape[0] // 2, pieces[0].shape[1] * H
    return pl.pallas_call(
        clip_kernel,
        out_shape=struct((rows, width), F32),
        in_specs=[SMEM] + [VMEM] * (1 + NX),
        out_specs=VMEM,
        compiler_params=pltpu.CompilerParams(vmem_limit_bytes=8 * MIB),
        cost_estimate=pl.CostEstimate(flops=MIB, bytes_accessed=MIB, transcendentals=0),
        name="clip",
    )(place, squares, *pieces)


def body(inputs, grad_out, w_qkv):
    user_count, row_count, feature_count = inputs.shape
    seqlen_total = row_count * lax.axis_size("seq")
    dp_count = lax.axis_size("dp")
    scaling = 1.0 / math.sqrt(DH * seqlen_total)
    index = lax.axis_index("seq")
    y, x, c = index // GROUP, (index // 2) % NX, index % 2
    place = jnp.stack([y, x, c])
    head = x * 2 + c
    total_rows = user_count * row_count

    to_right, to_left, to_other = messages(place, inputs, grad_out)
    left = send(to_right, dx=1)
    right = send(to_left, dx=-1)
    other = send(to_other, dc=1)
    w_head = jnp.concatenate(
        [head_columns(w_qkv, part * H + head) for part in range(3)], axis=1
    )
    own_units = ((0, None, 0, 0), (0, None, 0, 0), (2, 0, 16, 0), (2, 8, 17, 0))
    left_units = ((0, 0, 18, 2), (0, 10, 19, 2), (1, 0, 18, 2), (1, 10, 19, 2))
    right_units = ((0, 10, 18, 2), (0, 0, 19, 2), (1, 10, 18, 2), (1, 0, 19, 2))
    far_units = ((0, 0, 8, 1), (0, 10, 18, 1))
    own_part = blocks(place, w_head, (inputs, grad_out, other), own_units)

    far_low = send(left[:10], dx=1)
    far_high = send(right[:10], dx=-1)
    count = left.shape[0]
    crossing = relay(
        (left, right),
        (left.shape, right.shape),
        ((0, 0, 0, count, 0), (1, 1, 0, count, 0)),
        (own_part[3],),
    )
    left_other, right_other = (send(value, dc=1) for value in crossing)
    left_part = blocks(place, w_head, (left, left_other), left_units)
    right_part = blocks(place, w_head, (right, right_other), right_units)
    (far,) = relay(
        (far_low, far_high),
        ((20,) + left.shape[1:],),
        ((0, 0, 0, 10, 0), (0, 1, 0, 10, 10)),
        (own_part[3], left_part[3], right_part[3]),
    )
    far_other = send(far, dc=1)
    parts = [
        own_part,
        left_part,
        blocks(place, w_head, (far,), far_units),
        blocks(place, w_head, (far_other,), far_units),
        right_part,
    ]
    sent = totals(place, [part[3] for part in parts], [part[4] for part in parts])
    arrived = [send(value, dy=dy) for value, dy in zip(sent, FAR_FIRST)]
    grad_proj, give, *pieces = gradients(place, arrived, parts, scaling, user_count, dp_count)

    span = 2 * total_rows
    theirs = send(give, dc=1)
    returns = relay(
        (grad_proj, theirs),
        ((span, 3 * DH),) * (NX - 1),
        tuple((dx - 1, 0, dx * span, dx * span + total_rows, 0) for dx in range(1, NX))
        + tuple(
            (dx - 1, 1, dx * total_rows, (dx + 1) * total_rows, total_rows)
            for dx in range(1, NX)
        ),
    )
    back = [send(returns[dx - 1], dx=-dx) for dx in range(1, NX)]
    summands = pieces[:1] + [send(value, dy=dy) for value, dy in zip(pieces[1:], FAR_FIRST)]
    folded = fold(summands, returns[0])
    got = lax.all_to_all(folded, "dp", 0, 0)
    grad_rows, done = input_gradient(place, (grad_proj, theirs, *back), total_rows, w_qkv)
    grad_inputs = grad_rows.reshape(user_count, row_count, feature_count)

    squares, own, theirs = square_sum(place, got, done, dp_count)
    squares = lax.all_to_all(squares, "dp", 0, 0, tiled=True)
    parts = pair_rows(place, own, send(theirs, dc=1))
    squares = total_square(squares, lax.axis_size("seq"))
    squares = lax.all_to_all(squares, "seq", 0, 0, tiled=True)
    parts = parts[:1] + tuple(send(parts[dx], dx=dx) for dx in range(1, NX))
    return (grad_inputs, clip(place, squares, parts))


def solution(mesh):
    in_specs = (P("dp", "seq", None), P("dp", "seq", None), P())
    out_specs = (P("dp", "seq", None), P(("dp", "seq"), None))
    return jax.shard_map(body, mesh=mesh, in_specs=in_specs, out_specs=out_specs, check_vma=False)
```

```python
import functools
import math

import jax
import jax.numpy as jnp
from jax import lax
from jax.experimental import pallas as pl
from jax.experimental.pallas import tpu as pltpu
from jax.sharding import PartitionSpec as P

H = 8
DH = 128
D = 1024
NY = 4
NX = 4
GROUP = 2 * NX
FAR_FIRST = (2, 1, 3)
BF16 = jnp.bfloat16
F32 = jnp.float32
VMEM = pl.BlockSpec(memory_space=pltpu.VMEM)
SMEM = pl.BlockSpec(memory_space=pltpu.SMEM)
ANY = pl.BlockSpec(memory_space=pl.ANY)
MIB = 1 << 20


def seq_perm(dy, dx, dc):
    moves = []
    for y in range(NY):
        for x in range(NX):
            for c in range(2):
                source = (y * NX + x) * 2 + c
                target = (((y + dy) % NY) * NX + (x + dx) % NX) * 2 + (c ^ dc)
                moves.append((source, target))
    return moves


def send(value, dy=0, dx=0, dc=0):
    return lax.ppermute(value, "seq", seq_perm(dy, dx, dc))


def head_columns(array, head):
    return lax.dynamic_slice_in_dim(array, head * DH, DH, 1)


def struct(shape, dtype):
    return jax.ShapeDtypeStruct(shape, dtype)


def dot(a, b, over_a, over_b):
    return lax.dot_general(a, b, (((over_a,), (over_b,)), ((), ())), preferred_element_type=F32)


def message_kernel(place, inputs, grad_out, right, left, cross):
    x, c = place[1], place[2]

    def cot(user, dx, core):
        head = ((x + dx) % NX) * 2 + core
        return grad_out[user, :, pl.ds(pl.multiple_of(head * DH, DH), DH)].astype(F32)

    for user in range(2):
        passed, kept = (right, left) if user == 0 else (left, right)
        for j in range(H):
            value = inputs[user, :, j * DH : (j + 1) * DH].astype(F32)
            passed[j] = value
            kept[10 + j] = value
            cross[user * H + j] = value
        for core in range(2):
            passed[8 + core] = cot(user, 2, core)
            right[18 + 2 * core + user] = cot(user, 1, core)
            left[18 + 2 * core + user] = cot(user, NX - 1, core)
        cross[2 * H + user] = cot(user, 0, 1 - c)


def messages(place, inputs, grad_out):
    size = inputs.shape[1]
    return pl.pallas_call(
        message_kernel,
        out_shape=tuple(struct((count, size, DH), F32) for count in (22, 22, 18)),
        in_specs=[SMEM, VMEM, VMEM],
        out_specs=(VMEM,) * 3,
        compiler_params=pltpu.CompilerParams(vmem_limit_bytes=16 * MIB),
        cost_estimate=pl.CostEstimate(flops=MIB, bytes_accessed=3 * MIB, transcendentals=0),
        name="messages",
    )(place, inputs, grad_out)


def relay_kernel(cuts, *refs):
    sources, outs = refs
    for out, source, first, last, at in cuts:
        outs[out][at : at + last - first] = sources[source][first:last].astype(outs[out].dtype)


def relay(sources, shapes, cuts, after=()):
    def kernel(*refs):
        relay_kernel(cuts, refs[: len(sources)], refs[len(sources) + len(after) :])

    return pl.pallas_call(
        kernel,
        out_shape=tuple(struct(shape, F32) for shape in shapes),
        in_specs=[VMEM] * len(sources) + [ANY] * len(after),
        out_specs=(VMEM,) * len(shapes),
        compiler_params=pltpu.CompilerParams(vmem_limit_bytes=12 * MIB),
        cost_estimate=pl.CostEstimate(flops=MIB, bytes_accessed=2 * MIB, transcendentals=0),
        name="relay",
    )(*sources, *after)


def block_kernel(units, place, w, *refs):
    sources, refs = refs[:-7], refs[-7:]
    rows_t, proj, cot_half, key_state, query_state, intra, x_all = refs
    x, c = place[1], place[2]
    features, total = rows_t.shape
    size = total // len(units)
    causal = lax.broadcasted_iota(jnp.int32, (size, size), 0) >= lax.broadcasted_iota(
        jnp.int32, (size, size), 1
    )
    for n, (source, start, cot_start, cot_step) in enumerate(units):
        here = slice(n * size, (n + 1) * size)
        if start is None:
            x_all[here, :] = sources[source][n]
            columns = pl.ds(pl.multiple_of((x * 2 + c) * DH, DH), DH)
            cot_half[here, :] = sources[source + 1][n, :, columns]
        else:
            for j in range(features // DH):
                x_all[here, j * DH : (j + 1) * DH] = sources[source][start + j].astype(BF16)
            cot_half[here, :] = sources[source][cot_start + cot_step * c].astype(BF16)
    rows = x_all[...]
    proj[...] = dot(rows, w[...], 1, 0).astype(BF16)
    rows_t[...] = rows.T
    for n in range(len(units)):
        here = slice(n * size, (n + 1) * size)
        i, u = n // 2, n % 2
        q, k, v = (proj[here, part * DH : (part + 1) * DH] for part in range(3))
        g = cot_half[here, :]
        key_state[i, u] = dot(k, v, 0, 0)
        query_state[i, u] = dot(q, g, 0, 0)
        out_value = jnp.where(causal, dot(g, v, 1, 1), 0.0).astype(BF16)
        query_key = jnp.where(causal, dot(q, k, 1, 1), 0.0).astype(BF16)
        intra[here, :DH] = dot(out_value, k, 1, 0)
        intra[here, DH : 2 * DH] = dot(out_value, q, 0, 0)
        intra[here, 2 * DH :] = dot(query_key, g, 0, 0)


def blocks(place, w_head, sources, units):
    features = w_head.shape[0]
    size = sources[0].shape[1]
    total = len(units) * size
    return pl.pallas_call(
        functools.partial(block_kernel, units),
        out_shape=(
            struct((features, total), BF16),
            struct((total, 3 * DH), BF16),
            struct((total, DH), BF16),
            struct((len(units) // 2, 2, DH, DH), F32),
            struct((len(units) // 2, 2, DH, DH), F32),
            struct((total, 3 * DH), F32),
        ),
        in_specs=[SMEM] + [VMEM] * (1 + len(sources)),
        out_specs=(VMEM,) * 6,
        scratch_shapes=[pltpu.VMEM((total, features), BF16)],
        compiler_params=pltpu.CompilerParams(vmem_limit_bytes=24 * MIB),
        cost_estimate=pl.CostEstimate(
            flops=2 * total * features * 3 * DH, bytes_accessed=4 * MIB, transcendentals=0
        ),
        name="blocks",
    )(place, w_head, *sources)


def total_kernel(place, *refs):
    count = (len(refs) - NY + 1) // 2
    keys, queries, outs = refs[:count], refs[count : 2 * count], refs[2 * count :]
    key_total = sum(ref[i] for ref in keys for i in range(ref.shape[0]))
    query_total = sum(ref[i] for ref in queries for i in range(ref.shape[0]))
    for out, dy in zip(outs, FAR_FIRST):
        out[...] = jnp.where(place[0] + dy < NY, key_total, query_total)


def totals(place, key_states, query_states):
    shape = key_states[0].shape[1:]
    return pl.pallas_call(
        total_kernel,
        out_shape=(struct(shape, F32),) * (NY - 1),
        in_specs=[SMEM] + [VMEM] * (2 * len(key_states)),
        out_specs=(VMEM,) * (NY - 1),
        compiler_params=pltpu.CompilerParams(vmem_limit_bytes=16 * MIB),
        cost_estimate=pl.CostEstimate(flops=MIB, bytes_accessed=3 * MIB, transcendentals=0),
        name="totals",
    )(place, *key_states, *query_states)


def grad_kernel(scaling, users, dp_count, count, place, *refs):
    y, x, c = place[0], place[1], place[2]
    arrived, refs = refs[: NY - 1], refs[NY - 1 :]
    keys, refs = refs[:count], refs[count:]
    queries, refs = refs[:count], refs[count:]
    rows_t, refs = refs[:count], refs[count:]
    proj, refs = refs[:count], refs[count:]
    cots, refs = refs[:count], refs[count:]
    intra, refs = refs[:count], refs[count:]
    grad_proj, give, pieces, refs = refs[0], refs[1], refs[2 : 2 + NY], refs[2 + NY :]
    key_all, query_all, prior_all, later_all, product = refs
    first = 0
    for part in range(count):
        last = first + keys[part].shape[0]
        key_all[first:last] = keys[part][...]
        query_all[first:last] = queries[part][...]
        first = last
    prior = jnp.zeros(arrived[0].shape, F32)
    later = jnp.zeros(arrived[0].shape, F32)
    for ref, dy in zip(arrived, FAR_FIRST):
        value = ref[...]
        prior = prior + jnp.where(y >= dy, value, 0.0)
        later = later + jnp.where(y >= dy, 0.0, value)

    def slot(position):
        return ((x + NX - position // 2) % NX) * 2 + (c ^ (position % 2))

    for position in range(GROUP):
        here = slot(position)
        prior_all[here] = prior.astype(BF16)
        prior = prior + key_all[here]
    for position in reversed(range(GROUP)):
        here = slot(position)
        later_all[here] = later.astype(BF16)
        later = later + query_all[here]
    size = intra[0].shape[0] // (keys[0].shape[0] * users)
    block = 0
    for part in range(count):
        for i in range(keys[part].shape[0]):
            for u in range(users):
                here = slice((i * users + u) * size, (i * users + u + 1) * size)
                there = slice((block * users + u) * size, (block * users + u + 1) * size)
                k, v = proj[part][here, DH : 2 * DH], proj[part][here, 2 * DH :]
                prior_state, later_state = prior_all[block, u], later_all[block, u]
                inter = (
                    dot(cots[part][here, :], prior_state, 1, 1),
                    dot(v, later_state, 1, 1),
                    dot(k, later_state, 1, 0),
                )
                for kind in range(3):
                    columns = slice(kind * DH, (kind + 1) * DH)
                    grad_proj[there, columns] = (
                        scaling * (intra[part][here, columns] + inter[kind])
                    ).astype(BF16)
            block += 1
    total = users * size
    for dx in range(NX):
        there = slice((2 * dx + 1) * total, (2 * dx + 2) * total)
        give[dx * total : (dx + 1) * total, :] = grad_proj[there, :].astype(F32)
    value, first = 0.0, 0
    for part in range(count):
        last = first + rows_t[part].shape[1]
        value = value + dot(rows_t[part][...], grad_proj[first:last, :], 1, 0)
        first = last
    product[...] = value
    row_block = product.shape[0] // (dp_count * NY)
    for piece, dy in zip(pieces, (0,) + FAR_FIRST):
        target = (y + dy) % NY
        for z in range(dp_count):
            start = pl.multiple_of((z * NY + target) * row_block, row_block)
            piece[z] = product[pl.ds(start, row_block), :]


def gradients(place, arrived, parts, scaling, users, dp_count):
    rows_t, proj, cots, keys, queries, intra = zip(*parts)
    features = rows_t[0].shape[0]
    rows = sum(part.shape[1] for part in rows_t)
    row_block = features // (dp_count * NY)
    count = len(parts)
    return pl.pallas_call(
        functools.partial(grad_kernel, scaling, users, dp_count, count),
        out_shape=(struct((rows, 3 * DH), BF16), struct((rows // 2, 3 * DH), F32))
        + (struct((dp_count, row_block, 3 * DH), F32),) * NY,
        in_specs=[SMEM] + [VMEM] * (NY - 1 + 6 * count),
        out_specs=(VMEM,) * (2 + NY),
        scratch_shapes=[
            pltpu.VMEM((GROUP, users, DH, DH), F32),
            pltpu.VMEM((GROUP, users, DH, DH), F32),
            pltpu.VMEM((GROUP, users, DH, DH), BF16),
            pltpu.VMEM((GROUP, users, DH, DH), BF16),
            pltpu.VMEM((features, 3 * DH), F32),
        ],
        compiler_params=pltpu.CompilerParams(vmem_limit_bytes=32 * MIB),
        cost_estimate=pl.CostEstimate(
            flops=2 * rows * features * 3 * DH, bytes_accessed=10 * MIB, transcendentals=0
        ),
        name="gradients",
    )(place, *arrived, *keys, *queries, *rows_t, *proj, *cots, *intra)


def input_kernel(place, *refs):
    x, c = place[1], place[2]
    own, theirs, back = refs[0], refs[1], refs[2 : 1 + NX]
    w, out, done, full = refs[1 + NX :]
    total = out.shape[0]

    @pl.when(pl.program_id(0) == 0)
    def _():
        for dx in range(NX):
            for dc in range(2):
                head = ((x + dx) % NX) * 2 + (c ^ dc)
                source = (theirs if dc else own) if dx == 0 else back[dx - 1]
                first = total if dx and dc else 0
                for part in range(3):
                    columns = slice(part * DH, (part + 1) * DH)
                    start = pl.multiple_of((part * H + head) * DH, DH)
                    full[:, pl.ds(start, DH)] = source[first : first + total, columns].astype(BF16)
        done[...] = jnp.zeros(done.shape, F32)

    out[...] = dot(full[...], w[...], 1, 1).astype(BF16)


def input_gradient(place, sources, total, w_qkv):
    features, width = w_qkv.shape
    step = 256
    return pl.pallas_call(
        input_kernel,
        grid=(features // step,),
        out_shape=(struct((total, features), BF16), struct((8, DH), F32)),
        in_specs=[SMEM]
        + [VMEM] * len(sources)
        + [pl.BlockSpec((step, width), lambda i: (i, 0))],
        out_specs=(
            pl.BlockSpec((total, step), lambda i: (0, i)),
            pl.BlockSpec((8, DH), lambda i: (0, 0)),
        ),
        scratch_shapes=[pltpu.VMEM((total, width), BF16)],
        compiler_params=pltpu.CompilerParams(vmem_limit_bytes=48 * MIB),
        cost_estimate=pl.CostEstimate(
            flops=16 * total * features * width, bytes_accessed=80 * MIB, transcendentals=0
        ),
        name="input_gradient",
    )(place, *sources, w_qkv)


def fold_kernel(count, place, *refs):
    out = refs[-1]
    half = out.shape[0] // 2
    for z in range(out.shape[0]):
        to = jnp.where(place[2] == 0, z, (z + half) % out.shape[0])
        out[to] = sum(ref[z] for ref in refs[:count])


def fold(place, parts, after):
    return pl.pallas_call(
        functools.partial(fold_kernel, len(parts)),
        out_shape=struct(parts[0].shape, F32),
        in_specs=[SMEM] + [VMEM] * len(parts) + [ANY],
        out_specs=VMEM,
        compiler_params=pltpu.CompilerParams(vmem_limit_bytes=8 * MIB),
        cost_estimate=pl.CostEstimate(flops=MIB, bytes_accessed=2 * MIB, transcendentals=0),
        name="fold",
    )(place, *parts, after)


def square_kernel(place, got, after, squares, own, theirs, rows_of):
    c = place[2]
    count, rows = got.shape[0], own.shape[0] // NX
    value = sum(got[z] for z in range(count))
    for to in range(GROUP):
        there = slice((to // 2) * rows, (to // 2 + 1) * rows)
        rows_of[to % 2, there, :] = value[to * rows : (to + 1) * rows, :]
    squares[...] = jnp.full(squares.shape, jnp.sum(jnp.sum(value * value, axis=0, keepdims=True)))
    own[...] = rows_of[c]
    theirs[...] = rows_of[1 - c]


def square_sum(place, got, after, copies):
    rows, width = got.shape[1] // 2, got.shape[2]
    return pl.pallas_call(
        square_kernel,
        out_shape=(struct((copies, DH), F32),) + (struct((rows, width), F32),) * 2,
        in_specs=[SMEM, VMEM, ANY],
        out_specs=(VMEM,) * 3,
        scratch_shapes=[pltpu.VMEM((2, rows, width), F32)],
        compiler_params=pltpu.CompilerParams(vmem_limit_bytes=8 * MIB),
        cost_estimate=pl.CostEstimate(flops=MIB, bytes_accessed=MIB, transcendentals=0),
        name="square_sum",
    )(place, got, after)


def pair_kernel(place, own, theirs, *refs):
    x, pieces, rows_of = place[1], refs[:NX], refs[NX]
    rows = own.shape[0] // NX
    for to in range(NX):
        rows_of[to, :rows, :] = own[to * rows : (to + 1) * rows, :]
        rows_of[to, rows:, :] = theirs[to * rows : (to + 1) * rows, :]
    for dx in range(NX):
        pieces[dx][...] = rows_of[(x + dx) % NX]


def pair_rows(place, own, theirs):
    rows, width = 2 * own.shape[0] // NX, own.shape[1]
    return pl.pallas_call(
        pair_kernel,
        out_shape=(struct((rows, width), F32),) * NX,
        in_specs=[SMEM, VMEM, VMEM],
        out_specs=(VMEM,) * NX,
        scratch_shapes=[pltpu.VMEM((NX, rows, width), F32)],
        compiler_params=pltpu.CompilerParams(vmem_limit_bytes=8 * MIB),
        cost_estimate=pl.CostEstimate(flops=MIB, bytes_accessed=MIB, transcendentals=0),
        name="pair_rows",
    )(place, own, theirs)


def clip_kernel(place, squares, *refs):
    x, c, pieces, out = place[1], place[2], refs[:NX], refs[NX]
    rows = out.shape[0]
    total_sq = jnp.sum(squares[...], axis=0, keepdims=True)
    factor = jnp.minimum(1.0, D / jnp.sqrt(total_sq + 1e-06))
    for dx in range(NX):
        for core in range(2):
            head = ((x + NX - dx) % NX) * 2 + (c ^ core)
            for part in range(3):
                columns = slice(part * DH, (part + 1) * DH)
                start = pl.multiple_of((part * H + head) * DH, DH)
                value = pieces[dx][core * rows : (core + 1) * rows, columns]
                out[:, pl.ds(start, DH)] = value * factor


def clip(place, squares, pieces):
    rows, width = pieces[0].shape[0] // 2, pieces[0].shape[1] * H
    return pl.pallas_call(
        clip_kernel,
        out_shape=struct((rows, width), F32),
        in_specs=[SMEM] + [VMEM] * (1 + NX),
        out_specs=VMEM,
        compiler_params=pltpu.CompilerParams(vmem_limit_bytes=8 * MIB),
        cost_estimate=pl.CostEstimate(flops=MIB, bytes_accessed=MIB, transcendentals=0),
        name="clip",
    )(place, squares, *pieces)


def body(inputs, grad_out, w_qkv):
    user_count, row_count, feature_count = inputs.shape
    seqlen_total = row_count * lax.axis_size("seq")
    dp_count = lax.axis_size("dp")
    scaling = 1.0 / math.sqrt(DH * seqlen_total)
    index = lax.axis_index("seq")
    y, x, c = index // GROUP, (index // 2) % NX, index % 2
    place = jnp.stack([y, x, c])
    head = x * 2 + c
    total_rows = user_count * row_count

    to_right, to_left, to_other = messages(place, inputs, grad_out)
    left = send(to_right, dx=1)
    right = send(to_left, dx=-1)
    other = send(to_other, dc=1)
    w_head = jnp.concatenate(
        [head_columns(w_qkv, part * H + head) for part in range(3)], axis=1
    )
    own_units = ((0, None, 0, 0), (0, None, 0, 0), (2, 0, 16, 0), (2, 8, 17, 0))
    left_units = ((0, 0, 18, 2), (0, 10, 19, 2), (1, 0, 18, 2), (1, 10, 19, 2))
    right_units = ((0, 10, 18, 2), (0, 0, 19, 2), (1, 10, 18, 2), (1, 0, 19, 2))
    far_units = ((0, 0, 8, 1), (0, 10, 18, 1))
    own_part = blocks(place, w_head, (inputs, grad_out, other), own_units)

    far_low = send(left[:10], dx=1)
    far_high = send(right[:10], dx=-1)
    count = left.shape[0]
    crossing = relay(
        (left, right),
        (left.shape, right.shape),
        ((0, 0, 0, count, 0), (1, 1, 0, count, 0)),
        (own_part[3],),
    )
    left_other, right_other = (send(value, dc=1) for value in crossing)
    left_part = blocks(place, w_head, (left, left_other), left_units)
    right_part = blocks(place, w_head, (right, right_other), right_units)
    (far,) = relay(
        (far_low, far_high),
        ((20,) + left.shape[1:],),
        ((0, 0, 0, 10, 0), (0, 1, 0, 10, 10)),
        (own_part[3], left_part[3], right_part[3]),
    )
    far_other = send(far, dc=1)
    parts = [
        own_part,
        left_part,
        blocks(place, w_head, (far,), far_units),
        blocks(place, w_head, (far_other,), far_units),
        right_part,
    ]
    sent = totals(place, [part[3] for part in parts], [part[4] for part in parts])
    arrived = [send(value, dy=dy) for value, dy in zip(sent, FAR_FIRST)]
    grad_proj, give, *pieces = gradients(place, arrived, parts, scaling, user_count, dp_count)

    span = 2 * total_rows
    theirs = send(give, dc=1)
    returns = relay(
        (grad_proj, theirs),
        ((span, 3 * DH),) * (NX - 1),
        tuple((dx - 1, 0, dx * span, dx * span + total_rows, 0) for dx in range(1, NX))
        + tuple(
            (dx - 1, 1, dx * total_rows, (dx + 1) * total_rows, total_rows)
            for dx in range(1, NX)
        ),
    )
    back = [send(returns[dx - 1], dx=-dx) for dx in range(1, NX)]
    summands = pieces[:1] + [send(value, dy=dy) for value, dy in zip(pieces[1:], FAR_FIRST)]
    folded = fold(place, summands, returns[0])
    columns_of = []
    for column in range(NY * GROUP):
        turn = column % 2 * (dp_count // 2)
        order = [(z + turn) % dp_count for z in range(dp_count)]
        columns_of.append([z * NY * GROUP + column for z in order])
    got = lax.all_to_all(folded, ("dp", "seq"), 0, 0, axis_index_groups=columns_of)
    grad_rows, done = input_gradient(place, (grad_proj, theirs, *back), total_rows, w_qkv)
    grad_inputs = grad_rows.reshape(user_count, row_count, feature_count)

    squares, own, theirs = square_sum(place, got, done, dp_count * lax.axis_size("seq"))
    squares = lax.all_to_all(squares, ("dp", "seq"), 0, 0, tiled=True)
    parts = pair_rows(place, own, send(theirs, dc=1))
    parts = parts[:1] + tuple(send(parts[dx], dx=dx) for dx in range(1, NX))
    return (grad_inputs, clip(place, squares, parts))


def solution(mesh):
    in_specs = (P("dp", "seq", None), P("dp", "seq", None), P())
    out_specs = (P("dp", "seq", None), P(("dp", "seq"), None))
    return jax.shard_map(body, mesh=mesh, in_specs=in_specs, out_specs=out_specs, check_vma=False)
```

```python
import functools
import math

import jax
import jax.numpy as jnp
from jax import lax
from jax.experimental import pallas as pl
from jax.experimental.pallas import tpu as pltpu
from jax.sharding import PartitionSpec as P

H = 8
DH = 128
D = 1024
NY = 4
NX = 4
GROUP = 2 * NX
FAR_FIRST = (2, 1, 3)
BF16 = jnp.bfloat16
F32 = jnp.float32
VMEM = pl.BlockSpec(memory_space=pltpu.VMEM)
SMEM = pl.BlockSpec(memory_space=pltpu.SMEM)
ANY = pl.BlockSpec(memory_space=pl.ANY)
MIB = 1 << 20


def seq_perm(dy, dx, dc):
    moves = []
    for y in range(NY):
        for x in range(NX):
            for c in range(2):
                source = (y * NX + x) * 2 + c
                target = (((y + dy) % NY) * NX + (x + dx) % NX) * 2 + (c ^ dc)
                moves.append((source, target))
    return moves


def send(value, dy=0, dx=0, dc=0):
    return lax.ppermute(value, "seq", seq_perm(dy, dx, dc))


def head_columns(array, head):
    return lax.dynamic_slice_in_dim(array, head * DH, DH, 1)


def struct(shape, dtype):
    return jax.ShapeDtypeStruct(shape, dtype)


def dot(a, b, over_a, over_b):
    return lax.dot_general(a, b, (((over_a,), (over_b,)), ((), ())), preferred_element_type=F32)


def message_kernel(place, inputs, grad_out, right, left, cross):
    x, c = place[1], place[2]

    def cot(user, dx, core):
        head = ((x + dx) % NX) * 2 + core
        return grad_out[user, :, pl.ds(pl.multiple_of(head * DH, DH), DH)].astype(F32)

    for user in range(2):
        passed, kept = (right, left) if user == 0 else (left, right)
        for j in range(H):
            value = inputs[user, :, j * DH : (j + 1) * DH].astype(F32)
            passed[j] = value
            kept[10 + j] = value
            cross[user * H + j] = value
        for core in range(2):
            passed[8 + core] = cot(user, 2, core)
            right[18 + 2 * core + user] = cot(user, 1, core)
            left[18 + 2 * core + user] = cot(user, NX - 1, core)
        cross[2 * H + user] = cot(user, 0, 1 - c)


def messages(place, inputs, grad_out):
    size = inputs.shape[1]
    return pl.pallas_call(
        message_kernel,
        out_shape=tuple(struct((count, size, DH), F32) for count in (22, 22, 18)),
        in_specs=[SMEM, VMEM, VMEM],
        out_specs=(VMEM,) * 3,
        compiler_params=pltpu.CompilerParams(vmem_limit_bytes=16 * MIB),
        cost_estimate=pl.CostEstimate(flops=MIB, bytes_accessed=3 * MIB, transcendentals=0),
        name="messages",
    )(place, inputs, grad_out)


def relay_kernel(cuts, *refs):
    sources, outs = refs
    for out, source, first, last, at in cuts:
        outs[out][at : at + last - first] = sources[source][first:last].astype(outs[out].dtype)


def relay(sources, shapes, cuts, after=()):
    def kernel(*refs):
        relay_kernel(cuts, refs[: len(sources)], refs[len(sources) + len(after) :])

    return pl.pallas_call(
        kernel,
        out_shape=tuple(struct(shape, F32) for shape in shapes),
        in_specs=[VMEM] * len(sources) + [ANY] * len(after),
        out_specs=(VMEM,) * len(shapes),
        compiler_params=pltpu.CompilerParams(vmem_limit_bytes=12 * MIB),
        cost_estimate=pl.CostEstimate(flops=MIB, bytes_accessed=2 * MIB, transcendentals=0),
        name="relay",
    )(*sources, *after)


def block_kernel(units, place, w, *refs):
    sources, refs = refs[:-7], refs[-7:]
    rows_t, proj, cot_half, key_state, query_state, intra, x_all = refs
    x, c = place[1], place[2]
    features, total = rows_t.shape
    size = total // len(units)
    causal = lax.broadcasted_iota(jnp.int32, (size, size), 0) >= lax.broadcasted_iota(
        jnp.int32, (size, size), 1
    )
    for n, (source, start, cot_start, cot_step) in enumerate(units):
        here = slice(n * size, (n + 1) * size)
        if start is None:
            x_all[here, :] = sources[source][n]
            columns = pl.ds(pl.multiple_of((x * 2 + c) * DH, DH), DH)
            cot_half[here, :] = sources[source + 1][n, :, columns]
        else:
            for j in range(features // DH):
                x_all[here, j * DH : (j + 1) * DH] = sources[source][start + j].astype(BF16)
            cot_half[here, :] = sources[source][cot_start + cot_step * c].astype(BF16)
    rows = x_all[...]
    proj[...] = dot(rows, w[...], 1, 0).astype(BF16)
    rows_t[...] = rows.T
    for n in range(len(units)):
        here = slice(n * size, (n + 1) * size)
        i, u = n // 2, n % 2
        q, k, v = (proj[here, part * DH : (part + 1) * DH] for part in range(3))
        g = cot_half[here, :]
        key_state[i, u] = dot(k, v, 0, 0)
        query_state[i, u] = dot(q, g, 0, 0)
        out_value = jnp.where(causal, dot(g, v, 1, 1), 0.0).astype(BF16)
        query_key = jnp.where(causal, dot(q, k, 1, 1), 0.0).astype(BF16)
        intra[here, :DH] = dot(out_value, k, 1, 0)
        intra[here, DH : 2 * DH] = dot(out_value, q, 0, 0)
        intra[here, 2 * DH :] = dot(query_key, g, 0, 0)


def blocks(place, w_head, sources, units):
    features = w_head.shape[0]
    size = sources[0].shape[1]
    total = len(units) * size
    return pl.pallas_call(
        functools.partial(block_kernel, units),
        out_shape=(
            struct((features, total), BF16),
            struct((total, 3 * DH), BF16),
            struct((total, DH), BF16),
            struct((len(units) // 2, 2, DH, DH), F32),
            struct((len(units) // 2, 2, DH, DH), F32),
            struct((total, 3 * DH), F32),
        ),
        in_specs=[SMEM] + [VMEM] * (1 + len(sources)),
        out_specs=(VMEM,) * 6,
        scratch_shapes=[pltpu.VMEM((total, features), BF16)],
        compiler_params=pltpu.CompilerParams(vmem_limit_bytes=24 * MIB),
        cost_estimate=pl.CostEstimate(
            flops=2 * total * features * 3 * DH, bytes_accessed=4 * MIB, transcendentals=0
        ),
        name="blocks",
    )(place, w_head, *sources)


def total_kernel(place, *refs):
    count = (len(refs) - NY + 1) // 2
    keys, queries, outs = refs[:count], refs[count : 2 * count], refs[2 * count :]
    key_total = sum(ref[i] for ref in keys for i in range(ref.shape[0]))
    query_total = sum(ref[i] for ref in queries for i in range(ref.shape[0]))
    for out, dy in zip(outs, FAR_FIRST):
        out[...] = jnp.where(place[0] + dy < NY, key_total, query_total)


def totals(place, key_states, query_states):
    shape = key_states[0].shape[1:]
    return pl.pallas_call(
        total_kernel,
        out_shape=(struct(shape, F32),) * (NY - 1),
        in_specs=[SMEM] + [VMEM] * (2 * len(key_states)),
        out_specs=(VMEM,) * (NY - 1),
        compiler_params=pltpu.CompilerParams(vmem_limit_bytes=16 * MIB),
        cost_estimate=pl.CostEstimate(flops=MIB, bytes_accessed=3 * MIB, transcendentals=0),
        name="totals",
    )(place, *key_states, *query_states)


def grad_kernel(scaling, users, dp_count, count, place, *refs):
    y, x, c = place[0], place[1], place[2]
    arrived, refs = refs[: NY - 1], refs[NY - 1 :]
    keys, refs = refs[:count], refs[count:]
    queries, refs = refs[:count], refs[count:]
    rows_t, refs = refs[:count], refs[count:]
    proj, refs = refs[:count], refs[count:]
    cots, refs = refs[:count], refs[count:]
    intra, refs = refs[:count], refs[count:]
    grad_proj, give, pieces, refs = refs[0], refs[1], refs[2 : 2 + NY], refs[2 + NY :]
    key_all, query_all, prior_all, later_all, product = refs
    first = 0
    for part in range(count):
        last = first + keys[part].shape[0]
        key_all[first:last] = keys[part][...]
        query_all[first:last] = queries[part][...]
        first = last
    prior = jnp.zeros(arrived[0].shape, F32)
    later = jnp.zeros(arrived[0].shape, F32)
    for ref, dy in zip(arrived, FAR_FIRST):
        value = ref[...]
        prior = prior + jnp.where(y >= dy, value, 0.0)
        later = later + jnp.where(y >= dy, 0.0, value)

    def slot(position):
        return ((x + NX - position // 2) % NX) * 2 + (c ^ (position % 2))

    for position in range(GROUP):
        here = slot(position)
        prior_all[here] = prior.astype(BF16)
        prior = prior + key_all[here]
    for position in reversed(range(GROUP)):
        here = slot(position)
        later_all[here] = later.astype(BF16)
        later = later + query_all[here]
    size = intra[0].shape[0] // (keys[0].shape[0] * users)
    block = 0
    for part in range(count):
        for i in range(keys[part].shape[0]):
            for u in range(users):
                here = slice((i * users + u) * size, (i * users + u + 1) * size)
                there = slice((block * users + u) * size, (block * users + u + 1) * size)
                k, v = proj[part][here, DH : 2 * DH], proj[part][here, 2 * DH :]
                prior_state, later_state = prior_all[block, u], later_all[block, u]
                inter = (
                    dot(cots[part][here, :], prior_state, 1, 1),
                    dot(v, later_state, 1, 1),
                    dot(k, later_state, 1, 0),
                )
                for kind in range(3):
                    columns = slice(kind * DH, (kind + 1) * DH)
                    grad_proj[there, columns] = (
                        scaling * (intra[part][here, columns] + inter[kind])
                    ).astype(BF16)
            block += 1
    total = users * size
    for dx in range(NX):
        there = slice((2 * dx + 1) * total, (2 * dx + 2) * total)
        give[dx * total : (dx + 1) * total, :] = grad_proj[there, :].astype(F32)
    value, first = 0.0, 0
    for part in range(count):
        last = first + rows_t[part].shape[1]
        value = value + dot(rows_t[part][...], grad_proj[first:last, :], 1, 0)
        first = last
    product[...] = value
    row_block = product.shape[0] // (dp_count * NY)
    for piece, dy in zip(pieces, (0,) + FAR_FIRST):
        target = (y + dy) % NY
        for z in range(dp_count):
            start = pl.multiple_of((z * NY + target) * row_block, row_block)
            piece[z] = product[pl.ds(start, row_block), :]


def gradients(place, arrived, parts, scaling, users, dp_count):
    rows_t, proj, cots, keys, queries, intra = zip(*parts)
    features = rows_t[0].shape[0]
    rows = sum(part.shape[1] for part in rows_t)
    row_block = features // (dp_count * NY)
    count = len(parts)
    return pl.pallas_call(
        functools.partial(grad_kernel, scaling, users, dp_count, count),
        out_shape=(struct((rows, 3 * DH), BF16), struct((rows // 2, 3 * DH), F32))
        + (struct((dp_count, row_block, 3 * DH), F32),) * NY,
        in_specs=[SMEM] + [VMEM] * (NY - 1 + 6 * count),
        out_specs=(VMEM,) * (2 + NY),
        scratch_shapes=[
            pltpu.VMEM((GROUP, users, DH, DH), F32),
            pltpu.VMEM((GROUP, users, DH, DH), F32),
            pltpu.VMEM((GROUP, users, DH, DH), BF16),
            pltpu.VMEM((GROUP, users, DH, DH), BF16),
            pltpu.VMEM((features, 3 * DH), F32),
        ],
        compiler_params=pltpu.CompilerParams(vmem_limit_bytes=32 * MIB),
        cost_estimate=pl.CostEstimate(
            flops=2 * rows * features * 3 * DH, bytes_accessed=10 * MIB, transcendentals=0
        ),
        name="gradients",
    )(place, *arrived, *keys, *queries, *rows_t, *proj, *cots, *intra)


def input_kernel(place, *refs):
    x, c = place[1], place[2]
    own, theirs, back = refs[0], refs[1], refs[2 : 1 + NX]
    w, out, done, full = refs[1 + NX :]
    total = out.shape[0]

    @pl.when(pl.program_id(0) == 0)
    def _():
        for dx in range(NX):
            for dc in range(2):
                head = ((x + dx) % NX) * 2 + (c ^ dc)
                source = (theirs if dc else own) if dx == 0 else back[dx - 1]
                first = total if dx and dc else 0
                for part in range(3):
                    columns = slice(part * DH, (part + 1) * DH)
                    start = pl.multiple_of((part * H + head) * DH, DH)
                    full[:, pl.ds(start, DH)] = source[first : first + total, columns].astype(BF16)
        done[...] = jnp.zeros(done.shape, F32)

    out[...] = dot(full[...], w[...], 1, 1).astype(BF16)


def input_gradient(place, sources, total, w_qkv):
    features, width = w_qkv.shape
    step = 256
    return pl.pallas_call(
        input_kernel,
        grid=(features // step,),
        out_shape=(struct((total, features), BF16), struct((8, DH), F32)),
        in_specs=[SMEM]
        + [VMEM] * len(sources)
        + [pl.BlockSpec((step, width), lambda i: (i, 0))],
        out_specs=(
            pl.BlockSpec((total, step), lambda i: (0, i)),
            pl.BlockSpec((8, DH), lambda i: (0, 0)),
        ),
        scratch_shapes=[pltpu.VMEM((total, width), BF16)],
        compiler_params=pltpu.CompilerParams(vmem_limit_bytes=48 * MIB),
        cost_estimate=pl.CostEstimate(
            flops=16 * total * features * width, bytes_accessed=80 * MIB, transcendentals=0
        ),
        name="input_gradient",
    )(place, *sources, w_qkv)


def fold_kernel(count, place, *refs):
    out = refs[-1]
    half = out.shape[0] // 2
    for z in range(out.shape[0]):
        to = jnp.where(place[2] == 0, z, (z + half) % out.shape[0])
        out[to] = sum(ref[z] for ref in refs[:count])


def fold(place, parts, after):
    return pl.pallas_call(
        functools.partial(fold_kernel, len(parts)),
        out_shape=struct(parts[0].shape, F32),
        in_specs=[SMEM] + [VMEM] * len(parts) + [ANY],
        out_specs=VMEM,
        compiler_params=pltpu.CompilerParams(vmem_limit_bytes=8 * MIB),
        cost_estimate=pl.CostEstimate(flops=MIB, bytes_accessed=2 * MIB, transcendentals=0),
        name="fold",
    )(place, *parts, after)


def square_kernel(place, got, after, *refs):
    x, pieces, rows_of = place[1], refs[:NX], refs[NX]
    rows, width = rows_of.shape[1], rows_of.shape[2]
    value = sum(got[z] for z in range(got.shape[0]))
    square = jnp.sum(jnp.sum(value * value, axis=0, keepdims=True))
    for to in range(NX):
        rows_of[to] = value[to * rows : (to + 1) * rows, :]
    for dx in range(NX):
        pieces[dx][:rows, :] = rows_of[(x + dx) % NX]
        pieces[dx][rows:, :] = jnp.full((rows, width), square)


def square_sum(place, got, after):
    rows, width = got.shape[1] // NX, got.shape[2]
    return pl.pallas_call(
        square_kernel,
        out_shape=(struct((2 * rows, width), F32),) * NX,
        in_specs=[SMEM, VMEM, ANY],
        out_specs=(VMEM,) * NX,
        scratch_shapes=[pltpu.VMEM((NX, rows, width), F32)],
        compiler_params=pltpu.CompilerParams(vmem_limit_bytes=8 * MIB),
        cost_estimate=pl.CostEstimate(flops=MIB, bytes_accessed=MIB, transcendentals=0),
        name="square_sum",
    )(place, got, after)


def core_kernel(place, *refs):
    c, pieces = place[2], refs[:NX]
    squares, mine, theirs, rows_of = refs[NX:]
    rows = mine.shape[0] // NX
    for dx in range(NX):
        for core in range(2):
            there = slice(dx * rows, (dx + 1) * rows)
            rows_of[core, there, :] = pieces[dx][core * rows : (core + 1) * rows, :]
    mine[...] = rows_of[c]
    theirs[...] = rows_of[1 - c]
    square = sum(piece[2 * rows : 2 * rows + 1, :DH] for piece in pieces)
    squares[...] = jnp.broadcast_to(square, squares.shape)


def by_core(place, pieces, copies):
    rows, width = NX * pieces[0].shape[0] // 4, pieces[0].shape[1]
    return pl.pallas_call(
        core_kernel,
        out_shape=(struct((copies, DH), F32),) + (struct((rows, width), F32),) * 2,
        in_specs=[SMEM] + [VMEM] * NX,
        out_specs=(VMEM,) * 3,
        scratch_shapes=[pltpu.VMEM((2, rows, width), F32)],
        compiler_params=pltpu.CompilerParams(vmem_limit_bytes=8 * MIB),
        cost_estimate=pl.CostEstimate(flops=MIB, bytes_accessed=MIB, transcendentals=0),
        name="by_core",
    )(place, *pieces)


def clip_kernel(place, squares, mine, theirs, out):
    x, c = place[1], place[2]
    rows = out.shape[0]
    total_sq = jnp.sum(squares[...], axis=0, keepdims=True)
    factor = jnp.minimum(1.0, D / jnp.sqrt(total_sq + 1e-06))
    for dx in range(NX):
        for core, source in enumerate((mine, theirs)):
            head = ((x + NX - dx) % NX) * 2 + (c ^ core)
            for part in range(3):
                columns = slice(part * DH, (part + 1) * DH)
                start = pl.multiple_of((part * H + head) * DH, DH)
                value = source[dx * rows : (dx + 1) * rows, columns]
                out[:, pl.ds(start, DH)] = value * factor


def clip(place, squares, mine, theirs):
    rows, width = mine.shape[0] // NX, mine.shape[1] * H
    return pl.pallas_call(
        clip_kernel,
        out_shape=struct((rows, width), F32),
        in_specs=[SMEM] + [VMEM] * 3,
        out_specs=VMEM,
        compiler_params=pltpu.CompilerParams(vmem_limit_bytes=8 * MIB),
        cost_estimate=pl.CostEstimate(flops=MIB, bytes_accessed=MIB, transcendentals=0),
        name="clip",
    )(place, squares, mine, theirs)


def body(inputs, grad_out, w_qkv):
    user_count, row_count, feature_count = inputs.shape
    seqlen_total = row_count * lax.axis_size("seq")
    dp_count = lax.axis_size("dp")
    scaling = 1.0 / math.sqrt(DH * seqlen_total)
    index = lax.axis_index("seq")
    y, x, c = index // GROUP, (index // 2) % NX, index % 2
    place = jnp.stack([y, x, c])
    head = x * 2 + c
    total_rows = user_count * row_count

    to_right, to_left, to_other = messages(place, inputs, grad_out)
    left = send(to_right, dx=1)
    right = send(to_left, dx=-1)
    other = send(to_other, dc=1)
    w_head = jnp.concatenate(
        [head_columns(w_qkv, part * H + head) for part in range(3)], axis=1
    )
    own_units = ((0, None, 0, 0), (0, None, 0, 0), (2, 0, 16, 0), (2, 8, 17, 0))
    left_units = ((0, 0, 18, 2), (0, 10, 19, 2), (1, 0, 18, 2), (1, 10, 19, 2))
    right_units = ((0, 10, 18, 2), (0, 0, 19, 2), (1, 10, 18, 2), (1, 0, 19, 2))
    far_units = ((0, 0, 8, 1), (0, 10, 18, 1))
    own_part = blocks(place, w_head, (inputs, grad_out, other), own_units)

    far_low = send(left[:10], dx=1)
    far_high = send(right[:10], dx=-1)
    count = left.shape[0]
    crossing = relay(
        (left, right),
        (left.shape, right.shape),
        ((0, 0, 0, count, 0), (1, 1, 0, count, 0)),
        (own_part[3],),
    )
    left_other, right_other = (send(value, dc=1) for value in crossing)
    left_part = blocks(place, w_head, (left, left_other), left_units)
    right_part = blocks(place, w_head, (right, right_other), right_units)
    (far,) = relay(
        (far_low, far_high),
        ((20,) + left.shape[1:],),
        ((0, 0, 0, 10, 0), (0, 1, 0, 10, 10)),
        (own_part[3], left_part[3], right_part[3]),
    )
    far_other = send(far, dc=1)
    parts = [
        own_part,
        left_part,
        blocks(place, w_head, (far,), far_units),
        blocks(place, w_head, (far_other,), far_units),
        right_part,
    ]
    sent = totals(place, [part[3] for part in parts], [part[4] for part in parts])
    arrived = [send(value, dy=dy) for value, dy in zip(sent, FAR_FIRST)]
    grad_proj, give, *pieces = gradients(place, arrived, parts, scaling, user_count, dp_count)

    span = 2 * total_rows
    theirs = send(give, dc=1)
    returns = relay(
        (grad_proj, theirs),
        ((span, 3 * DH),) * (NX - 1),
        tuple((dx - 1, 0, dx * span, dx * span + total_rows, 0) for dx in range(1, NX))
        + tuple(
            (dx - 1, 1, dx * total_rows, (dx + 1) * total_rows, total_rows)
            for dx in range(1, NX)
        ),
    )
    back = [send(returns[dx - 1], dx=-dx) for dx in range(1, NX)]
    summands = pieces[:1] + [send(value, dy=dy) for value, dy in zip(pieces[1:], FAR_FIRST)]
    folded = fold(place, summands, returns[0])
    columns_of = []
    for column in range(NY * GROUP):
        turn = column % 2 * (dp_count // 2)
        order = [(z + turn) % dp_count for z in range(dp_count)]
        columns_of.append([z * NY * GROUP + column for z in order])
    got = lax.all_to_all(folded, ("dp", "seq"), 0, 0, axis_index_groups=columns_of)
    grad_rows, done = input_gradient(place, (grad_proj, theirs, *back), total_rows, w_qkv)
    grad_inputs = grad_rows.reshape(user_count, row_count, feature_count)

    parts = square_sum(place, got, done)
    arrived_rows = {dx: send(parts[dx], dx=dx) for dx in FAR_FIRST}
    pieces = [parts[0]] + [arrived_rows[dx] for dx in range(1, NX)]
    squares, mine, theirs = by_core(place, pieces, 2 * dp_count * NY)
    slabs = [
        [
            (z * NY + y_of) * GROUP + 2 * x_of + core
            for z in range(dp_count)
            for y_of in range(NY)
            for core in range(2)
        ]
        for x_of in range(NX)
    ]
    squares = lax.all_to_all(
        squares, ("dp", "seq"), 0, 0, axis_index_groups=slabs, tiled=True
    )
    return (grad_inputs, clip(place, squares, mine, send(theirs, dc=1)))


def solution(mesh):
    in_specs = (P("dp", "seq", None), P("dp", "seq", None), P())
    out_specs = (P("dp", "seq", None), P(("dp", "seq"), None))
    return jax.shard_map(body, mesh=mesh, in_specs=in_specs, out_specs=out_specs, check_vma=False)
```

```python
import functools
import math

import jax
import jax.numpy as jnp
from jax import lax
from jax.experimental import pallas as pl
from jax.experimental.pallas import tpu as pltpu
from jax.sharding import PartitionSpec as P

H = 8
DH = 128
D = 1024
NY = 4
NX = 4
GROUP = 2 * NX
FAR_FIRST = (2, 1, 3)
BF16 = jnp.bfloat16
F32 = jnp.float32
VMEM = pl.BlockSpec(memory_space=pltpu.VMEM)
SMEM = pl.BlockSpec(memory_space=pltpu.SMEM)
ANY = pl.BlockSpec(memory_space=pl.ANY)
MIB = 1 << 20


def seq_perm(dy, dx, dc):
    moves = []
    for y in range(NY):
        for x in range(NX):
            for c in range(2):
                source = (y * NX + x) * 2 + c
                target = (((y + dy) % NY) * NX + (x + dx) % NX) * 2 + (c ^ dc)
                moves.append((source, target))
    return moves


def send(value, dy=0, dx=0, dc=0):
    return lax.ppermute(value, "seq", seq_perm(dy, dx, dc))


def head_columns(array, head):
    return lax.dynamic_slice_in_dim(array, head * DH, DH, 1)


def struct(shape, dtype):
    return jax.ShapeDtypeStruct(shape, dtype)


def dot(a, b, over_a, over_b):
    return lax.dot_general(a, b, (((over_a,), (over_b,)), ((), ())), preferred_element_type=F32)


def message_kernel(place, inputs, grad_out, right, left, cross):
    x, c = place[1], place[2]

    def cot(user, dx, core):
        head = ((x + dx) % NX) * 2 + core
        return grad_out[user, :, pl.ds(pl.multiple_of(head * DH, DH), DH)].astype(F32)

    for user in range(2):
        passed, kept = (right, left) if user == 0 else (left, right)
        for j in range(H):
            value = inputs[user, :, j * DH : (j + 1) * DH].astype(F32)
            passed[j] = value
            kept[10 + j] = value
            cross[user * H + j] = value
        for core in range(2):
            passed[8 + core] = cot(user, 2, core)
            right[18 + 2 * core + user] = cot(user, 1, core)
            left[18 + 2 * core + user] = cot(user, NX - 1, core)
        cross[2 * H + user] = cot(user, 0, 1 - c)


def messages(place, inputs, grad_out):
    size = inputs.shape[1]
    return pl.pallas_call(
        message_kernel,
        out_shape=tuple(struct((count, size, DH), F32) for count in (22, 22, 18)),
        in_specs=[SMEM, VMEM, VMEM],
        out_specs=(VMEM,) * 3,
        compiler_params=pltpu.CompilerParams(vmem_limit_bytes=16 * MIB),
        cost_estimate=pl.CostEstimate(flops=MIB, bytes_accessed=3 * MIB, transcendentals=0),
        name="messages",
    )(place, inputs, grad_out)


def relay_kernel(cuts, *refs):
    sources, outs = refs
    for out, source, first, last, at in cuts:
        outs[out][at : at + last - first] = sources[source][first:last].astype(outs[out].dtype)


def relay(sources, shapes, cuts, after=()):
    def kernel(*refs):
        relay_kernel(cuts, refs[: len(sources)], refs[len(sources) + len(after) :])

    return pl.pallas_call(
        kernel,
        out_shape=tuple(struct(shape, F32) for shape in shapes),
        in_specs=[VMEM] * len(sources) + [ANY] * len(after),
        out_specs=(VMEM,) * len(shapes),
        compiler_params=pltpu.CompilerParams(vmem_limit_bytes=12 * MIB),
        cost_estimate=pl.CostEstimate(flops=MIB, bytes_accessed=2 * MIB, transcendentals=0),
        name="relay",
    )(*sources, *after)


def block_kernel(units, place, w, *refs):
    sources, refs = refs[:-7], refs[-7:]
    rows_t, proj, cot_half, key_state, query_state, intra, x_all = refs
    x, c = place[1], place[2]
    features, total = rows_t.shape
    size = total // len(units)
    causal = lax.broadcasted_iota(jnp.int32, (size, size), 0) >= lax.broadcasted_iota(
        jnp.int32, (size, size), 1
    )
    for n, (source, start, cot_start, cot_step) in enumerate(units):
        here = slice(n * size, (n + 1) * size)
        if start is None:
            x_all[here, :] = sources[source][n]
            columns = pl.ds(pl.multiple_of((x * 2 + c) * DH, DH), DH)
            cot_half[here, :] = sources[source + 1][n, :, columns]
        else:
            for j in range(features // DH):
                x_all[here, j * DH : (j + 1) * DH] = sources[source][start + j].astype(BF16)
            cot_half[here, :] = sources[source][cot_start + cot_step * c].astype(BF16)
    rows = x_all[...]
    proj[...] = dot(rows, w[...], 1, 0).astype(BF16)
    rows_t[...] = rows.T
    for n in range(len(units)):
        here = slice(n * size, (n + 1) * size)
        i, u = n // 2, n % 2
        q, k, v = (proj[here, part * DH : (part + 1) * DH] for part in range(3))
        g = cot_half[here, :]
        key_state[i, u] = dot(k, v, 0, 0)
        query_state[i, u] = dot(q, g, 0, 0)
        out_value = jnp.where(causal, dot(g, v, 1, 1), 0.0).astype(BF16)
        query_key = jnp.where(causal, dot(q, k, 1, 1), 0.0).astype(BF16)
        intra[here, :DH] = dot(out_value, k, 1, 0)
        intra[here, DH : 2 * DH] = dot(out_value, q, 0, 0)
        intra[here, 2 * DH :] = dot(query_key, g, 0, 0)


def blocks(place, w_head, sources, units):
    features = w_head.shape[0]
    size = sources[0].shape[1]
    total = len(units) * size
    return pl.pallas_call(
        functools.partial(block_kernel, units),
        out_shape=(
            struct((features, total), BF16),
            struct((total, 3 * DH), BF16),
            struct((total, DH), BF16),
            struct((len(units) // 2, 2, DH, DH), F32),
            struct((len(units) // 2, 2, DH, DH), F32),
            struct((total, 3 * DH), F32),
        ),
        in_specs=[SMEM] + [VMEM] * (1 + len(sources)),
        out_specs=(VMEM,) * 6,
        scratch_shapes=[pltpu.VMEM((total, features), BF16)],
        compiler_params=pltpu.CompilerParams(vmem_limit_bytes=24 * MIB),
        cost_estimate=pl.CostEstimate(
            flops=2 * total * features * 3 * DH, bytes_accessed=4 * MIB, transcendentals=0
        ),
        name="blocks",
    )(place, w_head, *sources)


def total_kernel(place, *refs):
    count = (len(refs) - NY + 1) // 2
    keys, queries, outs = refs[:count], refs[count : 2 * count], refs[2 * count :]
    key_total = sum(ref[i] for ref in keys for i in range(ref.shape[0]))
    query_total = sum(ref[i] for ref in queries for i in range(ref.shape[0]))
    for out, dy in zip(outs, FAR_FIRST):
        out[...] = jnp.where(place[0] + dy < NY, key_total, query_total)


def totals(place, key_states, query_states):
    shape = key_states[0].shape[1:]
    return pl.pallas_call(
        total_kernel,
        out_shape=(struct(shape, F32),) * (NY - 1),
        in_specs=[SMEM] + [VMEM] * (2 * len(key_states)),
        out_specs=(VMEM,) * (NY - 1),
        compiler_params=pltpu.CompilerParams(vmem_limit_bytes=16 * MIB),
        cost_estimate=pl.CostEstimate(flops=MIB, bytes_accessed=3 * MIB, transcendentals=0),
        name="totals",
    )(place, *key_states, *query_states)


def grad_kernel(scaling, users, dp_count, count, place, *refs):
    y, x, c = place[0], place[1], place[2]
    arrived, refs = refs[: NY - 1], refs[NY - 1 :]
    keys, refs = refs[:count], refs[count:]
    queries, refs = refs[:count], refs[count:]
    rows_t, refs = refs[:count], refs[count:]
    proj, refs = refs[:count], refs[count:]
    cots, refs = refs[:count], refs[count:]
    intra, refs = refs[:count], refs[count:]
    grad_proj, give, piece, key_all, query_all, prior_all, later_all, picked = refs
    first = 0
    for part in range(count):
        last = first + keys[part].shape[0]
        key_all[first:last] = keys[part][...]
        query_all[first:last] = queries[part][...]
        first = last
    prior = jnp.zeros(arrived[0].shape, F32)
    later = jnp.zeros(arrived[0].shape, F32)
    for ref, dy in zip(arrived, FAR_FIRST):
        value = ref[...]
        prior = prior + jnp.where(y >= dy, value, 0.0)
        later = later + jnp.where(y >= dy, 0.0, value)

    def slot(position):
        return ((x + NX - position // 2) % NX) * 2 + (c ^ (position % 2))

    for position in range(GROUP):
        here = slot(position)
        prior_all[here] = prior.astype(BF16)
        prior = prior + key_all[here]
    for position in reversed(range(GROUP)):
        here = slot(position)
        later_all[here] = later.astype(BF16)
        later = later + query_all[here]
    size = intra[0].shape[0] // (keys[0].shape[0] * users)
    block = 0
    for part in range(count):
        for i in range(keys[part].shape[0]):
            for u in range(users):
                here = slice((i * users + u) * size, (i * users + u + 1) * size)
                there = slice((block * users + u) * size, (block * users + u + 1) * size)
                k, v = proj[part][here, DH : 2 * DH], proj[part][here, 2 * DH :]
                prior_state, later_state = prior_all[block, u], later_all[block, u]
                inter = (
                    dot(cots[part][here, :], prior_state, 1, 1),
                    dot(v, later_state, 1, 1),
                    dot(k, later_state, 1, 0),
                )
                for kind in range(3):
                    columns = slice(kind * DH, (kind + 1) * DH)
                    grad_proj[there, columns] = (
                        scaling * (intra[part][here, columns] + inter[kind])
                    ).astype(BF16)
            block += 1
    total = users * size
    for dx in range(NX):
        there = slice((2 * dx + 1) * total, (2 * dx + 2) * total)
        give[dx * total : (dx + 1) * total, :] = grad_proj[there, :].astype(F32)
    rows_for(y, FAR_FIRST[0], rows_t, grad_proj, picked, piece)


def rows_for(y, dy, rows_t, grad_proj, picked, piece):
    dp_count, row_block = piece.shape[0], piece.shape[1]
    target = (y + dy) % NY
    first = 0
    for part in rows_t:
        last = first + part.shape[1]
        for z in range(dp_count):
            start = pl.multiple_of((z * NY + target) * row_block, row_block)
            picked[z * row_block : (z + 1) * row_block, first:last] = part[
                pl.ds(start, row_block), :
            ]
        first = last
    value = dot(picked[...], grad_proj[...], 1, 0)
    for z in range(dp_count):
        piece[z] = value[z * row_block : (z + 1) * row_block, :]


def rest_kernel(place, *refs):
    rows_t, grad_proj, refs = refs[: -1 - NY], refs[-1 - NY], refs[-NY:]
    for piece, dy in zip(refs, FAR_FIRST[1:] + (0,)):
        rows_for(place[0], dy, rows_t, grad_proj, refs[-1], piece)


def rest_of_rows(place, rows_t, grad_proj, shape):
    tokens = grad_proj.shape[0]
    return pl.pallas_call(
        rest_kernel,
        out_shape=(struct(shape, F32),) * (NY - 1),
        in_specs=[SMEM] + [VMEM] * (len(rows_t) + 1),
        out_specs=(VMEM,) * (NY - 1),
        scratch_shapes=[pltpu.VMEM((shape[0] * shape[1], tokens), BF16)],
        compiler_params=pltpu.CompilerParams(vmem_limit_bytes=24 * MIB),
        cost_estimate=pl.CostEstimate(flops=MIB, bytes_accessed=4 * MIB, transcendentals=0),
        name="rest_of_rows",
    )(place, *rows_t, grad_proj)


def gradients(place, arrived, parts, scaling, users, dp_count):
    rows_t, proj, cots, keys, queries, intra = zip(*parts)
    features = rows_t[0].shape[0]
    rows = sum(part.shape[1] for part in rows_t)
    row_block = features // (dp_count * NY)
    count = len(parts)
    return pl.pallas_call(
        functools.partial(grad_kernel, scaling, users, dp_count, count),
        out_shape=(struct((rows, 3 * DH), BF16), struct((rows // 2, 3 * DH), F32))
        + (struct((dp_count, row_block, 3 * DH), F32),),
        in_specs=[SMEM] + [VMEM] * (NY - 1 + 6 * count),
        out_specs=(VMEM,) * 3,
        scratch_shapes=[
            pltpu.VMEM((GROUP, users, DH, DH), F32),
            pltpu.VMEM((GROUP, users, DH, DH), F32),
            pltpu.VMEM((GROUP, users, DH, DH), BF16),
            pltpu.VMEM((GROUP, users, DH, DH), BF16),
            pltpu.VMEM((dp_count * row_block, rows), BF16),
        ],
        compiler_params=pltpu.CompilerParams(vmem_limit_bytes=32 * MIB),
        cost_estimate=pl.CostEstimate(
            flops=2 * rows * features * 3 * DH, bytes_accessed=10 * MIB, transcendentals=0
        ),
        name="gradients",
    )(place, *arrived, *keys, *queries, *rows_t, *proj, *cots, *intra)


def input_kernel(place, *refs):
    x, c = place[1], place[2]
    own, theirs, back = refs[0], refs[1], refs[2 : 1 + NX]
    w, out, done, full = refs[1 + NX :]
    total = out.shape[0]

    @pl.when(pl.program_id(0) == 0)
    def _():
        for dx in range(NX):
            for dc in range(2):
                head = ((x + dx) % NX) * 2 + (c ^ dc)
                source = (theirs if dc else own) if dx == 0 else back[dx - 1]
                first = total if dx and dc else 0
                for part in range(3):
                    columns = slice(part * DH, (part + 1) * DH)
                    start = pl.multiple_of((part * H + head) * DH, DH)
                    full[:, pl.ds(start, DH)] = source[first : first + total, columns].astype(BF16)
        done[...] = jnp.zeros(done.shape, F32)

    out[...] = dot(full[...], w[...], 1, 1).astype(BF16)


def input_gradient(place, sources, total, w_qkv):
    features, width = w_qkv.shape
    step = 256
    return pl.pallas_call(
        input_kernel,
        grid=(features // step,),
        out_shape=(struct((total, features), BF16), struct((8, DH), F32)),
        in_specs=[SMEM]
        + [VMEM] * len(sources)
        + [pl.BlockSpec((step, width), lambda i: (i, 0))],
        out_specs=(
            pl.BlockSpec((total, step), lambda i: (0, i)),
            pl.BlockSpec((8, DH), lambda i: (0, 0)),
        ),
        scratch_shapes=[pltpu.VMEM((total, width), BF16)],
        compiler_params=pltpu.CompilerParams(vmem_limit_bytes=48 * MIB),
        cost_estimate=pl.CostEstimate(
            flops=16 * total * features * width, bytes_accessed=80 * MIB, transcendentals=0
        ),
        name="input_gradient",
    )(place, *sources, w_qkv)


def fold_kernel(count, place, *refs):
    out = refs[-1]
    dp_count = out.shape[0]
    for core in range(2):

        @pl.when(place[2] == core)
        def _():
            for z in range(dp_count):
                to = (z + core * (dp_count // 2)) % dp_count
                out[to] = sum(ref[z] for ref in refs[:count])


def fold(place, parts, after):
    return pl.pallas_call(
        functools.partial(fold_kernel, len(parts)),
        out_shape=struct(parts[0].shape, F32),
        in_specs=[SMEM] + [VMEM] * len(parts) + [ANY],
        out_specs=VMEM,
        compiler_params=pltpu.CompilerParams(vmem_limit_bytes=8 * MIB),
        cost_estimate=pl.CostEstimate(flops=MIB, bytes_accessed=2 * MIB, transcendentals=0),
        name="fold",
    )(place, *parts, after)


def square_kernel(place, got, after, squares, *refs):
    x, pieces, rows_of = place[1], refs[:NX], refs[NX]
    rows = rows_of.shape[1]
    value = sum(got[z] for z in range(got.shape[0]))
    squares[...] = jnp.full(squares.shape, jnp.sum(jnp.sum(value * value, axis=0, keepdims=True)))
    for to in range(NX):
        rows_of[to] = value[to * rows : (to + 1) * rows, :]
    for dx in range(NX):
        pieces[dx][...] = rows_of[(x + dx) % NX]


def square_sum(place, got, after, copies):
    rows, width = got.shape[1] // NX, got.shape[2]
    return pl.pallas_call(
        square_kernel,
        out_shape=(struct((copies, DH), F32),) + (struct((rows, width), F32),) * NX,
        in_specs=[SMEM, VMEM, ANY],
        out_specs=(VMEM,) * (1 + NX),
        scratch_shapes=[pltpu.VMEM((NX, rows, width), F32)],
        compiler_params=pltpu.CompilerParams(vmem_limit_bytes=8 * MIB),
        cost_estimate=pl.CostEstimate(flops=MIB, bytes_accessed=MIB, transcendentals=0),
        name="square_sum",
    )(place, got, after)


def core_kernel(place, *refs):
    c, pieces = place[2], refs[:NX]
    mine, theirs, rows_of = refs[NX:]
    rows = mine.shape[0] // NX
    for dx in range(NX):
        for core in range(2):
            there = slice(dx * rows, (dx + 1) * rows)
            rows_of[core, there, :] = pieces[dx][core * rows : (core + 1) * rows, :]
    mine[...] = rows_of[c]
    theirs[...] = rows_of[1 - c]


def by_core(place, pieces):
    rows, width = NX * pieces[0].shape[0] // 2, pieces[0].shape[1]
    return pl.pallas_call(
        core_kernel,
        out_shape=(struct((rows, width), F32),) * 2,
        in_specs=[SMEM] + [VMEM] * NX,
        out_specs=(VMEM,) * 2,
        scratch_shapes=[pltpu.VMEM((2, rows, width), F32)],
        compiler_params=pltpu.CompilerParams(vmem_limit_bytes=8 * MIB),
        cost_estimate=pl.CostEstimate(flops=MIB, bytes_accessed=MIB, transcendentals=0),
        name="by_core",
    )(place, *pieces)


def clip_kernel(place, squares, mine, theirs, out):
    x, c = place[1], place[2]
    rows = out.shape[0]
    total_sq = jnp.sum(squares[...], axis=0, keepdims=True)
    factor = jnp.minimum(1.0, D / jnp.sqrt(total_sq + 1e-06))
    for dx in range(NX):
        for core, source in enumerate((mine, theirs)):
            head = ((x + NX - dx) % NX) * 2 + (c ^ core)
            for part in range(3):
                columns = slice(part * DH, (part + 1) * DH)
                start = pl.multiple_of((part * H + head) * DH, DH)
                value = source[dx * rows : (dx + 1) * rows, columns]
                out[:, pl.ds(start, DH)] = value * factor


def clip(place, squares, mine, theirs):
    rows, width = mine.shape[0] // NX, mine.shape[1] * H
    return pl.pallas_call(
        clip_kernel,
        out_shape=struct((rows, width), F32),
        in_specs=[SMEM] + [VMEM] * 3,
        out_specs=VMEM,
        compiler_params=pltpu.CompilerParams(vmem_limit_bytes=8 * MIB),
        cost_estimate=pl.CostEstimate(flops=MIB, bytes_accessed=MIB, transcendentals=0),
        name="clip",
    )(place, squares, mine, theirs)


def body(inputs, grad_out, w_qkv):
    user_count, row_count, feature_count = inputs.shape
    seqlen_total = row_count * lax.axis_size("seq")
    dp_count = lax.axis_size("dp")
    scaling = 1.0 / math.sqrt(DH * seqlen_total)
    index = lax.axis_index("seq")
    y, x, c = index // GROUP, (index // 2) % NX, index % 2
    place = jnp.stack([y, x, c])
    head = x * 2 + c
    total_rows = user_count * row_count

    to_right, to_left, to_other = messages(place, inputs, grad_out)
    left = send(to_right, dx=1)
    right = send(to_left, dx=-1)
    other = send(to_other, dc=1)
    w_head = jnp.concatenate(
        [head_columns(w_qkv, part * H + head) for part in range(3)], axis=1
    )
    own_units = ((0, None, 0, 0), (0, None, 0, 0), (2, 0, 16, 0), (2, 8, 17, 0))
    left_units = ((0, 0, 18, 2), (0, 10, 19, 2), (1, 0, 18, 2), (1, 10, 19, 2))
    right_units = ((0, 10, 18, 2), (0, 0, 19, 2), (1, 10, 18, 2), (1, 0, 19, 2))
    far_units = ((0, 0, 8, 1), (0, 10, 18, 1))
    own_part = blocks(place, w_head, (inputs, grad_out, other), own_units)

    far_low = send(left[:10], dx=1)
    far_high = send(right[:10], dx=-1)
    count = left.shape[0]
    crossing = relay(
        (left, right),
        (left.shape, right.shape),
        ((0, 0, 0, count, 0), (1, 1, 0, count, 0)),
        (own_part[3],),
    )
    left_other, right_other = (send(value, dc=1) for value in crossing)
    left_part = blocks(place, w_head, (left, left_other), left_units)
    right_part = blocks(place, w_head, (right, right_other), right_units)
    (far,) = relay(
        (far_low, far_high),
        ((20,) + left.shape[1:],),
        ((0, 0, 0, 10, 0), (0, 1, 0, 10, 10)),
        (own_part[3], left_part[3], right_part[3]),
    )
    far_other = send(far, dc=1)
    parts = [
        own_part,
        left_part,
        blocks(place, w_head, (far,), far_units),
        blocks(place, w_head, (far_other,), far_units),
        right_part,
    ]
    sent = totals(place, [part[3] for part in parts], [part[4] for part in parts])
    arrived = [send(value, dy=dy) for value, dy in zip(sent, FAR_FIRST)]
    grad_proj, give, far_piece = gradients(
        place, arrived, parts, scaling, user_count, dp_count
    )

    span = 2 * total_rows
    theirs = send(give, dc=1)
    returns = relay(
        (grad_proj, theirs),
        ((span, 3 * DH),) * (NX - 1),
        tuple((dx - 1, 0, dx * span, dx * span + total_rows, 0) for dx in range(1, NX))
        + tuple(
            (dx - 1, 1, dx * total_rows, (dx + 1) * total_rows, total_rows)
            for dx in range(1, NX)
        ),
    )
    back = [send(returns[dx - 1], dx=-dx) for dx in range(1, NX)]
    *near, kept = rest_of_rows(place, [part[0] for part in parts], grad_proj, far_piece.shape)
    summands = [send(value, dy=dy) for value, dy in zip([far_piece] + near, FAR_FIRST)]
    summands.append(kept)
    folded = fold(place, summands, returns[0])
    columns_of = []
    for column in range(NY * GROUP):
        turn = column % 2 * (dp_count // 2)
        order = [(z + turn) % dp_count for z in range(dp_count)]
        columns_of.append([z * NY * GROUP + column for z in order])
    got = lax.all_to_all(folded, ("dp", "seq"), 0, 0, axis_index_groups=columns_of)
    grad_rows, done = input_gradient(place, (grad_proj, theirs, *back), total_rows, w_qkv)
    grad_inputs = grad_rows.reshape(user_count, row_count, feature_count)

    squares, *parts = square_sum(place, got, done, dp_count * lax.axis_size("seq"))
    squares = lax.all_to_all(squares, ("dp", "seq"), 0, 0, tiled=True)
    arrived_rows = {dx: send(parts[dx], dx=dx) for dx in FAR_FIRST}
    mine, theirs = by_core(place, [parts[0]] + [arrived_rows[dx] for dx in range(1, NX)])
    return (grad_inputs, clip(place, squares, mine, send(theirs, dc=1)))


def solution(mesh):
    in_specs = (P("dp", "seq", None), P("dp", "seq", None), P())
    out_specs = (P("dp", "seq", None), P(("dp", "seq"), None))
    return jax.shard_map(body, mesh=mesh, in_specs=in_specs, out_specs=out_specs, check_vma=False)
```

```python
import functools
import math

import jax
import jax.numpy as jnp
from jax import lax
from jax.experimental import pallas as pl
from jax.experimental.pallas import tpu as pltpu
from jax.sharding import PartitionSpec as P

H = 8
DH = 128
D = 1024
NY = 4
NX = 4
GROUP = 2 * NX
FAR_FIRST = (2, 1, 3)
BF16 = jnp.bfloat16
F32 = jnp.float32
VMEM = pl.BlockSpec(memory_space=pltpu.VMEM)
SMEM = pl.BlockSpec(memory_space=pltpu.SMEM)
ANY = pl.BlockSpec(memory_space=pl.ANY)
MIB = 1 << 20


def seq_perm(dy, dx, dc):
    moves = []
    for y in range(NY):
        for x in range(NX):
            for c in range(2):
                source = (y * NX + x) * 2 + c
                target = (((y + dy) % NY) * NX + (x + dx) % NX) * 2 + (c ^ dc)
                moves.append((source, target))
    return moves


def send(value, dy=0, dx=0, dc=0):
    return lax.ppermute(value, "seq", seq_perm(dy, dx, dc))


def head_columns(array, head):
    return lax.dynamic_slice_in_dim(array, head * DH, DH, 1)


def struct(shape, dtype):
    return jax.ShapeDtypeStruct(shape, dtype)


def dot(a, b, over_a, over_b):
    return lax.dot_general(a, b, (((over_a,), (over_b,)), ((), ())), preferred_element_type=F32)


def message_kernel(place, inputs, grad_out, right, left, cross):
    x, c = place[1], place[2]

    def cot(user, dx, core):
        head = ((x + dx) % NX) * 2 + core
        return grad_out[user, :, pl.ds(pl.multiple_of(head * DH, DH), DH)].astype(F32)

    for user in range(2):
        passed, kept = (right, left) if user == 0 else (left, right)
        for j in range(H):
            value = inputs[user, :, j * DH : (j + 1) * DH].astype(F32)
            passed[j] = value
            kept[10 + j] = value
            cross[user * H + j] = value
        for core in range(2):
            passed[8 + core] = cot(user, 2, core)
            right[18 + 2 * core + user] = cot(user, 1, core)
            left[18 + 2 * core + user] = cot(user, NX - 1, core)
        cross[2 * H + user] = cot(user, 0, 1 - c)


def messages(place, inputs, grad_out):
    size = inputs.shape[1]
    return pl.pallas_call(
        message_kernel,
        out_shape=tuple(struct((count, size, DH), F32) for count in (22, 22, 18)),
        in_specs=[SMEM, VMEM, VMEM],
        out_specs=(VMEM,) * 3,
        compiler_params=pltpu.CompilerParams(vmem_limit_bytes=16 * MIB),
        cost_estimate=pl.CostEstimate(flops=MIB, bytes_accessed=3 * MIB, transcendentals=0),
        name="messages",
    )(place, inputs, grad_out)


def relay_kernel(cuts, *refs):
    sources, outs = refs
    for out, source, first, last, at in cuts:
        outs[out][at : at + last - first] = sources[source][first:last].astype(outs[out].dtype)


def relay(sources, shapes, cuts, after=()):
    def kernel(*refs):
        relay_kernel(cuts, refs[: len(sources)], refs[len(sources) + len(after) :])

    return pl.pallas_call(
        kernel,
        out_shape=tuple(struct(shape, F32) for shape in shapes),
        in_specs=[VMEM] * len(sources) + [ANY] * len(after),
        out_specs=(VMEM,) * len(shapes),
        compiler_params=pltpu.CompilerParams(vmem_limit_bytes=12 * MIB),
        cost_estimate=pl.CostEstimate(flops=MIB, bytes_accessed=2 * MIB, transcendentals=0),
        name="relay",
    )(*sources, *after)


def block_kernel(units, place, w, *refs):
    sources, refs = refs[:-7], refs[-7:]
    rows_t, proj, cot_half, key_state, query_state, intra, x_all = refs
    x, c = place[1], place[2]
    features, total = rows_t.shape
    size = total // len(units)
    causal = lax.broadcasted_iota(jnp.int32, (size, size), 0) >= lax.broadcasted_iota(
        jnp.int32, (size, size), 1
    )
    for n, (source, start, cot_start, cot_step) in enumerate(units):
        here = slice(n * size, (n + 1) * size)
        if start is None:
            x_all[here, :] = sources[source][n]
            columns = pl.ds(pl.multiple_of((x * 2 + c) * DH, DH), DH)
            cot_half[here, :] = sources[source + 1][n, :, columns]
        else:
            for j in range(features // DH):
                x_all[here, j * DH : (j + 1) * DH] = sources[source][start + j].astype(BF16)
            cot_half[here, :] = sources[source][cot_start + cot_step * c].astype(BF16)
    rows = x_all[...]
    proj[...] = dot(rows, w[...], 1, 0).astype(BF16)
    rows_t[...] = rows.T
    for n in range(len(units)):
        here = slice(n * size, (n + 1) * size)
        i, u = n // 2, n % 2
        q, k, v = (proj[here, part * DH : (part + 1) * DH] for part in range(3))
        g = cot_half[here, :]
        key_state[i, u] = dot(k, v, 0, 0)
        query_state[i, u] = dot(q, g, 0, 0)
        out_value = jnp.where(causal, dot(g, v, 1, 1), 0.0).astype(BF16)
        query_key = jnp.where(causal, dot(q, k, 1, 1), 0.0).astype(BF16)
        intra[here, :DH] = dot(out_value, k, 1, 0)
        intra[here, DH : 2 * DH] = dot(out_value, q, 0, 0)
        intra[here, 2 * DH :] = dot(query_key, g, 0, 0)


def blocks(place, w_head, sources, units):
    features = w_head.shape[0]
    size = sources[0].shape[1]
    total = len(units) * size
    return pl.pallas_call(
        functools.partial(block_kernel, units),
        out_shape=(
            struct((features, total), BF16),
            struct((total, 3 * DH), BF16),
            struct((total, DH), BF16),
            struct((len(units) // 2, 2, DH, DH), F32),
            struct((len(units) // 2, 2, DH, DH), F32),
            struct((total, 3 * DH), F32),
        ),
        in_specs=[SMEM] + [VMEM] * (1 + len(sources)),
        out_specs=(VMEM,) * 6,
        scratch_shapes=[pltpu.VMEM((total, features), BF16)],
        compiler_params=pltpu.CompilerParams(vmem_limit_bytes=24 * MIB),
        cost_estimate=pl.CostEstimate(
            flops=2 * total * features * 3 * DH, bytes_accessed=4 * MIB, transcendentals=0
        ),
        name="blocks",
    )(place, w_head, *sources)


def total_kernel(place, *refs):
    count = (len(refs) - NY + 1) // 2
    keys, queries, outs = refs[:count], refs[count : 2 * count], refs[2 * count :]
    key_total = sum(ref[i] for ref in keys for i in range(ref.shape[0]))
    query_total = sum(ref[i] for ref in queries for i in range(ref.shape[0]))
    for out, dy in zip(outs, FAR_FIRST):
        out[...] = jnp.where(place[0] + dy < NY, key_total, query_total)


def totals(place, key_states, query_states):
    shape = key_states[0].shape[1:]
    return pl.pallas_call(
        total_kernel,
        out_shape=(struct(shape, F32),) * (NY - 1),
        in_specs=[SMEM] + [VMEM] * (2 * len(key_states)),
        out_specs=(VMEM,) * (NY - 1),
        compiler_params=pltpu.CompilerParams(vmem_limit_bytes=16 * MIB),
        cost_estimate=pl.CostEstimate(flops=MIB, bytes_accessed=3 * MIB, transcendentals=0),
        name="totals",
    )(place, *key_states, *query_states)


def grad_kernel(scaling, users, dp_count, count, place, *refs):
    y, x, c = place[0], place[1], place[2]
    arrived, refs = refs[: NY - 1], refs[NY - 1 :]
    keys, refs = refs[:count], refs[count:]
    queries, refs = refs[:count], refs[count:]
    rows_t, refs = refs[:count], refs[count:]
    proj, refs = refs[:count], refs[count:]
    cots, refs = refs[:count], refs[count:]
    intra, refs = refs[:count], refs[count:]
    grad_proj, give, piece, key_all, query_all, prior_all, later_all, picked = refs
    first = 0
    for part in range(count):
        last = first + keys[part].shape[0]
        key_all[first:last] = keys[part][...]
        query_all[first:last] = queries[part][...]
        first = last
    prior = jnp.zeros(arrived[0].shape, F32)
    later = jnp.zeros(arrived[0].shape, F32)
    for ref, dy in zip(arrived, FAR_FIRST):
        value = ref[...]
        prior = prior + jnp.where(y >= dy, value, 0.0)
        later = later + jnp.where(y >= dy, 0.0, value)

    def slot(position):
        return ((x + NX - position // 2) % NX) * 2 + (c ^ (position % 2))

    for position in range(GROUP):
        here = slot(position)
        prior_all[here] = prior.astype(BF16)
        prior = prior + key_all[here]
    for position in reversed(range(GROUP)):
        here = slot(position)
        later_all[here] = later.astype(BF16)
        later = later + query_all[here]
    size = intra[0].shape[0] // (keys[0].shape[0] * users)
    block = 0
    for part in range(count):
        for i in range(keys[part].shape[0]):
            for u in range(users):
                here = slice((i * users + u) * size, (i * users + u + 1) * size)
                there = slice((block * users + u) * size, (block * users + u + 1) * size)
                k, v = proj[part][here, DH : 2 * DH], proj[part][here, 2 * DH :]
                prior_state, later_state = prior_all[block, u], later_all[block, u]
                inter = (
                    dot(cots[part][here, :], prior_state, 1, 1),
                    dot(v, later_state, 1, 1),
                    dot(k, later_state, 1, 0),
                )
                for kind in range(3):
                    columns = slice(kind * DH, (kind + 1) * DH)
                    grad_proj[there, columns] = (
                        scaling * (intra[part][here, columns] + inter[kind])
                    ).astype(BF16)
            block += 1
    total = users * size
    for dx in range(NX):
        there = slice((2 * dx + 1) * total, (2 * dx + 2) * total)
        give[dx * total : (dx + 1) * total, :] = grad_proj[there, :].astype(F32)
    rows_for(y, FAR_FIRST[0], rows_t, grad_proj, picked, piece)


def rows_for(y, dy, rows_t, grad_proj, picked, piece):
    dp_count, row_block = piece.shape[0], piece.shape[1]
    target = (y + dy) % NY
    first = 0
    for part in rows_t:
        last = first + part.shape[1]
        for z in range(dp_count):
            start = pl.multiple_of((z * NY + target) * row_block, row_block)
            picked[z * row_block : (z + 1) * row_block, first:last] = part[
                pl.ds(start, row_block), :
            ]
        first = last
    value = dot(picked[...], grad_proj[...], 1, 0)
    for z in range(dp_count):
        piece[z] = value[z * row_block : (z + 1) * row_block, :]


def rest_kernel(place, *refs):
    rows_t, grad_proj, refs = refs[: -1 - NY], refs[-1 - NY], refs[-NY:]
    for piece, dy in zip(refs, FAR_FIRST[1:] + (0,)):
        rows_for(place[0], dy, rows_t, grad_proj, refs[-1], piece)


def rest_of_rows(place, rows_t, grad_proj, shape):
    tokens = grad_proj.shape[0]
    return pl.pallas_call(
        rest_kernel,
        out_shape=(struct(shape, F32),) * (NY - 1),
        in_specs=[SMEM] + [VMEM] * (len(rows_t) + 1),
        out_specs=(VMEM,) * (NY - 1),
        scratch_shapes=[pltpu.VMEM((shape[0] * shape[1], tokens), BF16)],
        compiler_params=pltpu.CompilerParams(vmem_limit_bytes=24 * MIB),
        cost_estimate=pl.CostEstimate(flops=MIB, bytes_accessed=4 * MIB, transcendentals=0),
        name="rest_of_rows",
    )(place, *rows_t, grad_proj)


def gradients(place, arrived, parts, scaling, users, dp_count):
    rows_t, proj, cots, keys, queries, intra = zip(*parts)
    features = rows_t[0].shape[0]
    rows = sum(part.shape[1] for part in rows_t)
    row_block = features // (dp_count * NY)
    count = len(parts)
    return pl.pallas_call(
        functools.partial(grad_kernel, scaling, users, dp_count, count),
        out_shape=(struct((rows, 3 * DH), BF16), struct((rows // 2, 3 * DH), F32))
        + (struct((dp_count, row_block, 3 * DH), F32),),
        in_specs=[SMEM] + [VMEM] * (NY - 1 + 6 * count),
        out_specs=(VMEM,) * 3,
        scratch_shapes=[
            pltpu.VMEM((GROUP, users, DH, DH), F32),
            pltpu.VMEM((GROUP, users, DH, DH), F32),
            pltpu.VMEM((GROUP, users, DH, DH), BF16),
            pltpu.VMEM((GROUP, users, DH, DH), BF16),
            pltpu.VMEM((dp_count * row_block, rows), BF16),
        ],
        compiler_params=pltpu.CompilerParams(vmem_limit_bytes=32 * MIB),
        cost_estimate=pl.CostEstimate(
            flops=2 * rows * features * 3 * DH, bytes_accessed=10 * MIB, transcendentals=0
        ),
        name="gradients",
    )(place, *arrived, *keys, *queries, *rows_t, *proj, *cots, *intra)


def input_kernel(place, *refs):
    x, c = place[1], place[2]
    own, theirs, back = refs[0], refs[1], refs[2 : 1 + NX]
    w, out, done, full = refs[1 + NX :]
    total = out.shape[0]

    @pl.when(pl.program_id(0) == 0)
    def _():
        for dx in range(NX):
            for dc in range(2):
                head = ((x + dx) % NX) * 2 + (c ^ dc)
                source = (theirs if dc else own) if dx == 0 else back[dx - 1]
                first = total if dx and dc else 0
                for part in range(3):
                    columns = slice(part * DH, (part + 1) * DH)
                    start = pl.multiple_of((part * H + head) * DH, DH)
                    full[:, pl.ds(start, DH)] = source[first : first + total, columns].astype(BF16)
        done[...] = jnp.zeros(done.shape, F32)

    out[...] = dot(full[...], w[...], 1, 1).astype(BF16)


def input_gradient(place, sources, total, w_qkv):
    features, width = w_qkv.shape
    step = 256
    return pl.pallas_call(
        input_kernel,
        grid=(features // step,),
        out_shape=(struct((total, features), BF16), struct((8, DH), F32)),
        in_specs=[SMEM]
        + [VMEM] * len(sources)
        + [pl.BlockSpec((step, width), lambda i: (i, 0))],
        out_specs=(
            pl.BlockSpec((total, step), lambda i: (0, i)),
            pl.BlockSpec((8, DH), lambda i: (0, 0)),
        ),
        scratch_shapes=[pltpu.VMEM((total, width), BF16)],
        compiler_params=pltpu.CompilerParams(vmem_limit_bytes=48 * MIB),
        cost_estimate=pl.CostEstimate(
            flops=16 * total * features * width, bytes_accessed=80 * MIB, transcendentals=0
        ),
        name="input_gradient",
    )(place, *sources, w_qkv)


def fold_kernel(count, place, *refs):
    out = refs[-1]
    dp_count = out.shape[0]
    for core in range(2):

        @pl.when(place[2] == core)
        def _():
            for z in range(dp_count):
                to = (z + core * (dp_count // 2)) % dp_count
                out[to] = sum(ref[z] for ref in refs[:count])


def fold(place, parts, after):
    return pl.pallas_call(
        functools.partial(fold_kernel, len(parts)),
        out_shape=struct(parts[0].shape, F32),
        in_specs=[SMEM] + [VMEM] * len(parts) + [ANY],
        out_specs=VMEM,
        compiler_params=pltpu.CompilerParams(vmem_limit_bytes=8 * MIB),
        cost_estimate=pl.CostEstimate(flops=MIB, bytes_accessed=2 * MIB, transcendentals=0),
        name="fold",
    )(place, *parts, after)


def square_kernel(got, after, out):
    count, width = out.shape[0], got.shape[2] // DH
    rows = got.shape[1] // count
    value = sum(got[z] for z in range(got.shape[0]))
    square = jnp.sum(jnp.sum(value * value, axis=0, keepdims=True))
    for to in range(count):
        for part in range(width):
            out[to, part * rows : (part + 1) * rows, :] = value[
                to * rows : (to + 1) * rows, part * DH : (part + 1) * DH
            ]
        out[to, width * rows :, :] = jnp.full((rows, DH), square)


def square_sum(got, after):
    rows = (got.shape[2] // DH + 1) * got.shape[1] // GROUP
    return pl.pallas_call(
        square_kernel,
        out_shape=struct((GROUP, rows, DH), F32),
        in_specs=[VMEM, ANY],
        out_specs=VMEM,
        compiler_params=pltpu.CompilerParams(vmem_limit_bytes=8 * MIB),
        cost_estimate=pl.CostEstimate(flops=MIB, bytes_accessed=MIB, transcendentals=0),
        name="square_sum",
    )(got, after)


def group_square_kernel(parts, out):
    last = parts.shape[1] - 1
    square = sum(parts[i, last : last + 1, :] for i in range(parts.shape[0]))
    out[...] = jnp.broadcast_to(square, out.shape)


def group_square(parts, copies):
    return pl.pallas_call(
        group_square_kernel,
        out_shape=struct((copies, DH), F32),
        in_specs=[VMEM],
        out_specs=VMEM,
        compiler_params=pltpu.CompilerParams(vmem_limit_bytes=8 * MIB),
        cost_estimate=pl.CostEstimate(flops=MIB, bytes_accessed=MIB, transcendentals=0),
        name="group_square",
    )(parts)


def clip_kernel(squares, parts, out):
    rows = out.shape[0]
    total_sq = jnp.sum(squares[...], axis=0, keepdims=True)
    factor = jnp.minimum(1.0, D / jnp.sqrt(total_sq + 1e-06))
    for head in range(H):
        for part in range(3):
            start = (part * H + head) * DH
            out[:, start : start + DH] = parts[head, part * rows : (part + 1) * rows, :] * factor


def clip(squares, parts):
    rows = parts.shape[1] // 4
    return pl.pallas_call(
        clip_kernel,
        out_shape=struct((rows, 3 * H * DH), F32),
        in_specs=[VMEM, VMEM],
        out_specs=VMEM,
        compiler_params=pltpu.CompilerParams(vmem_limit_bytes=8 * MIB),
        cost_estimate=pl.CostEstimate(flops=MIB, bytes_accessed=MIB, transcendentals=0),
        name="clip",
    )(squares, parts)


def body(inputs, grad_out, w_qkv):
    user_count, row_count, feature_count = inputs.shape
    seqlen_total = row_count * lax.axis_size("seq")
    dp_count = lax.axis_size("dp")
    scaling = 1.0 / math.sqrt(DH * seqlen_total)
    index = lax.axis_index("seq")
    y, x, c = index // GROUP, (index // 2) % NX, index % 2
    place = jnp.stack([y, x, c])
    head = x * 2 + c
    total_rows = user_count * row_count

    to_right, to_left, to_other = messages(place, inputs, grad_out)
    left = send(to_right, dx=1)
    right = send(to_left, dx=-1)
    other = send(to_other, dc=1)
    w_head = jnp.concatenate(
        [head_columns(w_qkv, part * H + head) for part in range(3)], axis=1
    )
    own_units = ((0, None, 0, 0), (0, None, 0, 0), (2, 0, 16, 0), (2, 8, 17, 0))
    left_units = ((0, 0, 18, 2), (0, 10, 19, 2), (1, 0, 18, 2), (1, 10, 19, 2))
    right_units = ((0, 10, 18, 2), (0, 0, 19, 2), (1, 10, 18, 2), (1, 0, 19, 2))
    far_units = ((0, 0, 8, 1), (0, 10, 18, 1))
    own_part = blocks(place, w_head, (inputs, grad_out, other), own_units)

    far_low = send(left[:10], dx=1)
    far_high = send(right[:10], dx=-1)
    count = left.shape[0]
    crossing = relay(
        (left, right),
        (left.shape, right.shape),
        ((0, 0, 0, count, 0), (1, 1, 0, count, 0)),
        (own_part[3],),
    )
    left_other, right_other = (send(value, dc=1) for value in crossing)
    left_part = blocks(place, w_head, (left, left_other), left_units)
    right_part = blocks(place, w_head, (right, right_other), right_units)
    (far,) = relay(
        (far_low, far_high),
        ((20,) + left.shape[1:],),
        ((0, 0, 0, 10, 0), (0, 1, 0, 10, 10)),
        (own_part[3], left_part[3], right_part[3]),
    )
    far_other = send(far, dc=1)
    parts = [
        own_part,
        left_part,
        blocks(place, w_head, (far,), far_units),
        blocks(place, w_head, (far_other,), far_units),
        right_part,
    ]
    sent = totals(place, [part[3] for part in parts], [part[4] for part in parts])
    arrived = [send(value, dy=dy) for value, dy in zip(sent, FAR_FIRST)]
    grad_proj, give, far_piece = gradients(
        place, arrived, parts, scaling, user_count, dp_count
    )

    span = 2 * total_rows
    theirs = send(give, dc=1)
    returns = relay(
        (grad_proj, theirs),
        ((span, 3 * DH),) * (NX - 1),
        tuple((dx - 1, 0, dx * span, dx * span + total_rows, 0) for dx in range(1, NX))
        + tuple(
            (dx - 1, 1, dx * total_rows, (dx + 1) * total_rows, total_rows)
            for dx in range(1, NX)
        ),
    )
    back = [send(returns[dx - 1], dx=-dx) for dx in range(1, NX)]
    *near, kept = rest_of_rows(place, [part[0] for part in parts], grad_proj, far_piece.shape)
    summands = [send(value, dy=dy) for value, dy in zip([far_piece] + near, FAR_FIRST)]
    summands.append(kept)
    folded = fold(place, summands, returns[0])
    columns_of = []
    for column in range(NY * GROUP):
        turn = column % 2 * (dp_count // 2)
        order = [(z + turn) % dp_count for z in range(dp_count)]
        columns_of.append([z * NY * GROUP + column for z in order])
    got = lax.all_to_all(folded, ("dp", "seq"), 0, 0, axis_index_groups=columns_of)
    grad_rows, done = input_gradient(place, (grad_proj, theirs, *back), total_rows, w_qkv)
    grad_inputs = grad_rows.reshape(user_count, row_count, feature_count)

    seq_count = lax.axis_size("seq")
    groups = [
        [first + t for t in range(GROUP)] for first in range(0, dp_count * seq_count, GROUP)
    ]
    across = [[t + first[0] for first in groups] for t in range(GROUP)]
    parts = lax.all_to_all(
        square_sum(got, done), ("dp", "seq"), 0, 0, axis_index_groups=groups
    )
    squares = lax.all_to_all(
        group_square(parts, dp_count * NY),
        ("dp", "seq"),
        0,
        0,
        axis_index_groups=across,
        tiled=True,
    )
    return (grad_inputs, clip(squares, parts))


def solution(mesh):
    in_specs = (P("dp", "seq", None), P("dp", "seq", None), P())
    out_specs = (P("dp", "seq", None), P(("dp", "seq"), None))
    return jax.shard_map(body, mesh=mesh, in_specs=in_specs, out_specs=out_specs, check_vma=False)
```

```python
import functools
import math

import jax
import jax.numpy as jnp
from jax import lax
from jax.experimental import pallas as pl
from jax.experimental.pallas import tpu as pltpu
from jax.sharding import PartitionSpec as P

H = 8
DH = 128
D = 1024
NY = 4
NX = 4
GROUP = 2 * NX
FAR_FIRST = (2, 1, 3)
BF16 = jnp.bfloat16
F32 = jnp.float32
VMEM = pl.BlockSpec(memory_space=pltpu.VMEM)
SMEM = pl.BlockSpec(memory_space=pltpu.SMEM)
ANY = pl.BlockSpec(memory_space=pl.ANY)
MIB = 1 << 20


def seq_perm(dy, dx, dc):
    moves = []
    for y in range(NY):
        for x in range(NX):
            for c in range(2):
                source = (y * NX + x) * 2 + c
                target = (((y + dy) % NY) * NX + (x + dx) % NX) * 2 + (c ^ dc)
                moves.append((source, target))
    return moves


def send(value, dy=0, dx=0, dc=0):
    return lax.ppermute(value, "seq", seq_perm(dy, dx, dc))


def head_columns(array, head):
    return lax.dynamic_slice_in_dim(array, head * DH, DH, 1)


def struct(shape, dtype):
    return jax.ShapeDtypeStruct(shape, dtype)


def dot(a, b, over_a, over_b):
    return lax.dot_general(a, b, (((over_a,), (over_b,)), ((), ())), preferred_element_type=F32)


def message_kernel(place, inputs, grad_out, right, left, cross):
    x, c = place[1], place[2]

    def cot(user, dx, core):
        head = ((x + dx) % NX) * 2 + core
        return grad_out[user, :, pl.ds(pl.multiple_of(head * DH, DH), DH)].astype(F32)

    for user in range(2):
        passed, kept = (right, left) if user == 0 else (left, right)
        for j in range(H):
            value = inputs[user, :, j * DH : (j + 1) * DH].astype(F32)
            passed[j] = value
            kept[10 + j] = value
            cross[user * H + j] = value
        for core in range(2):
            passed[8 + core] = cot(user, 2, core)
            right[18 + 2 * core + user] = cot(user, 1, core)
            left[18 + 2 * core + user] = cot(user, NX - 1, core)
        cross[2 * H + user] = cot(user, 0, 1 - c)


def messages(place, inputs, grad_out):
    size = inputs.shape[1]
    return pl.pallas_call(
        message_kernel,
        out_shape=tuple(struct((count, size, DH), F32) for count in (22, 22, 18)),
        in_specs=[SMEM, VMEM, VMEM],
        out_specs=(VMEM,) * 3,
        compiler_params=pltpu.CompilerParams(vmem_limit_bytes=16 * MIB),
        cost_estimate=pl.CostEstimate(flops=MIB, bytes_accessed=3 * MIB, transcendentals=0),
        name="messages",
    )(place, inputs, grad_out)


def relay_kernel(cuts, *refs):
    sources, outs = refs
    for out, source, first, last, at in cuts:
        outs[out][at : at + last - first] = sources[source][first:last].astype(outs[out].dtype)


def relay(sources, shapes, cuts, after=()):
    def kernel(*refs):
        relay_kernel(cuts, refs[: len(sources)], refs[len(sources) + len(after) :])

    return pl.pallas_call(
        kernel,
        out_shape=tuple(struct(shape, F32) for shape in shapes),
        in_specs=[VMEM] * len(sources) + [ANY] * len(after),
        out_specs=(VMEM,) * len(shapes),
        compiler_params=pltpu.CompilerParams(vmem_limit_bytes=12 * MIB),
        cost_estimate=pl.CostEstimate(flops=MIB, bytes_accessed=2 * MIB, transcendentals=0),
        name="relay",
    )(*sources, *after)


def block_kernel(units, place, w, *refs):
    sources, refs = refs[:-7], refs[-7:]
    rows_t, proj, cot_half, key_state, query_state, intra, x_all = refs
    x, c = place[1], place[2]
    features, total = rows_t.shape
    size = total // len(units)
    causal = lax.broadcasted_iota(jnp.int32, (size, size), 0) >= lax.broadcasted_iota(
        jnp.int32, (size, size), 1
    )
    for n, (source, start, cot_start, cot_step) in enumerate(units):
        here = slice(n * size, (n + 1) * size)
        if start is None:
            x_all[here, :] = sources[source][n]
            columns = pl.ds(pl.multiple_of((x * 2 + c) * DH, DH), DH)
            cot_half[here, :] = sources[source + 1][n, :, columns]
        else:
            for j in range(features // DH):
                x_all[here, j * DH : (j + 1) * DH] = sources[source][start + j].astype(BF16)
            cot_half[here, :] = sources[source][cot_start + cot_step * c].astype(BF16)
    rows = x_all[...]
    proj[...] = dot(rows, w[...], 1, 0).astype(BF16)
    rows_t[...] = rows.T
    for n in range(len(units)):
        here = slice(n * size, (n + 1) * size)
        i, u = n // 2, n % 2
        q, k, v = (proj[here, part * DH : (part + 1) * DH] for part in range(3))
        g = cot_half[here, :]
        key_state[i, u] = dot(k, v, 0, 0)
        query_state[i, u] = dot(q, g, 0, 0)
        out_value = jnp.where(causal, dot(g, v, 1, 1), 0.0).astype(BF16)
        query_key = jnp.where(causal, dot(q, k, 1, 1), 0.0).astype(BF16)
        intra[here, :DH] = dot(out_value, k, 1, 0)
        intra[here, DH : 2 * DH] = dot(out_value, q, 0, 0)
        intra[here, 2 * DH :] = dot(query_key, g, 0, 0)


def blocks(place, w_head, sources, units):
    features = w_head.shape[0]
    size = sources[0].shape[1]
    total = len(units) * size
    return pl.pallas_call(
        functools.partial(block_kernel, units),
        out_shape=(
            struct((features, total), BF16),
            struct((total, 3 * DH), BF16),
            struct((total, DH), BF16),
            struct((len(units) // 2, 2, DH, DH), F32),
            struct((len(units) // 2, 2, DH, DH), F32),
            struct((total, 3 * DH), F32),
        ),
        in_specs=[SMEM] + [VMEM] * (1 + len(sources)),
        out_specs=(VMEM,) * 6,
        scratch_shapes=[pltpu.VMEM((total, features), BF16)],
        compiler_params=pltpu.CompilerParams(vmem_limit_bytes=24 * MIB),
        cost_estimate=pl.CostEstimate(
            flops=2 * total * features * 3 * DH, bytes_accessed=4 * MIB, transcendentals=0
        ),
        name="blocks",
    )(place, w_head, *sources)


def total_kernel(place, *refs):
    count = (len(refs) - NY + 1) // 2
    keys, queries, outs = refs[:count], refs[count : 2 * count], refs[2 * count :]
    key_total = sum(ref[i] for ref in keys for i in range(ref.shape[0]))
    query_total = sum(ref[i] for ref in queries for i in range(ref.shape[0]))
    for out, dy in zip(outs, FAR_FIRST):
        out[...] = jnp.where(place[0] + dy < NY, key_total, query_total)


def totals(place, key_states, query_states):
    shape = key_states[0].shape[1:]
    return pl.pallas_call(
        total_kernel,
        out_shape=(struct(shape, F32),) * (NY - 1),
        in_specs=[SMEM] + [VMEM] * (2 * len(key_states)),
        out_specs=(VMEM,) * (NY - 1),
        compiler_params=pltpu.CompilerParams(vmem_limit_bytes=16 * MIB),
        cost_estimate=pl.CostEstimate(flops=MIB, bytes_accessed=3 * MIB, transcendentals=0),
        name="totals",
    )(place, *key_states, *query_states)


def grad_kernel(scaling, users, dp_count, count, place, *refs):
    y, x, c = place[0], place[1], place[2]
    arrived, refs = refs[: NY - 1], refs[NY - 1 :]
    keys, refs = refs[:count], refs[count:]
    queries, refs = refs[:count], refs[count:]
    rows_t, refs = refs[:count], refs[count:]
    proj, refs = refs[:count], refs[count:]
    cots, refs = refs[:count], refs[count:]
    intra, refs = refs[:count], refs[count:]
    grad_proj, give, piece, key_all, query_all, prior_all, later_all, picked = refs
    first = 0
    for part in range(count):
        last = first + keys[part].shape[0]
        key_all[first:last] = keys[part][...]
        query_all[first:last] = queries[part][...]
        first = last
    prior = jnp.zeros(arrived[0].shape, F32)
    later = jnp.zeros(arrived[0].shape, F32)
    for ref, dy in zip(arrived, FAR_FIRST):
        value = ref[...]
        prior = prior + jnp.where(y >= dy, value, 0.0)
        later = later + jnp.where(y >= dy, 0.0, value)

    def slot(position):
        return ((x + NX - position // 2) % NX) * 2 + (c ^ (position % 2))

    for position in range(GROUP):
        here = slot(position)
        prior_all[here] = prior.astype(BF16)
        prior = prior + key_all[here]
    for position in reversed(range(GROUP)):
        here = slot(position)
        later_all[here] = later.astype(BF16)
        later = later + query_all[here]
    size = intra[0].shape[0] // (keys[0].shape[0] * users)
    block = 0
    for part in range(count):
        for i in range(keys[part].shape[0]):
            for u in range(users):
                here = slice((i * users + u) * size, (i * users + u + 1) * size)
                there = slice((block * users + u) * size, (block * users + u + 1) * size)
                k, v = proj[part][here, DH : 2 * DH], proj[part][here, 2 * DH :]
                prior_state, later_state = prior_all[block, u], later_all[block, u]
                inter = (
                    dot(cots[part][here, :], prior_state, 1, 1),
                    dot(v, later_state, 1, 1),
                    dot(k, later_state, 1, 0),
                )
                for kind in range(3):
                    columns = slice(kind * DH, (kind + 1) * DH)
                    grad_proj[there, columns] = (
                        scaling * (intra[part][here, columns] + inter[kind])
                    ).astype(BF16)
            block += 1
    total = users * size
    for dx in range(NX):
        there = slice((2 * dx + 1) * total, (2 * dx + 2) * total)
        give[dx * total : (dx + 1) * total, :] = grad_proj[there, :].astype(F32)
    rows_for(y, FAR_FIRST[0], rows_t, grad_proj, picked, piece)


def rows_for(y, dy, rows_t, grad_proj, picked, piece):
    dp_count, row_block = piece.shape[0], piece.shape[1]
    target = (y + dy) % NY
    first = 0
    for part in rows_t:
        last = first + part.shape[1]
        for z in range(dp_count):
            start = pl.multiple_of((z * NY + target) * row_block, row_block)
            picked[z * row_block : (z + 1) * row_block, first:last] = part[
                pl.ds(start, row_block), :
            ]
        first = last
    value = dot(picked[...], grad_proj[...], 1, 0)
    for z in range(dp_count):
        piece[z] = value[z * row_block : (z + 1) * row_block, :]


def rest_kernel(place, *refs):
    rows_t, grad_proj, refs = refs[: -1 - NY], refs[-1 - NY], refs[-NY:]
    for piece, dy in zip(refs, FAR_FIRST[1:] + (0,)):
        rows_for(place[0], dy, rows_t, grad_proj, refs[-1], piece)


def rest_of_rows(place, rows_t, grad_proj, shape):
    tokens = grad_proj.shape[0]
    return pl.pallas_call(
        rest_kernel,
        out_shape=(struct(shape, F32),) * (NY - 1),
        in_specs=[SMEM] + [VMEM] * (len(rows_t) + 1),
        out_specs=(VMEM,) * (NY - 1),
        scratch_shapes=[pltpu.VMEM((shape[0] * shape[1], tokens), BF16)],
        compiler_params=pltpu.CompilerParams(vmem_limit_bytes=24 * MIB),
        cost_estimate=pl.CostEstimate(flops=MIB, bytes_accessed=4 * MIB, transcendentals=0),
        name="rest_of_rows",
    )(place, *rows_t, grad_proj)


def gradients(place, arrived, parts, scaling, users, dp_count):
    rows_t, proj, cots, keys, queries, intra = zip(*parts)
    features = rows_t[0].shape[0]
    rows = sum(part.shape[1] for part in rows_t)
    row_block = features // (dp_count * NY)
    count = len(parts)
    return pl.pallas_call(
        functools.partial(grad_kernel, scaling, users, dp_count, count),
        out_shape=(struct((rows, 3 * DH), BF16), struct((rows // 2, 3 * DH), F32))
        + (struct((dp_count, row_block, 3 * DH), F32),),
        in_specs=[SMEM] + [VMEM] * (NY - 1 + 6 * count),
        out_specs=(VMEM,) * 3,
        scratch_shapes=[
            pltpu.VMEM((GROUP, users, DH, DH), F32),
            pltpu.VMEM((GROUP, users, DH, DH), F32),
            pltpu.VMEM((GROUP, users, DH, DH), BF16),
            pltpu.VMEM((GROUP, users, DH, DH), BF16),
            pltpu.VMEM((dp_count * row_block, rows), BF16),
        ],
        compiler_params=pltpu.CompilerParams(vmem_limit_bytes=32 * MIB),
        cost_estimate=pl.CostEstimate(
            flops=2 * rows * features * 3 * DH, bytes_accessed=10 * MIB, transcendentals=0
        ),
        name="gradients",
    )(place, *arrived, *keys, *queries, *rows_t, *proj, *cots, *intra)


def input_kernel(place, *refs):
    x, c = place[1], place[2]
    own, theirs, back = refs[0], refs[1], refs[2 : 1 + NX]
    w, out, done, full = refs[1 + NX :]
    total = out.shape[0]

    @pl.when(pl.program_id(0) == 0)
    def _():
        for dx in range(NX):
            for dc in range(2):
                head = ((x + dx) % NX) * 2 + (c ^ dc)
                source = (theirs if dc else own) if dx == 0 else back[dx - 1]
                first = total if dx and dc else 0
                for part in range(3):
                    columns = slice(part * DH, (part + 1) * DH)
                    start = pl.multiple_of((part * H + head) * DH, DH)
                    full[:, pl.ds(start, DH)] = source[first : first + total, columns].astype(BF16)
        done[...] = jnp.zeros(done.shape, F32)

    out[...] = dot(full[...], w[...], 1, 1).astype(BF16)


def input_gradient(place, sources, total, w_qkv):
    features, width = w_qkv.shape
    step = 256
    return pl.pallas_call(
        input_kernel,
        grid=(features // step,),
        out_shape=(struct((total, features), BF16), struct((8, DH), F32)),
        in_specs=[SMEM]
        + [VMEM] * len(sources)
        + [pl.BlockSpec((step, width), lambda i: (i, 0))],
        out_specs=(
            pl.BlockSpec((total, step), lambda i: (0, i)),
            pl.BlockSpec((8, DH), lambda i: (0, 0)),
        ),
        scratch_shapes=[pltpu.VMEM((total, width), BF16)],
        compiler_params=pltpu.CompilerParams(vmem_limit_bytes=48 * MIB),
        cost_estimate=pl.CostEstimate(
            flops=16 * total * features * width, bytes_accessed=80 * MIB, transcendentals=0
        ),
        name="input_gradient",
    )(place, *sources, w_qkv)


def fold_kernel(count, place, *refs):
    out = refs[-1]
    dp_count = out.shape[0]
    for core in range(2):

        @pl.when(place[2] == core)
        def _():
            for z in range(dp_count):
                to = (z + core * (dp_count // 2)) % dp_count
                out[to] = sum(ref[z] for ref in refs[:count])


def fold(place, parts, after):
    return pl.pallas_call(
        functools.partial(fold_kernel, len(parts)),
        out_shape=struct(parts[0].shape, F32),
        in_specs=[SMEM] + [VMEM] * len(parts) + [ANY],
        out_specs=VMEM,
        compiler_params=pltpu.CompilerParams(vmem_limit_bytes=8 * MIB),
        cost_estimate=pl.CostEstimate(flops=MIB, bytes_accessed=2 * MIB, transcendentals=0),
        name="fold",
    )(place, *parts, after)


def square_kernel(got, after, out):
    count, width = out.shape[0], got.shape[2] // DH
    rows = got.shape[1] // count
    value = sum(got[z] for z in range(got.shape[0]))
    square = jnp.sum(jnp.sum(value * value, axis=0, keepdims=True))
    for to in range(count):
        for part in range(width):
            out[to, part * rows : (part + 1) * rows, :] = value[
                to * rows : (to + 1) * rows, part * DH : (part + 1) * DH
            ]
        out[to, width * rows :, :] = jnp.full((rows, DH), square)


def square_sum(got, after):
    rows = (got.shape[2] // DH + 1) * got.shape[1] // GROUP
    return pl.pallas_call(
        square_kernel,
        out_shape=struct((GROUP, rows, DH), F32),
        in_specs=[VMEM, ANY],
        out_specs=VMEM,
        compiler_params=pltpu.CompilerParams(vmem_limit_bytes=8 * MIB),
        cost_estimate=pl.CostEstimate(flops=MIB, bytes_accessed=MIB, transcendentals=0),
        name="square_sum",
    )(got, after)


def group_square_kernel(parts, out):
    last = parts.shape[1] - 1
    square = sum(parts[i, last : last + 1, :] for i in range(parts.shape[0]))
    out[...] = jnp.broadcast_to(square, out.shape)


def group_square(parts, copies):
    return pl.pallas_call(
        group_square_kernel,
        out_shape=struct((copies, DH), F32),
        in_specs=[VMEM],
        out_specs=VMEM,
        compiler_params=pltpu.CompilerParams(vmem_limit_bytes=8 * MIB),
        cost_estimate=pl.CostEstimate(flops=MIB, bytes_accessed=MIB, transcendentals=0),
        name="group_square",
    )(parts)


def clip_kernel(squares, parts, out):
    rows = out.shape[0]
    total_sq = jnp.sum(squares[...], axis=0, keepdims=True)
    factor = jnp.minimum(1.0, D / jnp.sqrt(total_sq + 1e-06))
    for head in range(H):
        for part in range(3):
            start = (part * H + head) * DH
            out[:, start : start + DH] = parts[head, part * rows : (part + 1) * rows, :] * factor


def clip(squares, parts):
    rows = parts.shape[1] // 4
    return pl.pallas_call(
        clip_kernel,
        out_shape=struct((rows, 3 * H * DH), F32),
        in_specs=[VMEM, VMEM],
        out_specs=VMEM,
        compiler_params=pltpu.CompilerParams(vmem_limit_bytes=8 * MIB),
        cost_estimate=pl.CostEstimate(flops=MIB, bytes_accessed=MIB, transcendentals=0),
        name="clip",
    )(squares, parts)


def body(inputs, grad_out, w_qkv):
    user_count, row_count, feature_count = inputs.shape
    seqlen_total = row_count * lax.axis_size("seq")
    dp_count = lax.axis_size("dp")
    scaling = 1.0 / math.sqrt(DH * seqlen_total)
    index = lax.axis_index("seq")
    y, x, c = index // GROUP, (index // 2) % NX, index % 2
    place = jnp.stack([y, x, c])
    head = x * 2 + c
    total_rows = user_count * row_count

    to_right, to_left, to_other = messages(place, inputs, grad_out)
    left = send(to_right, dx=1)
    right = send(to_left, dx=-1)
    other = send(to_other, dc=1)
    w_head = jnp.concatenate(
        [head_columns(w_qkv, part * H + head) for part in range(3)], axis=1
    )
    own_units = ((0, None, 0, 0), (0, None, 0, 0), (2, 0, 16, 0), (2, 8, 17, 0))
    left_units = ((0, 0, 18, 2), (0, 10, 19, 2), (1, 0, 18, 2), (1, 10, 19, 2))
    right_units = ((0, 10, 18, 2), (0, 0, 19, 2), (1, 10, 18, 2), (1, 0, 19, 2))
    far_units = ((0, 0, 8, 1), (0, 10, 18, 1))
    own_part = blocks(place, w_head, (inputs, grad_out, other), own_units)

    far_low = send(left[:10], dx=1)
    far_high = send(right[:10], dx=-1)
    count = left.shape[0]
    crossing = relay(
        (left, right),
        (left.shape, right.shape),
        ((0, 0, 0, count, 0), (1, 1, 0, count, 0)),
        (own_part[3],),
    )
    left_other, right_other = (send(value, dc=1) for value in crossing)
    left_part = blocks(place, w_head, (left, left_other), left_units)
    right_part = blocks(place, w_head, (right, right_other), right_units)
    (far,) = relay(
        (far_low, far_high),
        ((20,) + left.shape[1:],),
        ((0, 0, 0, 10, 0), (0, 1, 0, 10, 10)),
        (own_part[3], left_part[3], right_part[3]),
    )
    far_other = send(far, dc=1)
    parts = [
        own_part,
        left_part,
        blocks(place, w_head, (far,), far_units),
        blocks(place, w_head, (far_other,), far_units),
        right_part,
    ]
    sent = totals(place, [part[3] for part in parts], [part[4] for part in parts])
    arrived = [send(value, dy=dy) for value, dy in zip(sent, FAR_FIRST)]
    grad_proj, give, far_piece = gradients(
        place, arrived, parts, scaling, user_count, dp_count
    )

    span = 2 * total_rows
    theirs = send(give, dc=1)
    returns = relay(
        (grad_proj, theirs),
        ((span, 3 * DH),) * (NX - 1),
        tuple((dx - 1, 0, dx * span, dx * span + total_rows, 0) for dx in range(1, NX))
        + tuple(
            (dx - 1, 1, dx * total_rows, (dx + 1) * total_rows, total_rows)
            for dx in range(1, NX)
        ),
    )
    back = [send(returns[dx - 1], dx=-dx) for dx in range(1, NX)]
    *near, kept = rest_of_rows(place, [part[0] for part in parts], grad_proj, far_piece.shape)
    summands = [send(value, dy=dy) for value, dy in zip([far_piece] + near, FAR_FIRST)]
    summands.append(kept)
    folded = fold(place, summands, returns[0])
    columns_of = []
    for column in range(NY * GROUP):
        turn = column % 2 * (dp_count // 2)
        order = [(z + turn) % dp_count for z in range(dp_count)]
        columns_of.append([z * NY * GROUP + column for z in order])
    got = lax.all_to_all(folded, ("dp", "seq"), 0, 0, axis_index_groups=columns_of)
    grad_rows, done = input_gradient(place, (grad_proj, theirs, *back), total_rows, w_qkv)
    grad_inputs = grad_rows.reshape(user_count, row_count, feature_count)

    seq_count = lax.axis_size("seq")
    groups = [
        [first + t for t in range(GROUP)] for first in range(0, dp_count * seq_count, GROUP)
    ]
    half = len(groups) // 2
    turned = (groups, groups[half:] + groups[:half])
    across = [[t + first[0] for first in turned[t % 2]] for t in range(GROUP)]
    parts = lax.all_to_all(
        square_sum(got, done), ("dp", "seq"), 0, 0, axis_index_groups=groups
    )
    squares = lax.all_to_all(
        group_square(parts, dp_count * NY),
        ("dp", "seq"),
        0,
        0,
        axis_index_groups=across,
        tiled=True,
    )
    return (grad_inputs, clip(squares, parts))


def solution(mesh):
    in_specs = (P("dp", "seq", None), P("dp", "seq", None), P())
    out_specs = (P("dp", "seq", None), P(("dp", "seq"), None))
    return jax.shard_map(body, mesh=mesh, in_specs=in_specs, out_specs=out_specs, check_vma=False)
```

```python
import functools
import math

import jax
import jax.numpy as jnp
from jax import lax
from jax.experimental import pallas as pl
from jax.experimental.pallas import tpu as pltpu
from jax.sharding import PartitionSpec as P

H = 8
DH = 128
D = 1024
NY = 4
NX = 4
GROUP = 2 * NX
FAR_FIRST = (2, 1, 3)
BF16 = jnp.bfloat16
F32 = jnp.float32
VMEM = pl.BlockSpec(memory_space=pltpu.VMEM)
SMEM = pl.BlockSpec(memory_space=pltpu.SMEM)
ANY = pl.BlockSpec(memory_space=pl.ANY)
MIB = 1 << 20


def seq_perm(dy, dx, dc):
    moves = []
    for y in range(NY):
        for x in range(NX):
            for c in range(2):
                source = (y * NX + x) * 2 + c
                target = (((y + dy) % NY) * NX + (x + dx) % NX) * 2 + (c ^ dc)
                moves.append((source, target))
    return moves


def send(value, dy=0, dx=0, dc=0):
    return lax.ppermute(value, "seq", seq_perm(dy, dx, dc))


def head_columns(array, head):
    return lax.dynamic_slice_in_dim(array, head * DH, DH, 1)


def struct(shape, dtype):
    return jax.ShapeDtypeStruct(shape, dtype)


def dot(a, b, over_a, over_b):
    return lax.dot_general(a, b, (((over_a,), (over_b,)), ((), ())), preferred_element_type=F32)


def message_kernel(place, inputs, grad_out, right, left, cross):
    x, c = place[1], place[2]

    def cot(user, dx, core):
        head = ((x + dx) % NX) * 2 + core
        return grad_out[user, :, pl.ds(pl.multiple_of(head * DH, DH), DH)].astype(F32)

    for user in range(2):
        passed, kept = (right, left) if user == 0 else (left, right)
        for j in range(H):
            value = inputs[user, :, j * DH : (j + 1) * DH].astype(F32)
            passed[j] = value
            kept[10 + j] = value
            cross[user * H + j] = value
        for core in range(2):
            passed[8 + core] = cot(user, 2, core)
            right[18 + 2 * core + user] = cot(user, 1, core)
            left[18 + 2 * core + user] = cot(user, NX - 1, core)
        cross[2 * H + user] = cot(user, 0, 1 - c)


def messages(place, inputs, grad_out):
    size = inputs.shape[1]
    return pl.pallas_call(
        message_kernel,
        out_shape=tuple(struct((count, size, DH), F32) for count in (22, 22, 18)),
        in_specs=[SMEM, VMEM, VMEM],
        out_specs=(VMEM,) * 3,
        compiler_params=pltpu.CompilerParams(vmem_limit_bytes=16 * MIB),
        cost_estimate=pl.CostEstimate(flops=MIB, bytes_accessed=3 * MIB, transcendentals=0),
        name="messages",
    )(place, inputs, grad_out)


def relay_kernel(cuts, *refs):
    sources, outs = refs
    for out, source, first, last, at in cuts:
        outs[out][at : at + last - first] = sources[source][first:last].astype(outs[out].dtype)


def relay(sources, shapes, cuts, after=()):
    def kernel(*refs):
        relay_kernel(cuts, refs[: len(sources)], refs[len(sources) + len(after) :])

    return pl.pallas_call(
        kernel,
        out_shape=tuple(struct(shape, F32) for shape in shapes),
        in_specs=[VMEM] * len(sources) + [ANY] * len(after),
        out_specs=(VMEM,) * len(shapes),
        compiler_params=pltpu.CompilerParams(vmem_limit_bytes=12 * MIB),
        cost_estimate=pl.CostEstimate(flops=MIB, bytes_accessed=2 * MIB, transcendentals=0),
        name="relay",
    )(*sources, *after)


def block_kernel(units, place, w, *refs):
    sources, refs = refs[:-7], refs[-7:]
    rows_t, proj, cot_half, key_state, query_state, intra, x_all = refs
    x, c = place[1], place[2]
    features, total = rows_t.shape
    size = total // len(units)
    causal = lax.broadcasted_iota(jnp.int32, (size, size), 0) >= lax.broadcasted_iota(
        jnp.int32, (size, size), 1
    )
    for n, (source, start, cot_start, cot_step) in enumerate(units):
        here = slice(n * size, (n + 1) * size)
        if start is None:
            x_all[here, :] = sources[source][n]
            columns = pl.ds(pl.multiple_of((x * 2 + c) * DH, DH), DH)
            cot_half[here, :] = sources[source + 1][n, :, columns]
        else:
            for j in range(features // DH):
                x_all[here, j * DH : (j + 1) * DH] = sources[source][start + j].astype(BF16)
            cot_half[here, :] = sources[source][cot_start + cot_step * c].astype(BF16)
    rows = x_all[...]
    proj[...] = dot(rows, w[...], 1, 0).astype(BF16)
    rows_t[...] = rows.T
    for n in range(len(units)):
        here = slice(n * size, (n + 1) * size)
        i, u = n // 2, n % 2
        q, k, v = (proj[here, part * DH : (part + 1) * DH] for part in range(3))
        g = cot_half[here, :]
        key_state[i, u] = dot(k, v, 0, 0)
        query_state[i, u] = dot(q, g, 0, 0)
        out_value = jnp.where(causal, dot(g, v, 1, 1), 0.0).astype(BF16)
        query_key = jnp.where(causal, dot(q, k, 1, 1), 0.0).astype(BF16)
        intra[here, :DH] = dot(out_value, k, 1, 0)
        intra[here, DH : 2 * DH] = dot(out_value, q, 0, 0)
        intra[here, 2 * DH :] = dot(query_key, g, 0, 0)


def blocks(place, w_head, sources, units):
    features = w_head.shape[0]
    size = sources[0].shape[1]
    total = len(units) * size
    return pl.pallas_call(
        functools.partial(block_kernel, units),
        out_shape=(
            struct((features, total), BF16),
            struct((total, 3 * DH), BF16),
            struct((total, DH), BF16),
            struct((len(units) // 2, 2, DH, DH), F32),
            struct((len(units) // 2, 2, DH, DH), F32),
            struct((total, 3 * DH), F32),
        ),
        in_specs=[SMEM] + [VMEM] * (1 + len(sources)),
        out_specs=(VMEM,) * 6,
        scratch_shapes=[pltpu.VMEM((total, features), BF16)],
        compiler_params=pltpu.CompilerParams(vmem_limit_bytes=24 * MIB),
        cost_estimate=pl.CostEstimate(
            flops=2 * total * features * 3 * DH, bytes_accessed=4 * MIB, transcendentals=0
        ),
        name="blocks",
    )(place, w_head, *sources)


def total_kernel(place, *refs):
    count = (len(refs) - NY + 1) // 2
    keys, queries, outs = refs[:count], refs[count : 2 * count], refs[2 * count :]
    key_total = sum(ref[i] for ref in keys for i in range(ref.shape[0]))
    query_total = sum(ref[i] for ref in queries for i in range(ref.shape[0]))
    for out, dy in zip(outs, FAR_FIRST):
        out[...] = jnp.where(place[0] + dy < NY, key_total, query_total)


def totals(place, key_states, query_states):
    shape = key_states[0].shape[1:]
    return pl.pallas_call(
        total_kernel,
        out_shape=(struct(shape, F32),) * (NY - 1),
        in_specs=[SMEM] + [VMEM] * (2 * len(key_states)),
        out_specs=(VMEM,) * (NY - 1),
        compiler_params=pltpu.CompilerParams(vmem_limit_bytes=16 * MIB),
        cost_estimate=pl.CostEstimate(flops=MIB, bytes_accessed=3 * MIB, transcendentals=0),
        name="totals",
    )(place, *key_states, *query_states)


def grad_kernel(scaling, users, dp_count, count, place, *refs):
    y, x, c = place[0], place[1], place[2]
    arrived, refs = refs[: NY - 1], refs[NY - 1 :]
    keys, refs = refs[:count], refs[count:]
    queries, refs = refs[:count], refs[count:]
    rows_t, refs = refs[:count], refs[count:]
    proj, refs = refs[:count], refs[count:]
    cots, refs = refs[:count], refs[count:]
    intra, refs = refs[:count], refs[count:]
    grad_proj, give, piece, key_all, query_all, prior_all, later_all, picked = refs
    first = 0
    for part in range(count):
        last = first + keys[part].shape[0]
        key_all[first:last] = keys[part][...]
        query_all[first:last] = queries[part][...]
        first = last
    prior = jnp.zeros(arrived[0].shape, F32)
    later = jnp.zeros(arrived[0].shape, F32)
    for ref, dy in zip(arrived, FAR_FIRST):
        value = ref[...]
        prior = prior + jnp.where(y >= dy, value, 0.0)
        later = later + jnp.where(y >= dy, 0.0, value)

    def slot(position):
        return ((x + NX - position // 2) % NX) * 2 + (c ^ (position % 2))

    for position in range(GROUP):
        here = slot(position)
        prior_all[here] = prior.astype(BF16)
        prior = prior + key_all[here]
    for position in reversed(range(GROUP)):
        here = slot(position)
        later_all[here] = later.astype(BF16)
        later = later + query_all[here]
    size = intra[0].shape[0] // (keys[0].shape[0] * users)
    block = 0
    for part in range(count):
        for i in range(keys[part].shape[0]):
            for u in range(users):
                here = slice((i * users + u) * size, (i * users + u + 1) * size)
                there = slice((block * users + u) * size, (block * users + u + 1) * size)
                k, v = proj[part][here, DH : 2 * DH], proj[part][here, 2 * DH :]
                prior_state, later_state = prior_all[block, u], later_all[block, u]
                inter = (
                    dot(cots[part][here, :], prior_state, 1, 1),
                    dot(v, later_state, 1, 1),
                    dot(k, later_state, 1, 0),
                )
                for kind in range(3):
                    columns = slice(kind * DH, (kind + 1) * DH)
                    grad_proj[there, columns] = (
                        scaling * (intra[part][here, columns] + inter[kind])
                    ).astype(BF16)
            block += 1
    total = users * size
    for dx in range(NX):
        there = slice((2 * dx + 1) * total, (2 * dx + 2) * total)
        give[dx * total : (dx + 1) * total, :] = grad_proj[there, :].astype(F32)
    rows_for(y, FAR_FIRST[0], rows_t, grad_proj, picked, piece)


def rows_for(y, dy, rows_t, grad_proj, picked, piece):
    dp_count, row_block = piece.shape[0], piece.shape[1]
    target = (y + dy) % NY
    first = 0
    for part in rows_t:
        last = first + part.shape[1]
        for z in range(dp_count):
            start = pl.multiple_of((z * NY + target) * row_block, row_block)
            picked[z * row_block : (z + 1) * row_block, first:last] = part[
                pl.ds(start, row_block), :
            ]
        first = last
    value = dot(picked[...], grad_proj[...], 1, 0)
    for z in range(dp_count):
        piece[z] = value[z * row_block : (z + 1) * row_block, :]


def rest_kernel(place, *refs):
    rows_t, grad_proj, refs = refs[: -1 - NY], refs[-1 - NY], refs[-NY:]
    for piece, dy in zip(refs, FAR_FIRST[1:] + (0,)):
        rows_for(place[0], dy, rows_t, grad_proj, refs[-1], piece)


def rest_of_rows(place, rows_t, grad_proj, shape):
    tokens = grad_proj.shape[0]
    return pl.pallas_call(
        rest_kernel,
        out_shape=(struct(shape, F32),) * (NY - 1),
        in_specs=[SMEM] + [VMEM] * (len(rows_t) + 1),
        out_specs=(VMEM,) * (NY - 1),
        scratch_shapes=[pltpu.VMEM((shape[0] * shape[1], tokens), BF16)],
        compiler_params=pltpu.CompilerParams(vmem_limit_bytes=24 * MIB),
        cost_estimate=pl.CostEstimate(flops=MIB, bytes_accessed=4 * MIB, transcendentals=0),
        name="rest_of_rows",
    )(place, *rows_t, grad_proj)


def gradients(place, arrived, parts, scaling, users, dp_count):
    rows_t, proj, cots, keys, queries, intra = zip(*parts)
    features = rows_t[0].shape[0]
    rows = sum(part.shape[1] for part in rows_t)
    row_block = features // (dp_count * NY)
    count = len(parts)
    return pl.pallas_call(
        functools.partial(grad_kernel, scaling, users, dp_count, count),
        out_shape=(struct((rows, 3 * DH), BF16), struct((rows // 2, 3 * DH), F32))
        + (struct((dp_count, row_block, 3 * DH), F32),),
        in_specs=[SMEM] + [VMEM] * (NY - 1 + 6 * count),
        out_specs=(VMEM,) * 3,
        scratch_shapes=[
            pltpu.VMEM((GROUP, users, DH, DH), F32),
            pltpu.VMEM((GROUP, users, DH, DH), F32),
            pltpu.VMEM((GROUP, users, DH, DH), BF16),
            pltpu.VMEM((GROUP, users, DH, DH), BF16),
            pltpu.VMEM((dp_count * row_block, rows), BF16),
        ],
        compiler_params=pltpu.CompilerParams(vmem_limit_bytes=32 * MIB),
        cost_estimate=pl.CostEstimate(
            flops=2 * rows * features * 3 * DH, bytes_accessed=10 * MIB, transcendentals=0
        ),
        name="gradients",
    )(place, *arrived, *keys, *queries, *rows_t, *proj, *cots, *intra)


def input_kernel(place, *refs):
    x, c = place[1], place[2]
    own, theirs, back = refs[0], refs[1], refs[2 : 1 + NX]
    w, out, done, full = refs[1 + NX :]
    total = out.shape[0]

    @pl.when(pl.program_id(0) == 0)
    def _():
        for dx in range(NX):
            for dc in range(2):
                head = ((x + dx) % NX) * 2 + (c ^ dc)
                source = (theirs if dc else own) if dx == 0 else back[dx - 1]
                first = total if dx and dc else 0
                for part in range(3):
                    columns = slice(part * DH, (part + 1) * DH)
                    start = pl.multiple_of((part * H + head) * DH, DH)
                    full[:, pl.ds(start, DH)] = source[first : first + total, columns].astype(BF16)
        done[...] = jnp.zeros(done.shape, F32)

    out[...] = dot(full[...], w[...], 1, 1).astype(BF16)


def input_gradient(place, sources, total, w_qkv):
    features, width = w_qkv.shape
    step = 256
    return pl.pallas_call(
        input_kernel,
        grid=(features // step,),
        out_shape=(struct((total, features), BF16), struct((8, DH), F32)),
        in_specs=[SMEM]
        + [VMEM] * len(sources)
        + [pl.BlockSpec((step, width), lambda i: (i, 0))],
        out_specs=(
            pl.BlockSpec((total, step), lambda i: (0, i)),
            pl.BlockSpec((8, DH), lambda i: (0, 0)),
        ),
        scratch_shapes=[pltpu.VMEM((total, width), BF16)],
        compiler_params=pltpu.CompilerParams(vmem_limit_bytes=48 * MIB),
        cost_estimate=pl.CostEstimate(
            flops=16 * total * features * width, bytes_accessed=80 * MIB, transcendentals=0
        ),
        name="input_gradient",
    )(place, *sources, w_qkv)


def fold_kernel(count, place, *refs):
    out = refs[-1]
    dp_count = out.shape[0]
    for core in range(2):

        @pl.when(place[2] == core)
        def _():
            for z in range(dp_count):
                to = (z + core * (dp_count // 2)) % dp_count
                out[to] = sum(ref[z] for ref in refs[:count])


def fold(place, parts, after):
    return pl.pallas_call(
        functools.partial(fold_kernel, len(parts)),
        out_shape=struct(parts[0].shape, F32),
        in_specs=[SMEM] + [VMEM] * len(parts) + [ANY],
        out_specs=VMEM,
        compiler_params=pltpu.CompilerParams(vmem_limit_bytes=8 * MIB),
        cost_estimate=pl.CostEstimate(flops=MIB, bytes_accessed=2 * MIB, transcendentals=0),
        name="fold",
    )(place, *parts, after)


def square_kernel(got, after, out):
    count, width = out.shape[0], got.shape[2] // DH
    rows = got.shape[1] // count
    value = sum(got[z] for z in range(got.shape[0]))
    square = jnp.sum(jnp.sum(value * value, axis=0, keepdims=True))
    for to in range(count):
        for part in range(width):
            out[to, part * rows : (part + 1) * rows, :] = value[
                to * rows : (to + 1) * rows, part * DH : (part + 1) * DH
            ]
        out[to, width * rows :, :] = jnp.full((rows, DH), square)


def square_sum(got, after):
    rows = (got.shape[2] // DH + 1) * got.shape[1] // GROUP
    return pl.pallas_call(
        square_kernel,
        out_shape=struct((GROUP, rows, DH), F32),
        in_specs=[VMEM, ANY],
        out_specs=VMEM,
        compiler_params=pltpu.CompilerParams(vmem_limit_bytes=8 * MIB),
        cost_estimate=pl.CostEstimate(flops=MIB, bytes_accessed=MIB, transcendentals=0),
        name="square_sum",
    )(got, after)


def group_square_kernel(parts, out):
    last = parts.shape[1] - 1
    square = sum(parts[i, last : last + 1, :] for i in range(parts.shape[0]))
    out[...] = jnp.broadcast_to(square, out.shape)


def group_square(parts, copies):
    return pl.pallas_call(
        group_square_kernel,
        out_shape=struct((copies, DH), F32),
        in_specs=[VMEM],
        out_specs=VMEM,
        compiler_params=pltpu.CompilerParams(vmem_limit_bytes=8 * MIB),
        cost_estimate=pl.CostEstimate(flops=MIB, bytes_accessed=MIB, transcendentals=0),
        name="group_square",
    )(parts)


def clip_kernel(squares, parts, out):
    rows = out.shape[0]
    total_sq = jnp.sum(squares[...], axis=0, keepdims=True)
    factor = jnp.minimum(1.0, D / jnp.sqrt(total_sq + 1e-06))
    for head in range(H):
        for part in range(3):
            start = (part * H + head) * DH
            out[:, start : start + DH] = parts[head, part * rows : (part + 1) * rows, :] * factor


def clip(squares, parts):
    rows = parts.shape[1] // 4
    return pl.pallas_call(
        clip_kernel,
        out_shape=struct((rows, 3 * H * DH), F32),
        in_specs=[VMEM, VMEM],
        out_specs=VMEM,
        compiler_params=pltpu.CompilerParams(vmem_limit_bytes=8 * MIB),
        cost_estimate=pl.CostEstimate(flops=MIB, bytes_accessed=MIB, transcendentals=0),
        name="clip",
    )(squares, parts)


def body(inputs, grad_out, w_qkv):
    user_count, row_count, feature_count = inputs.shape
    seqlen_total = row_count * lax.axis_size("seq")
    dp_count = lax.axis_size("dp")
    scaling = 1.0 / math.sqrt(DH * seqlen_total)
    index = lax.axis_index("seq")
    y, x, c = index // GROUP, (index // 2) % NX, index % 2
    place = jnp.stack([y, x, c])
    head = x * 2 + c
    total_rows = user_count * row_count

    to_right, to_left, to_other = messages(place, inputs, grad_out)
    left = send(to_right, dx=1)
    right = send(to_left, dx=-1)
    other = send(to_other, dc=1)
    w_head = jnp.concatenate(
        [head_columns(w_qkv, part * H + head) for part in range(3)], axis=1
    )
    own_units = ((0, None, 0, 0), (0, None, 0, 0), (2, 0, 16, 0), (2, 8, 17, 0))
    left_units = ((0, 0, 18, 2), (0, 10, 19, 2), (1, 0, 18, 2), (1, 10, 19, 2))
    right_units = ((0, 10, 18, 2), (0, 0, 19, 2), (1, 10, 18, 2), (1, 0, 19, 2))
    far_units = ((0, 0, 8, 1), (0, 10, 18, 1))
    own_part = blocks(place, w_head, (inputs, grad_out, other), own_units)

    far_low = send(left[:10], dx=1)
    far_high = send(right[:10], dx=-1)
    count = left.shape[0]
    crossing = relay(
        (left, right),
        (left.shape, right.shape),
        ((0, 0, 0, count, 0), (1, 1, 0, count, 0)),
        (own_part[3],),
    )
    left_other, right_other = (send(value, dc=1) for value in crossing)
    left_part = blocks(place, w_head, (left, left_other), left_units)
    right_part = blocks(place, w_head, (right, right_other), right_units)
    (far,) = relay(
        (far_low, far_high),
        ((20,) + left.shape[1:],),
        ((0, 0, 0, 10, 0), (0, 1, 0, 10, 10)),
        (own_part[3], left_part[3], right_part[3]),
    )
    far_other = send(far, dc=1)
    parts = [
        own_part,
        left_part,
        blocks(place, w_head, (far,), far_units),
        blocks(place, w_head, (far_other,), far_units),
        right_part,
    ]
    sent = totals(place, [part[3] for part in parts], [part[4] for part in parts])
    arrived = [send(value, dy=dy) for value, dy in zip(sent, FAR_FIRST)]
    grad_proj, give, far_piece = gradients(
        place, arrived, parts, scaling, user_count, dp_count
    )

    span = 2 * total_rows
    theirs = send(give, dc=1)
    returns = relay(
        (grad_proj, theirs),
        ((span, 3 * DH),) * (NX - 1),
        tuple((dx - 1, 0, dx * span, dx * span + total_rows, 0) for dx in range(1, NX))
        + tuple(
            (dx - 1, 1, dx * total_rows, (dx + 1) * total_rows, total_rows)
            for dx in range(1, NX)
        ),
    )
    back = [send(returns[dx - 1], dx=-dx) for dx in range(1, NX)]
    *near, kept = rest_of_rows(place, [part[0] for part in parts], grad_proj, far_piece.shape)
    summands = [send(value, dy=dy) for value, dy in zip([far_piece] + near, FAR_FIRST)]
    summands.append(kept)
    folded = fold(place, summands, returns[0])
    columns_of = []
    for column in range(NY * GROUP):
        turn = column % 2 * (dp_count // 2)
        order = [(z + turn) % dp_count for z in range(dp_count)]
        columns_of.append([z * NY * GROUP + column for z in order])
    got = lax.all_to_all(folded, ("dp", "seq"), 0, 0, axis_index_groups=columns_of)
    grad_rows, done = input_gradient(place, (grad_proj, theirs, *back), total_rows, w_qkv)
    grad_inputs = grad_rows.reshape(user_count, row_count, feature_count)

    seq_count = lax.axis_size("seq")
    groups = [
        [first + t for t in range(GROUP)] for first in range(0, dp_count * seq_count, GROUP)
    ]
    half = len(groups) // 2
    spread = [groups[13 * i % len(groups)] for i in range(len(groups))]
    turned = (spread, spread[half:] + spread[:half])
    across = [[t + first[0] for first in turned[t % 2]] for t in range(GROUP)]
    parts = lax.all_to_all(
        square_sum(got, done), ("dp", "seq"), 0, 0, axis_index_groups=groups
    )
    squares = lax.all_to_all(
        group_square(parts, dp_count * NY),
        ("dp", "seq"),
        0,
        0,
        axis_index_groups=across,
        tiled=True,
    )
    return (grad_inputs, clip(squares, parts))


def solution(mesh):
    in_specs = (P("dp", "seq", None), P("dp", "seq", None), P())
    out_specs = (P("dp", "seq", None), P(("dp", "seq"), None))
    return jax.shard_map(body, mesh=mesh, in_specs=in_specs, out_specs=out_specs, check_vma=False)
```
